32 devices in a mesh: dp: 4 (over x, core), ctx: 4 (over z), tensor: 2 (over y).
Axes of the slice: x: 2, y: 2, z: 4, core: 2. Of those that a mesh axis runs over, the one named last changes fastest.
Arguments:
- hidden_in: bfloat16 [8, 2048, 2560], P('dp', 'ctx'), may hold values from -6 to 6
- w_query: bfloat16 [2560, 2560], P(None, 'tensor'), may hold values from -0.125 to 0.125
- key_weight_matrix: bfloat16 [2560, 640], P(None, 'tensor'), may hold values from -0.125 to 0.125
- value_weight_matrix: bfloat16 [2560, 640], P(None, 'tensor'), may hold values from -0.125 to 0.125
- w_out: bfloat16 [2560, 2560], P('tensor'), may hold values from -0.5 to 0.5
- w_gate: bfloat16 [2560, 7168], P(None, 'tensor'), may hold values from -0.125 to 0.125
- w_up: bfloat16 [2560, 7168], P(None, 'tensor'), may hold values from -0.125 to 0.125
- w_down: bfloat16 [7168, 2560], P('tensor'), may hold values from -0.125 to 0.125
- attn_gain: float32 [2560], replicated, may hold values from 0.25 to 1.75
- mlp_gain: float32 [2560], replicated, may hold values from 0.25 to 1.75
- segments: int32 [8, 2048], P('dp', 'ctx'), may hold values from 0 to 2047, as said below
- valid_mask: int32 [8, 2048], P('dp', 'ctx'), may hold values from 0 to 1, as said below
- teacher: bfloat16 [8, 2048, 2560], P('dp', 'ctx'), may hold values from -8 to 8
Outputs:
- layer_out: bfloat16 [8, 2048, 2560], P('dp', 'ctx')
- loss: float32 [], replicated
- grad_input: float32 [8, 2048, 2560], P('dp', 'ctx')
- grad_query: float32 [2560, 2560], P(('dp', 'ctx'), 'tensor')
- grad_key: float32 [2560, 640], P(('dp', 'ctx'), 'tensor')
- grad_value: float32 [2560, 640], P(('dp', 'ctx'), 'tensor')
- grad_out: float32 [2560, 2560], P('tensor', ('dp', 'ctx'))
- grad_gate: float32 [2560, 7168], P(('dp', 'ctx'), 'tensor')
- grad_up: float32 [2560, 7168], P(('dp', 'ctx'), 'tensor')
- grad_down: float32 [7168, 2560], P('tensor', ('dp', 'ctx'))
- grad_attn_gain: float32 [2560], P(('dp', 'ctx'))
- grad_mlp_gain: float32 [2560], P(('dp', 'ctx'))
The draws below stay inside these ranges and needn't reach their ends.
Inputs may be any that keep to these rules, and one draw needn't show every extreme that they name: `segments`: within a sequence the numbers start at 0 and never fall; the last token of every sequence forms a document of its own; in each group of 2 sequences of one index of dp, one sequence has a document that covers tokens 512/2 to 1791. `valid_mask`: the first token of every sequence is valid.
All inputs are finite; a program needn't handle non-finite values.
Results may differ from the reference program's by a relative error of at most 0.023.
Values may be sent and summed in bfloat16 or wider, within the bound.
A program may use at most 512 MiB of HBM per device.

```python
import math
import jax
import jax.numpy as jnp
from jax import lax

MODEL_DIM = 2560
NQ = 32
KEY_VALUE_HEADS = 8
HEAD_SIZE = 80
FF = 7168
LENGTH = 2048
SEQS = 2
SEQUENCES = 8
PIECE = 512
TOKENS = 16384
N_TENSOR = 2


def draw_segments(key, part):
    key = jax.random.fold_in(key, 11)
    key_levels, key_bits, key_pick = jax.random.split(key, 3)
    block_count = LENGTH // 64
    levels = jax.random.randint(key_levels, (SEQUENCES, block_count), 3, 11)
    periods = jnp.repeat(jnp.left_shift(jnp.ones_like(levels), levels), 64, axis=1)
    uniform_bits = jax.random.randint(key_bits, (SEQUENCES, LENGTH), 0, 1048576)
    boundary = uniform_bits % periods == 0
    long_pick = jax.random.randint(key_pick, (SEQUENCES // SEQS,), 0, SEQS)
    chosen = jnp.arange(SEQUENCES, dtype=jnp.int32) % SEQS == jnp.repeat(long_pick, SEQS)
    places = jnp.arange(LENGTH, dtype=jnp.int32)
    quiet = (places >= PIECE // 2) & (places < LENGTH - PIECE // 2)
    boundary = boundary & jnp.logical_not(chosen[:, None] & quiet[None, :])
    boundary = boundary | (places[None, :] == LENGTH - 1)
    boundary = boundary & (places[None, :] > 0)
    first_places = jnp.where(boundary, places[None, :], 0).astype(jnp.int32)
    return lax.cummax(first_places, axis=1).astype(jnp.int32)


def draw_valid_mask(key, part):
    key = jax.random.fold_in(key, 23)
    seq_rows = jnp.arange(SEQUENCES, dtype=jnp.int32)[:, None]
    places = jnp.arange(LENGTH, dtype=jnp.int32)[None, :]
    device_groups = SEQUENCES // SEQS * (LENGTH // PIECE)
    device_rank = seq_rows // SEQS * (LENGTH // PIECE) + places // PIECE
    threshold = 300 + 600 * device_rank // max(device_groups - 1, 1)
    valid_bits = (jax.random.randint(key, (SEQUENCES, LENGTH), 0, 1000) < threshold).astype(jnp.int32)
    return jnp.where(places == 0, 1, valid_bits).astype(jnp.int32)


def draw_teacher(key, part):
    key = jax.random.fold_in(key, 37)
    seq_rows = jnp.arange(SEQUENCES, dtype=jnp.int32)[:, None]
    places = jnp.arange(LENGTH, dtype=jnp.int32)[None, :]
    device_groups = SEQUENCES // SEQS * (LENGTH // PIECE)
    device_rank = seq_rows // SEQS * (LENGTH // PIECE) + places // PIECE
    share = device_rank.astype(jnp.float32) / max(device_groups - 1, 1)
    row_scale = 0.4 + 1.6 * share
    noise = jnp.clip(jax.random.normal(key, (SEQUENCES, LENGTH, MODEL_DIM), jnp.float32), -4.0, 4.0)
    return (noise * row_scale[..., None]).astype(jnp.bfloat16)


def level_of(key, dims, pieces, smallest, top_value):
    def one(position, parts):
        steps = jax.random.uniform(jax.random.fold_in(jax.random.fold_in(key, 6), position), (parts,), jnp.float32, smallest / len(pieces), top_value / len(pieces))
        return jnp.repeat(jnp.exp(steps), dims[position] // parts).reshape((-1,) + (1,) * (len(dims) - position - 1))

    factor_of = one(*pieces[0])
    for cut in pieces[1:]:
        factor_of = factor_of * one(*cut)
    return factor_of


def normal_values(key, extent, width, bound, shards=(), kind=jnp.bfloat16):
    level = level_of(key, extent, shards, -0.22, 0.18) if shards else 1.0
    drawn = jax.random.normal(key, extent, jnp.float32) * width * level
    return jnp.minimum(jnp.maximum(drawn, -bound), bound).astype(kind)


def setup_inputs(seed: int = 0) -> dict:
    arg_keys = jax.random.split(jax.random.key(seed), 14)
    hidden_in = normal_values(arg_keys[0], (SEQUENCES, LENGTH, MODEL_DIM), 1.0, 6.0, ((0, 4), (1, 4)))
    w_query = normal_values(arg_keys[1], (MODEL_DIM, NQ * HEAD_SIZE), MODEL_DIM ** -0.5, 0.125, ((1, 2),))
    key_weight_matrix = normal_values(arg_keys[2], (MODEL_DIM, KEY_VALUE_HEADS * HEAD_SIZE), MODEL_DIM ** -0.5, 0.125, ((1, 2),))
    value_weight_matrix = normal_values(arg_keys[3], (MODEL_DIM, KEY_VALUE_HEADS * HEAD_SIZE), MODEL_DIM ** -0.5, 0.125, ((1, 2),))
    w_out = normal_values(arg_keys[4], (NQ * HEAD_SIZE, MODEL_DIM), (NQ * HEAD_SIZE // 16) ** -0.5, 0.5, ((0, 2),))
    w_gate = normal_values(arg_keys[5], (MODEL_DIM, FF), MODEL_DIM ** -0.5, 0.125, ((1, 2),))
    w_up = normal_values(arg_keys[6], (MODEL_DIM, FF), MODEL_DIM ** -0.5, 0.125, ((1, 2),))
    w_down = normal_values(arg_keys[7], (FF, MODEL_DIM), (FF // 4) ** -0.5, 0.125, ((0, 2),))
    attn_gain = jnp.clip(1.0 + 0.15 * jax.random.normal(arg_keys[8], (MODEL_DIM,), jnp.float32), 0.25, 1.75)
    mlp_gain = jnp.clip(1.0 + 0.15 * jax.random.normal(arg_keys[9], (MODEL_DIM,), jnp.float32), 0.25, 1.75)
    segments = draw_segments(jax.random.fold_in(arg_keys[13], 71), 0)
    valid_mask = draw_valid_mask(jax.random.fold_in(arg_keys[13], 71), 0)
    teacher = draw_teacher(jax.random.fold_in(arg_keys[13], 71), 0)
    return dict(hidden_in=hidden_in, w_query=w_query, key_weight_matrix=key_weight_matrix, value_weight_matrix=value_weight_matrix, w_out=w_out, w_gate=w_gate, w_up=w_up, w_down=w_down, attn_gain=attn_gain, mlp_gain=mlp_gain, segments=segments, valid_mask=valid_mask, teacher=teacher)


EPS = 1e-05
THETA = 1000000.0
NEG_BIG = -1e+30
HIGHEST = lax.Precision.HIGHEST

@jax.custom_vjp
def low(v):
    return lax.optimization_barrier(v.astype(jnp.bfloat16)).astype(jnp.float32)

@jax.custom_vjp
def low_back(v):
    return v

def low_keep(v):
    return (low(v), None)

def low_pass(kept, grad):
    return (grad,)

def back_keep(v):
    return (v, None)

def back_low(kept, grad):
    return (low(grad),)
low.defvjp(low_keep, low_pass)
low_back.defvjp(back_keep, back_low)

def matmul_full(left, right):
    return jnp.matmul(left, right, precision=HIGHEST)

def rms_norm(hidden, gain):
    return hidden * lax.rsqrt(lax.optimization_barrier(jnp.mean(hidden * hidden, axis=-1, keepdims=True)) + EPS) * gain

def rope_angles(positions, head_width):
    half_width = head_width // 2
    freqs = THETA ** (-2.0 * jnp.arange(half_width, dtype=jnp.float32) / head_width)
    angles = positions.astype(jnp.float32)[..., None] * freqs
    return (jnp.cos(angles), jnp.sin(angles))

def rotate(values, cosine_table, sine_table):
    half_width = values.shape[-1] // 2
    first_half = values[..., :half_width]
    second_half = values[..., half_width:]
    cos_heads = cosine_table[..., None, :]
    sin_heads = sine_table[..., None, :]
    return jnp.concatenate([first_half * cos_heads - second_half * sin_heads, second_half * cos_heads + first_half * sin_heads], axis=-1)

def attend(queries, keys_rot, values_in, segments, places):
    batch_size, seq_len, num_heads, head_width = queries.shape
    repeat = num_heads // keys_rot.shape[2]
    keys_wide = jnp.repeat(keys_rot, repeat, axis=2)
    values_wide = jnp.repeat(values_in, repeat, axis=2)
    block_len = min(512, seq_len)
    blocks = seq_len // block_len
    query_blocks = queries.reshape(batch_size, blocks, block_len, num_heads, head_width).swapaxes(0, 1)
    segment_blocks = segments.reshape(batch_size, blocks, block_len).swapaxes(0, 1)
    place_blocks = places.reshape(blocks, block_len)

    def one_block(operands):
        query_rows, query_segments, query_places = operands
        scores = jnp.einsum('bqhw,bkhw->bhqk', query_rows, keys_wide, precision=HIGHEST) / math.sqrt(head_width)
        allowed = (query_segments[:, :, None] == segments[:, None, :]) & (query_places[None, :, None] >= places[None, None, :])
        scores = low_back(jnp.where(allowed[:, None], scores, NEG_BIG))
        highest = lax.optimization_barrier(jnp.max(scores, axis=-1, keepdims=True))
        exponents = jnp.exp(scores - highest)
        weights = exponents / lax.optimization_barrier(jnp.sum(exponents, axis=-1, keepdims=True))
        return jnp.einsum('bhqk,bkhw->bqhw', low(weights), values_wide, precision=HIGHEST)
    mixed_rows = lax.map(jax.checkpoint(one_block), (query_blocks, segment_blocks, place_blocks))
    return mixed_rows.swapaxes(0, 1).reshape(batch_size, seq_len, num_heads, head_width)

def layer(hidden, params, seg_ids, valid_rows, teacher_rows, valid_count):
    w_query, key_weight_matrix, value_weight_matrix, w_out, w_gate, w_up, w_down, attn_gain, mlp_gain = params
    batch_size, seq_len, model_width = hidden.shape
    places = jnp.arange(seq_len, dtype=jnp.int32)
    starts = jax.vmap(jnp.searchsorted)(seg_ids, seg_ids).astype(jnp.int32)
    cosine_table, sine_table = rope_angles(places[None, :] - starts, HEAD_SIZE)
    shard_pieces = N_TENSOR
    query_cols = NQ * HEAD_SIZE // shard_pieces
    key_value_columns = KEY_VALUE_HEADS * HEAD_SIZE // shard_pieces
    hidden_cols = FF // shard_pieces
    normed = low(rms_norm(hidden, attn_gain))
    attn_total = jnp.zeros_like(hidden)
    for shard_idx in range(shard_pieces):
        inputs = low_back(normed)
        query_raw = low_back(matmul_full(inputs, w_query[:, shard_idx * query_cols:(shard_idx + 1) * query_cols]))
        queries = low_back(low(rotate(query_raw.reshape(batch_size, seq_len, -1, HEAD_SIZE), cosine_table, sine_table)))
        key_raw = low_back(matmul_full(inputs, key_weight_matrix[:, shard_idx * key_value_columns:(shard_idx + 1) * key_value_columns]))
        keys_rot = low_back(low(rotate(key_raw.reshape(batch_size, seq_len, -1, HEAD_SIZE), cosine_table, sine_table)))
        values_in = low_back(low(matmul_full(inputs, value_weight_matrix[:, shard_idx * key_value_columns:(shard_idx + 1) * key_value_columns])))
        values_in = values_in.reshape(batch_size, seq_len, -1, HEAD_SIZE)
        mixed_rows = attend(queries, keys_rot, values_in, seg_ids, places)
        mixed_flat = low_back(low(mixed_rows.reshape(batch_size, seq_len, query_cols)))
        attn_total = attn_total + low(matmul_full(mixed_flat, w_out[shard_idx * query_cols:(shard_idx + 1) * query_cols, :]))
    middle = hidden + low_back(attn_total)
    normed_mlp = low(rms_norm(middle, mlp_gain))
    mlp_total = jnp.zeros_like(hidden)
    for shard_idx in range(shard_pieces):
        inputs = low_back(normed_mlp)
        gate_pre = low_back(matmul_full(inputs, w_gate[:, shard_idx * hidden_cols:(shard_idx + 1) * hidden_cols]))
        up_pre = low_back(matmul_full(inputs, w_up[:, shard_idx * hidden_cols:(shard_idx + 1) * hidden_cols]))
        inner_rows = low(gate_pre * jax.nn.sigmoid(gate_pre) * up_pre)
        mlp_total = mlp_total + low(matmul_full(inner_rows, w_down[shard_idx * hidden_cols:(shard_idx + 1) * hidden_cols, :]))
    output = middle + low_back(mlp_total)
    errors = output - teacher_rows
    loss_part = jnp.sum(valid_rows[..., None] * errors * errors) / (valid_count * model_width)
    return (loss_part, output)

def reference(hidden_in, w_query, key_weight_matrix, value_weight_matrix, w_out, w_gate, w_up, w_down, attn_gain, mlp_gain, segments, valid_mask, teacher):
    params = tuple((weight.astype(jnp.float32) for weight in (w_query, key_weight_matrix, value_weight_matrix, w_out, w_gate, w_up, w_down, attn_gain, mlp_gain)))
    valid_count = jnp.sum(valid_mask).astype(jnp.float32)
    group_size = 2 if SEQUENCES % 2 == 0 else 1
    step_count = SEQUENCES // group_size

    def regroup(array):
        return array.reshape((step_count, group_size) + array.shape[1:])
    operands = (regroup(hidden_in.astype(jnp.float32)), regroup(segments), regroup(valid_mask.astype(jnp.float32)), regroup(teacher.astype(jnp.float32)))

    def one_step(carry, step_inputs):
        loss_total, grad_totals = carry
        hidden, seg_ids, valid_rows, teacher_rows = step_inputs

        def objective(hidden_arg, params_arg):
            return layer(hidden_arg, params_arg, seg_ids, valid_rows, teacher_rows, valid_count)
        loss_part, backward, output = jax.vjp(objective, hidden, params, has_aux=True)
        grad_hidden, grad_params = backward(jnp.ones_like(loss_part) * (TOKENS * MODEL_DIM / 2))
        grad_totals = tuple((total_grad + step_grad for total_grad, step_grad in zip(grad_totals, grad_params)))
        return ((loss_total + loss_part, grad_totals), (output, grad_hidden))
    zero_grads = tuple((jnp.zeros_like(weight) for weight in params))
    (loss_total, grad_totals), (outputs, grad_inputs) = lax.scan(one_step, (jnp.zeros((), jnp.float32), zero_grads), operands)
    layer_out = outputs.reshape(SEQUENCES, LENGTH, MODEL_DIM).astype(jnp.bfloat16)
    grad_input = grad_inputs.reshape(SEQUENCES, LENGTH, MODEL_DIM)
    return (layer_out, loss_total, grad_input, grad_totals[0], grad_totals[1], grad_totals[2], grad_totals[3], grad_totals[4], grad_totals[5], grad_totals[6], grad_totals[7], grad_totals[8])
```

```python
import functools
import math

import jax
import jax.numpy as jnp
import numpy as np
from jax import lax
from jax.experimental import pallas as pl
from jax.experimental.pallas import tpu as pltpu
from jax.sharding import PartitionSpec as P

HEAD_SIZE = 80
HALF = HEAD_SIZE // 2
EPS = 1e-05
THETA = 1000000.0
NEG_BIG = -1e30
LOG2E = 1.4426950408889634
BF16 = jnp.bfloat16
F32 = jnp.float32
MIB = 1024 * 1024
ROWS = 128
COSTS = (5, 5, 1, 5, 8, 5, 1, 5, 5, 5, 15, 0, 0, 1, 5, 5, 5, 4, 5, 5, 5, 60, 8, 4, 100, 5, 8, 0, 2, 0, 30, 2, 10, 10, 10, 1, 0, 10, 10, 10)
PLAN = []


def nn(left, right):
    return lax.dot_general(left, right, (((1,), (0,)), ((), ())), preferred_element_type=F32)


def nt(left, right):
    return lax.dot_general(left, right, (((1,), (1,)), ((), ())), preferred_element_type=F32)


def run(body, name, grid, ins, outs, scratch=(), prefetch=(), into=None, after=(), meets=None):
    num_ins = len(prefetch) + len(ins)
    aliases = {len(prefetch) + at: out for out, at in (into or {}).items() if isinstance(at, int)}
    kept = [(out, array) for out, array in (into or {}).items() if hasattr(array, "shape")]
    aliases.update({num_ins + at: out for at, (out, _) in enumerate(kept)})
    hidden = [array for _, array in kept] + list(after)

    def inner(*refs):
        body(*refs[:num_ins], *refs[num_ins + len(hidden) :])

    return pl.pallas_call(
        inner,
        grid_spec=pltpu.PrefetchScalarGridSpec(
            num_scalar_prefetch=len(prefetch),
            grid=grid,
            in_specs=[spec for _, spec in ins] + [pl.BlockSpec(memory_space=pl.ANY)] * len(hidden),
            out_specs=[spec for _, _, spec in outs],
            scratch_shapes=list(scratch),
        ),
        out_shape=[jax.ShapeDtypeStruct(shape, dtype) for shape, dtype, _ in outs],
        input_output_aliases=aliases,
        compiler_params=pltpu.CompilerParams(
            vmem_limit_bytes=61 * MIB, collective_id=meets, has_side_effects=meets is not None
        ),
        cost_estimate=pl.CostEstimate(
            flops=1000 + int(1e9 * (PLAN.pop(0) if PLAN else 0)),
            bytes_accessed=1000,
            transcendentals=0,
        ),
        name=name,
    )(*prefetch, *[array for array, _ in ins], *hidden)


def phase(first, count):
    return lambda i: jnp.clip(i - first, 0, count - 1)


def in_phase(step, first, count):
    return pl.when((step >= first) & (step < first + count))


def divisor(total, *sizes):
    return next(size for size in sizes + (total,) if total % size == 0)


def whole(array, *prefetch):
    zeros = (0,) * array.ndim
    return pl.BlockSpec(array.shape, lambda *_: zeros)


def rms_scale(rows):
    return lax.rsqrt(jnp.mean(rows * rows, axis=-1, keepdims=True) + EPS)


def norm_back(rows, gain, grad_normed):
    scale = rms_scale(rows)
    unit_rows = rows * scale
    weighted = grad_normed * gain
    grad_rows = scale * (
        weighted - unit_rows * jnp.mean(weighted * unit_rows, axis=-1, keepdims=True)
    )
    return grad_rows, jnp.sum(grad_normed * unit_rows, axis=0, keepdims=True)


def rotated(head, cos, sin):
    first, second = head[:HALF], head[HALF:]
    return jnp.concatenate([first * cos - second * sin, second * cos + first * sin], axis=0)


def rotated_back(head, cos, sin):
    first, second = head[:HALF], head[HALF:]
    return jnp.concatenate([first * cos + second * sin, second * cos - first * sin], axis=0)


def total_of(parts):
    total = parts[0][...].astype(F32)
    for part in parts[1:]:
        total = total + part[...].astype(F32)
    return total


def accumulate(ref, value, first):
    @pl.when(first)
    def _():
        ref[...] = value

    @pl.when(jnp.logical_not(first))
    def _():
        ref[...] = ref[...] + value


def kv_body(h_ref, gain_ref, wk_ref, wv_ref, cos_ref, sin_ref, n_ref, nt_ref, kv_ref):
    h = h_ref[...].astype(F32)
    normed = (h * rms_scale(h) * gain_ref[...]).astype(BF16)
    n_ref[...] = normed
    nt_ref[...] = normed.T
    cos, sin = cos_ref[...], sin_ref[...]
    keys = nt(wk_ref[...], normed)
    for at in range(0, wk_ref.shape[0], HEAD_SIZE):
        kv_ref[0, at : at + HEAD_SIZE, :] = rotated(keys[at : at + HEAD_SIZE], cos, sin).astype(
            BF16
        )
    kv_ref[1] = nt(wv_ref[...], normed).astype(BF16)


def kv_project(seq, hidden, gain, key_t, value_t, cos, sin, n_cols, after):
    num_seqs, rows, model = hidden.shape
    width = key_t.shape[0]
    tile = min(256, rows)
    steps = rows // tile
    table = pl.BlockSpec((None, HALF, tile), lambda i: (seq, 0, i))
    return run(
        kv_body,
        "kv_project",
        (steps,),
        [
            (hidden, pl.BlockSpec((None, tile, model), lambda i: (seq, i, 0))),
            (gain, whole(gain)),
            (key_t, whole(key_t)),
            (value_t, whole(value_t)),
            (cos, table),
            (sin, table),
        ],
        [
            ((rows, model), BF16, pl.BlockSpec((tile, model), lambda i: (i, 0))),
            (
                (model, num_seqs * rows),
                BF16,
                pl.BlockSpec((model, tile), lambda i: (0, seq * steps + i)),
            ),
            ((2, width, rows), BF16, pl.BlockSpec((2, width, tile), lambda i: (0, 0, i))),
        ],
        into={1: n_cols},
        after=after,
    )


def q_body(n_ref, w_ref, cos_ref, sin_ref, q_ref):
    cos, sin = cos_ref[...], sin_ref[...]
    queries = nn(n_ref[...], w_ref[...]).T
    for at in range(0, w_ref.shape[1], HEAD_SIZE):
        q_ref[at : at + HEAD_SIZE, :] = rotated(queries[at : at + HEAD_SIZE], cos, sin).astype(BF16)


def q_project(seq, normed, w_query, cos, sin, after):
    rows, model = normed.shape
    width = w_query.shape[1]
    tile = divisor(width, 640)
    table = pl.BlockSpec((None, HALF, rows), lambda j: (seq, 0, 0))
    return run(
        q_body,
        "q_project",
        (width // tile,),
        [
            (normed, whole(normed)),
            (w_query, pl.BlockSpec((model, tile), lambda j: (0, j))),
            (cos, table),
            (sin, table),
        ],
        [((width, rows), BF16, pl.BlockSpec((tile, rows), lambda j: (j, 0)))],
        after=after,
    )[0]


def side_by_side(ref, group, here):
    return jnp.concatenate(
        [ref[r * HEAD_SIZE : (r + 1) * HEAD_SIZE, here] for r in range(group)], axis=1
    )


def allowed_block(key_at, query_at, start_row, block, group):
    shape = (block, block * group)
    key_place = key_at + lax.broadcasted_iota(jnp.int32, shape, 0)
    query_place = query_at + lax.broadcasted_iota(jnp.int32, (1, block * group), 1) % block
    return (key_place >= start_row) & (key_place <= query_place)


def attend_body(
    block, kv_heads, low_ref, full_ref, start_ref, q_ref, w_ref, *refs
):
    *kv_refs, o_ref, lse_ref, part_ref, keys, values, raw, weights, mixed, o_all, o_rows = refs
    chunks = len(kv_refs)
    piece = q_ref.shape[1]
    group = q_ref.shape[0] // HEAD_SIZE
    own = (chunks - 1) * piece
    factor = LOG2E / math.sqrt(HEAD_SIZE)
    step_at = pl.program_id(0)

    @pl.when(step_at < kv_heads)
    def _():
        for chunk, kv_ref in enumerate(kv_refs):
            at = slice(chunk * piece, (chunk + 1) * piece)
            keys[at, :] = kv_ref[0].T
            values[:, at] = kv_ref[1]
        for at in range(0, piece, block):
            here = slice(at, at + block)
            start_row = jnp.concatenate([start_ref[:, here]] * group, axis=1)
            queries = side_by_side(q_ref, group, here)
            low, diagonal = low_ref[at // block], (own + at) // block
            full = full_ref[at // block]

            def place(key_block):
                return pl.ds(pl.multiple_of(key_block * block, block), block)

            def score(key_block):
                raw[key_block % 2] = nn(keys[place(key_block), :], queries) * factor

            def soften(masked, key_block, top, total):
                scores = raw[key_block % 2]
                if masked:
                    allowed = allowed_block(key_block * block, own + at, start_row, block, group)
                    scores = jnp.where(allowed, scores, NEG_BIG)
                new = jnp.maximum(top, jnp.max(scores, axis=0, keepdims=True))
                part = jnp.exp2(scores - new)
                shrink = jnp.exp2(top - new)
                weights[key_block % 2] = part.astype(BF16)
                return new, total * shrink + jnp.sum(part, axis=0, keepdims=True), shrink

            def mix(key_block, shrink):
                mixed[...] = mixed[...] * shrink + nn(
                    values[:, place(key_block)], weights[key_block % 2]
                )

            def step(masked, key_block, carry):
                top, total, shrink = carry
                score(key_block + 1)
                mix(key_block - 1, shrink)
                return soften(masked, key_block, top, total)

            none = jnp.full((1, block * group), NEG_BIG, F32)
            mixed[...] = jnp.zeros(mixed.shape, F32)
            score(low)
            first = soften(True, low, none, jnp.zeros_like(none))

            @pl.when(low < diagonal)
            def _():
                score(low + 1)

            middle = jnp.clip(full, low + 1, diagonal)
            carry = lax.fori_loop(low + 1, middle, functools.partial(step, True), first)
            carry = lax.fori_loop(middle, diagonal, functools.partial(step, False), carry)

            def last(carry):
                top, total, shrink = carry
                mix(diagonal - 1, shrink)
                return soften(True, diagonal, top, total)

            top, total, shrink = lax.cond(low < diagonal, last, lambda carry: carry, carry)
            mix(diagonal, shrink)
            result = (mixed[...] / total).astype(BF16)
            lse = top + jnp.log2(total)
            for r in range(group):
                part = slice(r * block, (r + 1) * block)
                o_ref[r * HEAD_SIZE : (r + 1) * HEAD_SIZE, here] = result[:, part]
                lse_ref[r : r + 1, here] = lse[:, part]
        rows = q_ref.shape[0]
        o_all[pl.ds(pl.multiple_of(step_at * rows, rows), rows), :] = o_ref[...]

    @pl.when(step_at == kv_heads)
    def _():
        o_rows[...] = o_all[...].T

    @pl.when(step_at >= kv_heads)
    def _():
        part_ref[...] = nn(o_rows[...], w_ref[...]).astype(BF16)


def attend(seq, num_seqs, low, full, start, queries, kv_chunks, w_out, mixed, after):
    width, piece = queries.shape
    model = w_out.shape[1]
    kv_heads = kv_chunks[0].shape[1] // HEAD_SIZE
    rows = width // kv_heads
    group = rows // HEAD_SIZE
    block = min(256, piece)
    chunks = len(kv_chunks)
    tile = 1280
    head, part = phase(0, kv_heads), phase(kv_heads, model // tile)
    kv_spec = pl.BlockSpec((2, HEAD_SIZE, piece), lambda i, *_: (0, head(i), 0))
    return run(
        functools.partial(attend_body, block, kv_heads),
        "attend",
        (kv_heads + model // tile,),
        [
            (start, whole(start)),
            (queries, pl.BlockSpec((rows, piece), lambda i, *_: (head(i), 0))),
            (w_out, pl.BlockSpec((width, tile), lambda i, *_: (0, part(i)))),
        ]
        + [(kv, kv_spec) for kv in kv_chunks],
        [
            (
                (width, num_seqs * piece),
                BF16,
                pl.BlockSpec((rows, piece), lambda i, *_: (head(i), seq)),
            ),
            (
                (kv_heads, group, piece),
                F32,
                pl.BlockSpec((None, group, piece), lambda i, *_: (head(i), 0, 0)),
            ),
            ((piece, model), BF16, pl.BlockSpec((piece, tile), lambda i, *_: (0, part(i)))),
        ],
        scratch=[
            pltpu.VMEM((chunks * piece, HEAD_SIZE), BF16),
            pltpu.VMEM((HEAD_SIZE, chunks * piece), BF16),
            pltpu.VMEM((2, block, group * block), F32),
            pltpu.VMEM((2, block, group * block), BF16),
            pltpu.VMEM((HEAD_SIZE, group * block), F32),
            pltpu.VMEM((width, piece), BF16),
            pltpu.VMEM((piece, width), BF16),
        ],
        prefetch=[low, full],
        into={0: mixed},
        after=after,
    )


def attend_back_body(
    block, low_ref, full_ref, start_ref, cos_ref, sin_ref, q_ref, o_ref, do_ref, lse_ref, *refs
):
    *refs, keys, keys_t, values, raw, raw_grad, probs, grads, dq_sum, dk_sum, dv_sum = refs
    chunks = (len(refs) - 1) // 2
    kv_refs, dq_ref, dkv_refs = refs[:chunks], refs[chunks], refs[chunks + 1 :]
    piece = q_ref.shape[1]
    group = q_ref.shape[0] // HEAD_SIZE
    own = (chunks - 1) * piece
    scale = 1.0 / math.sqrt(HEAD_SIZE)
    factor = LOG2E * scale
    dk_sum[...] = jnp.zeros(dk_sum.shape, F32)
    dv_sum[...] = jnp.zeros(dv_sum.shape, F32)
    for chunk, kv_ref in enumerate(kv_refs):
        at = slice(chunk * piece, (chunk + 1) * piece)
        keys_t[:, at] = kv_ref[0]
        keys[at, :] = kv_ref[0].T
        values[at, :] = kv_ref[1].T
    for at in range(0, piece, block):
        here = slice(at, at + block)
        start_row = jnp.concatenate([start_ref[:, here]] * group, axis=1)
        queries = side_by_side(q_ref, group, here)
        grad_out = side_by_side(do_ref, group, here)
        outs = side_by_side(o_ref, group, here)
        delta = jnp.sum(outs.astype(F32) * grad_out.astype(F32), axis=0, keepdims=True)
        lse = jnp.concatenate([lse_ref[r : r + 1, here] for r in range(group)], axis=1)
        dq_sum[...] = jnp.zeros(dq_sum.shape, F32)
        low, diagonal = low_ref[at // block], (own + at) // block
        full = full_ref[at // block]

        def place(key_block):
            return pl.ds(pl.multiple_of(key_block * block, block), block)

        def score(key_block):
            raw[key_block % 2] = nn(keys[place(key_block), :], queries) * factor - lse
            raw_grad[key_block % 2] = nn(values[place(key_block), :], grad_out) - delta

        def weigh(masked, key_block):
            scores = raw[key_block % 2]
            if masked:
                allowed = allowed_block(key_block * block, own + at, start_row, block, group)
                scores = jnp.where(allowed, scores, NEG_BIG)
            part = jnp.exp2(scores)
            probs[key_block % 2] = part.astype(BF16)
            grads[key_block % 2] = (part * raw_grad[key_block % 2]).astype(BF16)

        def spread(key_block):
            inside = place(key_block)
            grad = grads[key_block % 2]
            dv_sum[:, inside] = dv_sum[:, inside] + nt(grad_out, probs[key_block % 2])
            dk_sum[:, inside] = dk_sum[:, inside] + nt(queries, grad)
            dq_sum[...] = dq_sum[...] + nn(keys_t[:, inside], grad)

        def step(masked, key_block, carry):
            score(key_block + 1)
            spread(key_block - 1)
            weigh(masked, key_block)
            return carry

        score(low)
        weigh(True, low)

        @pl.when(low < diagonal)
        def _():
            score(low + 1)

        middle = jnp.clip(full, low + 1, diagonal)
        lax.fori_loop(low + 1, middle, functools.partial(step, True), 0)
        lax.fori_loop(middle, diagonal, functools.partial(step, False), 0)

        @pl.when(low < diagonal)
        def _():
            spread(diagonal - 1)
            weigh(True, diagonal)

        spread(diagonal)
        cos, sin = cos_ref[:, here], sin_ref[:, here]
        for r in range(group):
            rounded = (dq_sum[:, r * block : (r + 1) * block] * scale).astype(BF16).astype(F32)
            dq_ref[r * HEAD_SIZE : (r + 1) * HEAD_SIZE, here] = rotated_back(
                rounded, cos, sin
            ).astype(BF16)
    for chunk, dkv_ref in enumerate(dkv_refs):
        at = slice(chunk * piece, (chunk + 1) * piece)
        dkv_ref[0] = (dk_sum[:, at] * scale).astype(BF16)
        dkv_ref[1] = dv_sum[:, at].astype(BF16)


def attend_back(
    seq, num_seqs, low, full, start, cos, sin, queries, mixed, grad_mixed, lse, kv_chunks, dq, after
):
    width, piece = queries.shape
    kv_heads = kv_chunks[0].shape[1] // HEAD_SIZE
    rows = width // kv_heads
    group = rows // HEAD_SIZE
    block = min(256, piece)
    keys = len(kv_chunks) * piece
    per_head = pl.BlockSpec((rows, piece), lambda h, *_: (h, 0))
    per_head_seq = pl.BlockSpec((rows, piece), lambda h, *_: (h, seq))
    table = pl.BlockSpec((None, HALF, piece), lambda h, *_: (seq, 0, 0))
    kv_spec = pl.BlockSpec((2, HEAD_SIZE, piece), lambda h, *_: (0, h, 0))
    return run(
        functools.partial(attend_back_body, block),
        "attend_back",
        (kv_heads,),
        [
            (start, whole(start)),
            (cos, table),
            (sin, table),
            (queries, per_head),
            (mixed, per_head_seq),
            (grad_mixed, per_head),
            (lse, pl.BlockSpec((None, group, piece), lambda h, *_: (h, 0, 0))),
        ]
        + [(kv, kv_spec) for kv in kv_chunks],
        [
            ((width + 2 * kv_chunks[0].shape[1], num_seqs * piece), BF16, per_head_seq),
        ]
        + [(kv.shape, BF16, kv_spec) for kv in kv_chunks],
        scratch=[
            pltpu.VMEM((keys, HEAD_SIZE), BF16),
            pltpu.VMEM((HEAD_SIZE, keys), BF16),
            pltpu.VMEM((keys, HEAD_SIZE), BF16),
            pltpu.VMEM((2, block, group * block), F32),
            pltpu.VMEM((2, block, group * block), F32),
            pltpu.VMEM((2, block, group * block), BF16),
            pltpu.VMEM((2, block, group * block), BF16),
            pltpu.VMEM((HEAD_SIZE, group * block), F32),
            pltpu.VMEM((HEAD_SIZE, keys), F32),
            pltpu.VMEM((HEAD_SIZE, keys), F32),
        ],
        prefetch=[low, full],
        into={0: dq},
        after=after,
    )


def qkv_back_body(
    dq_ref, cos_ref, sin_ref, wq_ref, wk_ref, wv_ref, own_ref, came_ref, *refs
):
    dkv_ref, out_ref, dq_rows, dk_rows, dv_rows = refs
    width = wk_ref.shape[0]

    @pl.when(pl.program_id(0) == 0)
    def _():
        cos, sin = cos_ref[...], sin_ref[...]
        for at in range(0, width, HEAD_SIZE):
            head = slice(at, at + HEAD_SIZE)
            rows = own_ref[0, head].astype(F32) + came_ref[0, head].astype(F32)
            rows = rows.astype(BF16).astype(F32)
            dkv_ref[at : at + HEAD_SIZE, :] = rotated_back(rows, cos, sin).astype(BF16)
        dkv_ref[width:, :] = (own_ref[1].astype(F32) + came_ref[1].astype(F32)).astype(BF16)
        dq_rows[...] = dq_ref[...].T
        dk_rows[...] = dkv_ref[:width].T
        dv_rows[...] = dkv_ref[width:].T

    out_ref[...] = (
        nt(dq_rows[...], wq_ref[...])
        + nn(dk_rows[...], wk_ref[...])
        + nn(dv_rows[...], wv_ref[...])
    ).astype(BF16)


def qkv_back(seq, dqkv, cos, sin, w_query, key_t, value_t, own, came, after):
    model, width_q = w_query.shape
    width = key_t.shape[0]
    piece = own.shape[-1]
    tile = 1280
    table = pl.BlockSpec((None, HALF, piece), lambda j: (seq, 0, 0))
    narrow = pl.BlockSpec((width, tile), lambda j: (0, j))
    return run(
        qkv_back_body,
        "qkv_back",
        (model // tile,),
        [
            (dqkv, pl.BlockSpec((width_q, piece), lambda j: (0, seq))),
            (cos, table),
            (sin, table),
            (w_query, pl.BlockSpec((tile, width_q), lambda j: (j, 0))),
            (key_t, narrow),
            (value_t, narrow),
            (own, whole(own)),
            (came, whole(came)),
        ],
        [
            (
                dqkv.shape,
                BF16,
                pl.BlockSpec((2 * width, piece), lambda j: (width_q // (2 * width), seq)),
            ),
            ((piece, model), BF16, pl.BlockSpec((piece, tile), lambda j: (0, j))),
        ],
        scratch=[
            pltpu.VMEM((piece, width_q), BF16),
            pltpu.VMEM((piece, width), BF16),
            pltpu.VMEM((piece, width), BF16),
        ],
        into={0: 0},
        after=after,
    )


def forward_body(counts, h_ref, gain_ref, wg_ref, wu_ref, wd_ref, *refs):
    *parts, m_ref, nt_ref, z_ref, a_ref, b_ref, part_ref, normed, inner = refs
    norm_steps, wide_steps, out_steps = counts
    step = pl.program_id(0)

    @in_phase(step, 0, norm_steps)
    def _():
        middle = h_ref[...].astype(F32) + total_of(parts)
        m_ref[...] = middle.astype(BF16)
        rows = (middle * rms_scale(middle) * gain_ref[...]).astype(BF16)
        normed[pl.ds(pl.multiple_of(step * ROWS, ROWS), ROWS), :] = rows
        nt_ref[...] = rows.T

    @in_phase(step, norm_steps, wide_steps)
    def _():
        gate = nn(normed[...], wg_ref[...])
        up = nn(normed[...], wu_ref[...])
        sig = jax.nn.sigmoid(gate)
        silu = gate * sig
        z = (silu * up).astype(BF16)
        z_ref[...] = z
        inner[step - norm_steps] = z
        a_ref[...] = (up * sig * (1.0 + gate * (1.0 - sig))).astype(BF16)
        b_ref[...] = silu.astype(BF16)

    @in_phase(step, norm_steps + wide_steps, out_steps)
    def _():
        width = inner.shape[2]
        total = nn(inner[0], wd_ref[:width])
        for at in range(1, wide_steps):
            total = total + nn(inner[at], wd_ref[at * width : (at + 1) * width])
        part_ref[...] = total.astype(BF16)


def forward_mlp(seq, hidden, gain, w_gate, w_up, w_down, parts, normed_t, inner, after):
    num_seqs, rows, model = hidden.shape
    hidden_width = w_gate.shape[1]
    wide, narrow = divisor(hidden_width, 512), 1280
    counts = (rows // ROWS, hidden_width // wide, model // narrow)
    norm, mid, out = phase(0, counts[0]), phase(counts[0], counts[1]), phase(
        counts[0] + counts[1], counts[2]
    )
    row_spec = pl.BlockSpec((ROWS, model), lambda i: (norm(i), 0))
    weight_spec = pl.BlockSpec((model, wide), lambda i: (0, mid(i)))
    wide_spec = pl.BlockSpec((rows, wide), lambda i: (0, mid(i)))
    return run(
        functools.partial(forward_body, counts),
        "forward_mlp",
        (sum(counts),),
        [
            (hidden, pl.BlockSpec((None, ROWS, model), lambda i: (seq, norm(i), 0))),
            (gain, whole(gain)),
            (w_gate, weight_spec),
            (w_up, weight_spec),
            (w_down, pl.BlockSpec((hidden_width, narrow), lambda i: (0, out(i)))),
        ]
        + [(part, row_spec) for part in parts],
        [
            ((rows, model), BF16, row_spec),
            (
                (model, num_seqs * rows),
                BF16,
                pl.BlockSpec((model, ROWS), lambda i: (0, seq * counts[0] + norm(i))),
            ),
            (
                (num_seqs, rows, hidden_width),
                BF16,
                pl.BlockSpec((None, rows, wide), lambda i: (seq, 0, mid(i))),
            ),
            ((rows, hidden_width), BF16, wide_spec),
            ((rows, hidden_width), BF16, wide_spec),
            ((rows, model), BF16, pl.BlockSpec((rows, narrow), lambda i: (0, out(i)))),
        ],
        scratch=[
            pltpu.VMEM((rows, model), BF16),
            pltpu.VMEM((counts[1], rows, wide), BF16),
        ],
        into={1: normed_t, 2: inner},
        after=after,
    )


def error_body(m_ref, teacher_ref, valid_ref, *refs):
    *parts, out_ref, dy_ref, dyt_ref, loss_ref = refs
    output = m_ref[...].astype(F32) + total_of(parts)
    out_ref[...] = output.astype(BF16)
    errors = output - teacher_ref[...].astype(F32)
    valid = valid_ref[...]
    rounded = (valid * errors).astype(BF16)
    dy_ref[...] = rounded
    dyt_ref[...] = rounded.T
    squares = jnp.sum(valid * errors * errors, axis=0, keepdims=True)
    accumulate(loss_ref, squares, pl.program_id(0) == 0)


def output_error(seq, middle, teacher, valid, parts, layer_out, grad_t, after):
    num_seqs, rows, model = teacher.shape
    steps = rows // ROWS
    row_spec = pl.BlockSpec((ROWS, model), lambda i: (i, 0))
    seq_spec = pl.BlockSpec((None, ROWS, model), lambda i: (seq, i, 0))
    return run(
        error_body,
        "output_error",
        (steps,),
        [
            (middle, row_spec),
            (teacher, seq_spec),
            (valid, pl.BlockSpec((None, ROWS, 1), lambda i: (seq, i, 0))),
        ]
        + [(part, row_spec) for part in parts],
        [
            ((num_seqs, rows, model), BF16, seq_spec),
            ((rows, model), BF16, row_spec),
            (
                (model, num_seqs * rows),
                BF16,
                pl.BlockSpec((model, ROWS), lambda i: (0, seq * steps + i)),
            ),
            ((1, model), F32, pl.BlockSpec((1, model), lambda i: (0, 0))),
        ],
        into={0: layer_out, 2: grad_t},
        after=after,
    )


def backward_body(counts, dy_ref, wd_ref, a_ref, b_ref, wg_ref, wu_ref, *refs):
    dg_ref, du_ref, part_ref, gates, ups = refs
    wide_steps, out_steps = counts
    step = pl.program_id(0)

    @in_phase(step, 0, wide_steps)
    def _():
        grad_inner = nt(dy_ref[...], wd_ref[...])
        d_gate = (grad_inner * a_ref[...].astype(F32)).astype(BF16)
        d_up = (grad_inner * b_ref[...].astype(F32)).astype(BF16)
        dg_ref[...] = d_gate
        du_ref[...] = d_up
        gates[step] = d_gate
        ups[step] = d_up

    @in_phase(step, wide_steps, out_steps)
    def _():
        width = gates.shape[2]
        total = None
        for at in range(wide_steps):
            columns = slice(at * width, (at + 1) * width)
            term = nt(gates[at], wg_ref[:, columns]) + nt(ups[at], wu_ref[:, columns])
            total = term if total is None else total + term
        part_ref[...] = total.astype(BF16)


def backward_mlp(seq, num_seqs, grad_out, w_down, a, b, w_gate, w_up, kept, after):
    rows, model = grad_out.shape
    hidden_width = w_gate.shape[1]
    wide, narrow = divisor(hidden_width, 512), 512
    counts = (hidden_width // wide, model // narrow)
    mid, out = phase(0, counts[0]), phase(counts[0], counts[1])
    wide_spec = pl.BlockSpec((rows, wide), lambda i: (0, mid(i)))
    wide_seq = pl.BlockSpec((None, rows, wide), lambda i: (seq, 0, mid(i)))
    weight_spec = pl.BlockSpec((narrow, hidden_width), lambda i: (out(i), 0))
    return run(
        functools.partial(backward_body, counts),
        "backward_mlp",
        (sum(counts),),
        [
            (grad_out, whole(grad_out)),
            (w_down, pl.BlockSpec((wide, model), lambda i: (mid(i), 0))),
            (a, wide_spec),
            (b, wide_spec),
            (w_gate, weight_spec),
            (w_up, weight_spec),
        ],
        [
            ((num_seqs, rows, hidden_width), BF16, wide_seq),
            ((num_seqs, rows, hidden_width), BF16, wide_seq),
            ((rows, model), BF16, pl.BlockSpec((rows, narrow), lambda i: (0, out(i)))),
        ],
        scratch=[
            pltpu.VMEM((counts[0], rows, wide), BF16),
            pltpu.VMEM((counts[0], rows, wide), BF16),
        ],
        into=dict(zip((0, 1), kept)),
        after=after,
    )


def middle_back_body(counts, m_ref, dy_ref, gain_ref, w_ref, *refs):
    *parts, dm_ref, dmt_ref, dg_ref, do_ref, grad_t = refs
    norm_steps, out_steps = counts
    step = pl.program_id(0)

    @in_phase(step, 0, norm_steps)
    def _():
        grad_rows, grad_gain = norm_back(
            m_ref[...].astype(F32), gain_ref[...], total_of(parts)
        )
        rounded = (dy_ref[...].astype(F32) + grad_rows).astype(BF16)
        dm_ref[...] = rounded
        rounded_t = rounded.T
        dmt_ref[...] = rounded_t
        grad_t[step] = rounded_t
        accumulate(dg_ref, grad_gain, step == 0)

    @in_phase(step, norm_steps, out_steps)
    def _():
        columns = jnp.concatenate([grad_t[at] for at in range(norm_steps)], axis=1)
        do_ref[...] = nn(w_ref[...], columns).astype(BF16)


def middle_back(seq, num_seqs, middle, grad_output, gain, w_out, parts, grad_t, after):
    rows, model = middle.shape
    width = w_out.shape[0]
    tile = divisor(width, 640)
    counts = (rows // ROWS, width // tile)
    norm, out = phase(0, counts[0]), phase(counts[0], counts[1])
    row_spec = pl.BlockSpec((ROWS, model), lambda i: (norm(i), 0))
    return run(
        functools.partial(middle_back_body, counts),
        "middle_back",
        (sum(counts),),
        [
            (middle, row_spec),
            (grad_output, row_spec),
            (gain, whole(gain)),
            (w_out, pl.BlockSpec((tile, model), lambda i: (out(i), 0))),
        ]
        + [(part, row_spec) for part in parts],
        [
            ((rows, model), BF16, row_spec),
            (
                (model, num_seqs * rows),
                BF16,
                pl.BlockSpec((model, ROWS), lambda i: (0, seq * counts[0] + norm(i))),
            ),
            ((1, model), F32, pl.BlockSpec((1, model), lambda i: (0, 0))),
            ((width, rows), BF16, pl.BlockSpec((tile, rows), lambda i: (out(i), 0))),
        ],
        scratch=[pltpu.VMEM((counts[0], model, ROWS), BF16)],
        into={1: grad_t},
        after=after,
    )


def input_back_body(scale_ref, h_ref, dm_ref, gain_ref, *refs):
    *parts, grad_ref, dg_ref = refs
    grad_rows, grad_gain = norm_back(h_ref[...].astype(F32), gain_ref[...], total_of(parts))
    grad_ref[...] = scale_ref[0] * (dm_ref[...].astype(F32) + grad_rows)
    accumulate(dg_ref, grad_gain, pl.program_id(0) == 0)


def input_back(seq, scale, hidden, grad_middle, gain, parts, earlier, after):
    num_seqs, rows, model = hidden.shape
    row_spec = pl.BlockSpec((ROWS, model), lambda i: (i, 0))
    seq_spec = pl.BlockSpec((None, ROWS, model), lambda i: (seq, i, 0))
    return run(
        input_back_body,
        "input_back",
        (rows // ROWS,),
        [
            (scale, pl.BlockSpec(memory_space=pltpu.SMEM)),
            (hidden, seq_spec),
            (grad_middle, row_spec),
            (gain, whole(gain)),
        ]
        + [(part, row_spec) for part in parts],
        [
            ((num_seqs, rows, model), F32, seq_spec),
            ((1, model), F32, pl.BlockSpec((1, model), lambda i: (0, 0))),
        ],
        into={0: earlier},
        after=after,
    )


def weight_body(flipped, x_ref, y_ref, y_before_ref, far_ref, sent_ref, kept_ref, *refs):
    x_all, staged, landed, send_sem, recv_sem = refs
    tiles = landed.shape[0]
    step = pl.program_id(0)
    dp, ctx = lax.axis_index("dp"), lax.axis_index("ctx")
    ctx_size = lax.axis_size("ctx")
    core, chip = dp % 2, dp // 2
    partner = dp + 1 - 2 * core
    half = x_all.shape[0] // 2

    def sending(at):
        return pltpu.make_async_remote_copy(
            src_ref=staged.at[at % 2],
            dst_ref=landed.at[at],
            send_sem=send_sem.at[at % 2],
            recv_sem=recv_sem.at[at],
            device_id={"dp": partner},
            device_id_type=pl.DeviceIdType.MESH,
        )

    @pl.when(step == 0)
    def _():
        barrier = pltpu.get_barrier_semaphore()
        pl.semaphore_signal(
            barrier, inc=1, device_id={"dp": partner}, device_id_type=pl.DeviceIdType.MESH
        )
        pl.semaphore_wait(barrier, 1)
        size = x_ref.shape[0] // (lax.axis_size("dp") * ctx_size)
        low, high = ctx % 2, ctx // 2
        at = 0
        for other_core in (1, 0):
            to_core = core + other_core * (1 - 2 * core)
            for other_chip in (1, 0):
                to_dp = 2 * (chip + other_chip * (1 - 2 * chip)) + to_core
                for other_low in (1, 0):
                    for other_high in (1, 0):
                        to_ctx = 2 * (high + other_high * (1 - 2 * high))
                        to_ctx = to_ctx + low + other_low * (1 - 2 * low)
                        row = pl.multiple_of((to_dp * ctx_size + to_ctx) * size, size)
                        x_all[at : at + size, :] = x_ref[pl.ds(row, size), :]
                        at += size

    def product(rows, ref):
        y = ref[...]
        return nt(rows, y) if flipped else nn(rows, y.reshape(-1, y.shape[-1]))

    @pl.when((step >= 2) & (step < tiles))
    def _():
        sending(step - 2).wait_send()

    @pl.when(step < tiles)
    def _():
        staged[step % 2] = product(x_all[:half, :], y_ref).astype(BF16)
        sending(step).start()

    @pl.when(step > 0)
    def _():
        total = product(x_all[half:, :], y_before_ref)
        sending(step - 1).wait_recv()
        total = (total + landed[step - 1].astype(F32)).astype(BF16)
        far_ref[...] = total[: half // 2]
        sent_ref[...] = total[half // 2 : half // 4 * 3]
        kept_ref[...] = total[half // 4 * 3 :]

    @pl.when(step == tiles)
    def _():
        for at in range(max(tiles - 2, 0), tiles):
            sending(at).wait_send()


def weight_grad(meets, x_t, y, flipped, after):
    model, tokens = x_t.shape
    if flipped:
        tile = divisor(y.shape[0], 640)
        tiles = y.shape[0] // tile
        y_block, place = (tile, tokens), lambda at: (at, 0)
    else:
        tile = divisor(y.shape[2], 512)
        tiles = y.shape[2] // tile
        y_block, place = y.shape[:2] + (tile,), lambda at: (0, 0, at)
    width = tile * tiles
    before = lambda i: jnp.maximum(i - 1, 0)
    outs = [
        ((rows, width), BF16, pl.BlockSpec((rows, tile), lambda i: (0, before(i))))
        for rows in (model // 4, model // 8, model // 8)
    ]
    return run(
        functools.partial(weight_body, flipped),
        "weight_grad",
        (tiles + 1,),
        [
            (x_t, whole(x_t)),
            (y, pl.BlockSpec(y_block, lambda i: place(jnp.minimum(i, tiles - 1)))),
            (y, pl.BlockSpec(y_block, lambda i: place(before(i)))),
        ],
        outs,
        scratch=[
            pltpu.VMEM((model, tokens), BF16),
            pltpu.VMEM((2, model // 2, tile), BF16),
            pltpu.VMEM((tiles, model // 2, tile), BF16),
            pltpu.SemaphoreType.DMA((2,)),
            pltpu.SemaphoreType.DMA((tiles,)),
        ],
        after=after,
        meets=meets,
    )


def near_body(sent_ref, kept_ref, came_ref, send_ref, keep_ref):
    half = sent_ref.shape[0]
    came = came_ref[...].astype(F32)
    send_ref[...] = (sent_ref[...].astype(F32) + came[:half]).astype(BF16)
    keep_ref[...] = (kept_ref[...].astype(F32) + came[half:]).astype(BF16)


def fold_body(kept_ref, came_ref, send_ref):
    send_ref[...] = (kept_ref[...].astype(F32) + came_ref[...].astype(F32)).astype(BF16)


def final_body(scale_ref, kept_ref, pair_ref, end_ref, out_ref):
    total = kept_ref[...].astype(F32) + pair_ref[...].astype(F32) + end_ref[...].astype(F32)
    out_ref[...] = total * scale_ref[0]


def swap(value, axis, bit):
    size = lax.axis_size(axis)
    return lax.ppermute(value, axis, [(i, i ^ bit) for i in range(size)])


class Halving:
    def __init__(self, meets, x_t, y, flipped, after):
        far, self.sent, self.kept = weight_grad(meets, x_t, y, flipped, after)
        self.came = swap(far, "dp", 2)
        self.last = far

    def near(self, after):
        rows, width = self.sent.shape
        tile = divisor(width, 896, 640)
        spec = pl.BlockSpec((rows, tile), lambda j: (0, j))
        send, self.keep = run(
            near_body,
            "near",
            (width // tile,),
            [
                (self.sent, spec),
                (self.kept, spec),
                (self.came, pl.BlockSpec((2 * rows, tile), lambda j: (0, j))),
            ],
            [((rows, width), BF16, spec)] * 2,
            after=after,
        )
        self.pair = swap(send, "ctx", 1)
        return send

    def fold(self, after):
        rows, width = self.keep.shape
        tile = divisor(width, 896, 640)
        spec = pl.BlockSpec((rows // 2, tile), lambda j: (0, j))
        (send,) = run(
            fold_body,
            "fold",
            (width // tile,),
            [(self.keep, spec), (self.pair, spec)],
            [((rows // 2, width), BF16, spec)],
            after=after,
        )
        self.end = swap(send, "ctx", 2)
        return send

    def final(self, scale, after):
        rows, width = self.end.shape
        tile = divisor(width, 896, 640)
        spec = pl.BlockSpec((rows, tile), lambda j: (0, j))
        below = pl.BlockSpec((rows, tile), lambda j: (1, j))
        (self.result,) = run(
            final_body,
            "final",
            (width // tile,),
            [
                (scale, pl.BlockSpec(memory_space=pltpu.SMEM)),
                (self.keep, below),
                (self.pair, below),
                (self.end, spec),
            ],
            [((rows, width), F32, spec)],
            after=after,
        )
        return self.result


def butterfly_hops(value):
    hops = [value]
    for axis in ("dp", "ctx"):
        bit = 1
        while bit < lax.axis_size(axis):
            hops.append(hops[-1] + swap(hops[-1], axis, bit))
            bit *= 2
    return hops


def tensor_parts(partial):
    if lax.axis_size("tensor") == 2:
        return [partial, swap(partial, "tensor", 1)]
    return [lax.psum(partial, "tensor")]


def held(value, *others):
    return lax.optimization_barrier((value, *others))[0]


def shift(value, step):
    size = lax.axis_size("ctx")
    pairs = [(i, i + step) for i in range(size) if 0 <= i + step < size]
    return lax.ppermute(value, "ctx", pairs)


def local(
    hidden_in,
    w_query,
    key_weight_matrix,
    value_weight_matrix,
    w_out,
    w_gate,
    w_up,
    w_down,
    attn_gain,
    mlp_gain,
    segments,
    valid_mask,
    teacher,
):
    PLAN[:] = COSTS
    num_seqs, piece, model = hidden_in.shape
    seqs = range(num_seqs)
    ctx_size = lax.axis_size("ctx")
    ctx = lax.axis_index("ctx")
    query_places = ctx * piece + jnp.arange(piece, dtype=jnp.int32)
    positions = (query_places[None, :] - segments).astype(F32)
    freqs = THETA ** (-2.0 * jnp.arange(HALF, dtype=F32) / HEAD_SIZE)
    angles = positions[:, None, :] * freqs[None, :, None]
    cos, sin = jnp.cos(angles), jnp.sin(angles)
    starts = (segments + (ctx_size - 1 - ctx) * piece)[:, None, :]
    block = min(256, piece)
    lows = starts[:, 0, ::block] // block
    fulls = (starts[:, 0, block - 1 :: block] + block - 1) // block
    attn_gain_row, mlp_gain_row = attn_gain[None, :], mlp_gain[None, :]
    key_t, value_t = key_weight_matrix.T, value_weight_matrix.T
    valid = valid_mask.astype(F32)[..., None]

    counts = butterfly_hops(jnp.sum(valid_mask).reshape(1, 1))

    normed, queries, kv_chunks = [], [], []
    normed_t, last = None, hidden_in
    for s in seqs:
        n_rows, normed_t, kv_own = kv_project(
            s, hidden_in, attn_gain_row, key_t, value_t, cos, sin, normed_t, [last]
        )
        normed.append(n_rows)
        kv_chunks.append([kv_own])
        last = n_rows
    kv_chunks[0].append(shift(kv_chunks[0][0], 1))
    for s in seqs:
        queries.append(q_project(s, normed[s], w_query, cos, sin, [last, kv_chunks[0][-1]]))
        kv_chunks[0].append(shift(held(kv_chunks[0][-1], last), 1))
        last = queries[-1]
    for s in seqs[1:]:
        own = held(kv_chunks[s][0], kv_chunks[0][-1], last)
        for step in range(1, ctx_size):
            kv_chunks[s].append(shift(own, step))

    mixed, lse, attn_parts = None, [], []
    for s in seqs:
        mixed, lse_rows, partial = attend(
            s,
            num_seqs,
            lows[s],
            fulls[s],
            starts[s],
            queries[s],
            kv_chunks[s][::-1],
            w_out,
            mixed,
            [last],
        )
        lse.append(lse_rows)
        attn_parts.append(tensor_parts(partial))
        last = lse_rows

    middle, a_rows, b_rows, mlp_parts = [], [], [], []
    normed_mlp_t, inner = None, None
    for s in seqs:
        m_rows, normed_mlp_t, inner, a, b, partial = forward_mlp(
            s,
            hidden_in,
            mlp_gain_row,
            w_gate,
            w_up,
            w_down,
            attn_parts[s],
            normed_mlp_t,
            inner,
            [last, counts[1 + s]],
        )
        middle.append(m_rows)
        a_rows.append(a)
        b_rows.append(b)
        mlp_parts.append(tensor_parts(partial))
        last = m_rows

    tokens = num_seqs * piece * lax.axis_size("ctx") * lax.axis_size("dp")
    valid_count = counts[4].reshape(()).astype(F32)
    scale = (tokens / valid_count).reshape(1)

    layer_out, dy_t, kept = None, None, [None] * 2
    losses, grad_out_rows, dn2_parts = [], [], []
    for s in seqs:
        layer_out, dy, dy_t, loss_row = output_error(
            s,
            middle[s],
            teacher,
            valid,
            mlp_parts[s],
            layer_out,
            dy_t,
            [last, counts[3 + s]],
        )
        last = dy
        if s == num_seqs - 1:
            down = Halving(0, dy_t, inner, False, [last])
            last = down.last
        *kept, partial = backward_mlp(
            s, num_seqs, dy, w_down, a_rows[s], b_rows[s], w_gate, w_up, kept, [last]
        )
        losses.append(loss_row)
        grad_out_rows.append(dy)
        dn2_parts.append(tensor_parts(partial))
        last = partial

    gate = Halving(3, normed_mlp_t, kept[0], False, [last])
    last = gate.last

    grad_middle, mlp_gains, pieces = [], [], []
    dmb_t, dqkv = None, None

    def middle_step(s, after):
        nonlocal dmb_t
        dm, dmb_t, gain_row, grad_mixed = middle_back(
            s,
            num_seqs,
            middle[s],
            grad_out_rows[s],
            mlp_gain_row,
            w_out,
            dn2_parts[s],
            dmb_t,
            after,
        )
        grad_middle.append(dm)
        mlp_gains.append(gain_row)
        return grad_mixed

    def attention_step(s, grad_mixed, after):
        nonlocal dqkv
        dqkv, *parts = attend_back(
            s,
            num_seqs,
            lows[s],
            fulls[s],
            starts[s],
            cos,
            sin,
            queries[s],
            mixed,
            grad_mixed,
            lse[s],
            kv_chunks[s][::-1],
            dqkv,
            after,
        )
        pieces.append(parts)
        return parts[0]

    def hop(s, at, came):
        total = pieces[s][at]
        if came is not None:
            total = (total.astype(F32) + came.astype(F32)).astype(BF16)
        return shift(total, -1)

    grad_mixed = middle_step(0, [last])
    last = down.near([grad_mixed])
    last = attention_step(0, grad_mixed, [last])
    came = [hop(0, 0, None), None]
    grad_mixed = middle_step(1, [last])
    came[0] = hop(0, 1, held(came[0], grad_mixed))
    up = Halving(4, normed_mlp_t, kept[1], False, [grad_mixed])
    came[0] = hop(0, 2, held(came[0], up.last))
    last = attention_step(1, grad_mixed, [up.last])
    came[1] = hop(1, 0, None)
    last = gate.near([last])
    last = down.fold([last])
    out = Halving(1, dmb_t, mixed, True, [last])
    came[1] = hop(1, 1, held(came[1], out.last))

    dn1_parts = []
    dqkv, partial = qkv_back(
        0, dqkv, cos, sin, w_query, key_t, value_t, pieces[0][-1], came[0], [out.last]
    )
    dn1_parts.append(tensor_parts(partial))
    last = gate.fold([partial])
    came[1] = hop(1, 2, held(came[1], last))
    last = down.final(scale, [last])
    dqkv, partial = qkv_back(
        1, dqkv, cos, sin, w_query, key_t, value_t, pieces[1][-1], came[1], [last]
    )
    dn1_parts.append(tensor_parts(partial))

    qkv = Halving(2, normed_t, dqkv, True, [partial])
    last = up.near([qkv.last])

    grad_input, attn_gains = None, []

    def input_step(s, after):
        nonlocal grad_input
        grad_input, gain_row = input_back(
            s, scale, hidden_in, grad_middle[s], attn_gain_row, dn1_parts[s], grad_input, after
        )
        attn_gains.append(gain_row)
        return gain_row

    last = input_step(0, [last])
    last = out.near([last])
    last = gate.final(scale, [last])
    last = up.fold([last])
    last = input_step(1, [last])
    small = jnp.concatenate([sum(attn_gains), sum(mlp_gains), sum(losses)], axis=0)
    small = jnp.concatenate([small[:2], jnp.full_like(small[2:], jnp.sum(small[2]))], axis=0)
    hops = butterfly_hops(small)
    small = hops[-1]
    last = qkv.near([last, hops[1]])
    last = out.fold([last, hops[2]])
    last = up.final(scale, [last, hops[3]])
    last = qkv.fold([last])
    last = out.final(scale, [last])
    last = qkv.final(scale, [last])

    out_sum, gate_sum, up_sum, down_sum, qkv_sum = (
        halving.result for halving in (out, gate, up, down, qkv)
    )
    width, half = w_query.shape[1], key_t.shape[0]
    size = model // (lax.axis_size("dp") * ctx_size)
    here = (lax.axis_index("dp") * ctx_size + ctx) * size
    gains = lax.dynamic_slice_in_dim(small[:2], here, size, axis=1) * scale
    return (
        layer_out,
        small[2, 0] / (valid_count * model),
        grad_input,
        qkv_sum[:, :width],
        qkv_sum[:, width : width + half],
        qkv_sum[:, width + half :],
        out_sum.T,
        gate_sum,
        up_sum,
        down_sum.T,
        gains[0],
        gains[1],
    )


def solution(mesh):
    placed = (
        P("dp", "ctx", None),
        P(None, "tensor"),
        P(None, "tensor"),
        P(None, "tensor"),
        P("tensor", None),
        P(None, "tensor"),
        P(None, "tensor"),
        P("tensor", None),
        P(),
        P(),
        P("dp", "ctx"),
        P("dp", "ctx"),
        P("dp", "ctx", None),
    )
    return jax.shard_map(
        local,
        mesh=mesh,
        in_specs=placed,
        out_specs=(
            P("dp", "ctx", None),
            P(),
            P("dp", "ctx", None),
            P(("dp", "ctx"), "tensor"),
            P(("dp", "ctx"), "tensor"),
            P(("dp", "ctx"), "tensor"),
            P("tensor", ("dp", "ctx")),
            P(("dp", "ctx"), "tensor"),
            P(("dp", "ctx"), "tensor"),
            P("tensor", ("dp", "ctx")),
            P(("dp", "ctx")),
            P(("dp", "ctx")),
        ),
        check_vma=False,
    )
```

```python
import functools
import math

import jax
import jax.numpy as jnp
import numpy as np
from jax import lax
from jax.experimental import pallas as pl
from jax.experimental.pallas import tpu as pltpu
from jax.sharding import PartitionSpec as P

HEAD_SIZE = 80
HALF = HEAD_SIZE // 2
EPS = 1e-05
THETA = 1000000.0
NEG_BIG = -1e30
LOG2E = 1.4426950408889634
BF16 = jnp.bfloat16
F32 = jnp.float32
MIB = 1024 * 1024
ROWS = 128
WEIGHTS = {'at0': 60, 'at1': 2, 'fw0': 0, 'fw1': 0, 'er0': 0, 'bw0': 0, 'er1': 0.5, 'bw1': 2, 'Gg': 100, 'mb0': 100, 'ab0': 0, 'h00': 0, 'nd': 0, 'h01': 30, 'Gu': 0, 'h02': 0, 'ab1': 15, 'fd': 1, 'Go': 0, 'h11': 15, 'qb0': 15, 'ed': 10, 'h12': 10, 'ng': 0, 'Gq': 0.5, 'nu': 10, 'fg': 60, 'in0': 100, 'no': 15, 'eg': 0, 'fu': 10, 'in1': 60, 's0': 8, 'nq': 15, 's2': 10, 'eu': 1, 's3': 10, 'eo': 10, 'eq': 1, 'c2': 0.5, 'Gk': 2}
ORDER = (
    "c0", "c1", "at0", "at1", "c2", "fw0", "c3", "fw1", "er0", "bw0", "er1", "Gd", "bw1", "Gg", "mb0", "ab0", "h00", "nd", "mb1", "h01", "h02", "ab1", "h10", "ng", "h11", "Gu", "fd", "Go", "Gq", "h12", "qb0", "fg", "ed", "qb1", "Gk", "nu", "in0", "nq", "no", "fu", "in1", "s0", "eg", "nk", "s1", "fo", "s2", "eu", "s3", "fq", "fk", "eo", "eq", "ek",
)
PRESENT = [5]


def nn(left, right):
    return lax.dot_general(left, right, (((1,), (0,)), ((), ())), preferred_element_type=F32)


def nt(left, right):
    return lax.dot_general(left, right, (((1,), (1,)), ((), ())), preferred_element_type=F32)


def run(body, name, grid, ins, outs, scratch=(), prefetch=(), into=None, after=(), meets=None):
    num_ins = len(prefetch) + len(ins)
    kept = [(out, array) for out, array in (into or {}).items() if array is not None]
    aliases = {num_ins + at: out for at, (out, _) in enumerate(kept)}
    hidden = [array for _, array in kept] + list(after)

    def inner(*refs):
        body(*refs[:num_ins], *refs[num_ins + len(hidden) :])

    return pl.pallas_call(
        inner,
        grid_spec=pltpu.PrefetchScalarGridSpec(
            num_scalar_prefetch=len(prefetch),
            grid=grid,
            in_specs=[spec for _, spec in ins] + [pl.BlockSpec(memory_space=pl.ANY)] * len(hidden),
            out_specs=[spec for _, _, spec in outs],
            scratch_shapes=list(scratch),
        ),
        out_shape=[jax.ShapeDtypeStruct(shape, dtype) for shape, dtype, _ in outs],
        input_output_aliases=aliases,
        compiler_params=pltpu.CompilerParams(
            vmem_limit_bytes=61 * MIB, collective_id=meets, has_side_effects=meets is not None
        ),
        cost_estimate=pl.CostEstimate(
            flops=1000 + int(1e9 * PRESENT[0]),
            bytes_accessed=1000,
            transcendentals=0,
        ),
        name=name,
    )(*prefetch, *[array for array, _ in ins], *hidden)


def phase(first, count):
    return lambda i: jnp.clip(i - first, 0, count - 1)


def in_phase(step, first, count):
    return pl.when((step >= first) & (step < first + count))


def divisor(total, *sizes):
    return next(size for size in sizes + (total,) if total % size == 0)


def whole(array, *prefetch):
    zeros = (0,) * array.ndim
    return pl.BlockSpec(array.shape, lambda *_: zeros)


def rms_scale(rows):
    return lax.rsqrt(jnp.mean(rows * rows, axis=-1, keepdims=True) + EPS)


def norm_back(rows, gain, grad_normed):
    scale = rms_scale(rows)
    unit_rows = rows * scale
    weighted = grad_normed * gain
    grad_rows = scale * (
        weighted - unit_rows * jnp.mean(weighted * unit_rows, axis=-1, keepdims=True)
    )
    return grad_rows, jnp.sum(grad_normed * unit_rows, axis=0, keepdims=True)


def rotated(head, cos, sin):
    first, second = head[:HALF], head[HALF:]
    return jnp.concatenate([first * cos - second * sin, second * cos + first * sin], axis=0)


def rotated_back(head, cos, sin):
    first, second = head[:HALF], head[HALF:]
    return jnp.concatenate([first * cos + second * sin, second * cos - first * sin], axis=0)


def total_of(parts):
    total = parts[0][...].astype(F32)
    for part in parts[1:]:
        total = total + part[...].astype(F32)
    return total


def accumulate(ref, value, first):
    @pl.when(first)
    def _():
        ref[...] = value

    @pl.when(jnp.logical_not(first))
    def _():
        ref[...] = ref[...] + value


def kv_body(h_ref, gain_ref, wk_ref, wv_ref, cos_ref, sin_ref, n_ref, nt_ref, kv_ref):
    h = h_ref[...].astype(F32)
    normed = (h * rms_scale(h) * gain_ref[...]).astype(BF16)
    n_ref[...] = normed
    nt_ref[...] = normed.T
    cos, sin = cos_ref[...], sin_ref[...]
    keys = nt(wk_ref[...], normed)
    for at in range(0, wk_ref.shape[0], HEAD_SIZE):
        kv_ref[0, at : at + HEAD_SIZE, :] = rotated(keys[at : at + HEAD_SIZE], cos, sin).astype(
            BF16
        )
    kv_ref[1] = nt(wv_ref[...], normed).astype(BF16)


def kv_project(seq, hidden, gain, key_t, value_t, cos, sin, n_cols, after):
    num_seqs, rows, model = hidden.shape
    width = key_t.shape[0]
    tile = min(256, rows)
    steps = rows // tile
    table = pl.BlockSpec((None, HALF, tile), lambda i: (seq, 0, i))
    return run(
        kv_body,
        "kv_project",
        (steps,),
        [
            (hidden, pl.BlockSpec((None, tile, model), lambda i: (seq, i, 0))),
            (gain, whole(gain)),
            (key_t, whole(key_t)),
            (value_t, whole(value_t)),
            (cos, table),
            (sin, table),
        ],
        [
            ((rows, model), BF16, pl.BlockSpec((tile, model), lambda i: (i, 0))),
            (
                (model, num_seqs * rows),
                BF16,
                pl.BlockSpec((model, tile), lambda i: (0, seq * steps + i)),
            ),
            ((2, width, rows), BF16, pl.BlockSpec((2, width, tile), lambda i: (0, 0, i))),
        ],
        into={1: n_cols},
        after=after,
    )


def q_body(n_ref, w_ref, cos_ref, sin_ref, q_ref):
    factor = LOG2E / math.sqrt(HEAD_SIZE)
    cos, sin = cos_ref[...] * factor, sin_ref[...] * factor
    queries = nn(n_ref[...], w_ref[...]).T
    for at in range(0, w_ref.shape[1], HEAD_SIZE):
        q_ref[at : at + HEAD_SIZE, :] = rotated(queries[at : at + HEAD_SIZE], cos, sin).astype(BF16)


def q_project(seq, normed, w_query, cos, sin, after):
    rows, model = normed.shape
    width = w_query.shape[1]
    tile = divisor(width, 640)
    table = pl.BlockSpec((None, HALF, rows), lambda j: (seq, 0, 0))
    return run(
        q_body,
        "q_project",
        (width // tile,),
        [
            (normed, whole(normed)),
            (w_query, pl.BlockSpec((model, tile), lambda j: (0, j))),
            (cos, table),
            (sin, table),
        ],
        [((width, rows), BF16, pl.BlockSpec((tile, rows), lambda j: (j, 0)))],
        after=after,
    )[0]


def side_by_side(ref, group, here):
    return jnp.concatenate(
        [ref[r * HEAD_SIZE : (r + 1) * HEAD_SIZE, here] for r in range(group)], axis=1
    )


def allowed_block(key_at, query_at, start_row, block, group):
    shape = (block, block * group)
    key_place = key_at + lax.broadcasted_iota(jnp.int32, shape, 0)
    query_place = query_at + lax.broadcasted_iota(jnp.int32, (1, block * group), 1) % block
    return (key_place >= start_row) & (key_place <= query_place)


def key_loops(low, full, diagonal, step, carry):
    carry = lax.fori_loop(low, jnp.minimum(full, diagonal), functools.partial(step, True), carry)
    carry = lax.fori_loop(
        jnp.maximum(full, low), diagonal, functools.partial(step, False), carry
    )
    return step(True, diagonal, carry)


def attend_body(block, low_ref, full_ref, start_ref, q_ref, *refs):
    *kv_refs, o_ref, all_ref, lse_ref, keys, values, mixed = refs
    chunks = len(kv_refs)
    piece = q_ref.shape[1]
    group = q_ref.shape[0] // HEAD_SIZE
    own = (chunks - 1) * piece
    for chunk, kv_ref in enumerate(kv_refs):
        at = slice(chunk * piece, (chunk + 1) * piece)
        keys[at, :] = kv_ref[0].T
        values[:HEAD_SIZE, at] = kv_ref[1]
    values[HEAD_SIZE:, :] = jnp.ones((values.shape[0] - HEAD_SIZE, values.shape[1]), BF16)
    for at in range(0, piece, block):
        here = slice(at, at + block)
        start_row = jnp.concatenate([start_ref[:, here]] * group, axis=1)
        queries = side_by_side(q_ref, group, here)
        mixed[...] = jnp.zeros(mixed.shape, F32)

        def step(masked, key_block, top):
            key_at = pl.multiple_of(key_block * block, block)
            scores = nn(keys[pl.ds(key_at, block), :], queries)
            if masked:
                allowed = allowed_block(key_at, own + at, start_row, block, group)
                scores = jnp.where(allowed, scores, NEG_BIG)
            new = jnp.maximum(top, jnp.max(scores, axis=0, keepdims=True))
            weights = jnp.exp2(scores - new).astype(BF16)
            mixed[...] = mixed[...] * jnp.exp2(top - new) + nn(
                values[:, pl.ds(key_at, block)], weights
            )
            return new

        top = key_loops(
            low_ref[at // block],
            full_ref[at // block],
            (own + at) // block,
            step,
            jnp.full((1, block * group), NEG_BIG, F32),
        )
        total = mixed[HEAD_SIZE : HEAD_SIZE + 1, :]
        result = (mixed[:HEAD_SIZE, :] / total).astype(BF16)
        lse = top + jnp.log2(total)
        for r in range(group):
            head, part = slice(r * HEAD_SIZE, (r + 1) * HEAD_SIZE), slice(r * block, (r + 1) * block)
            o_ref[head, here] = result[:, part]
            all_ref[head, here] = result[:, part]
            lse_ref[r : r + 1, here] = lse[:, part]


def attend(seq, num_seqs, low, full, start, queries, kv_chunks, mixed, after):
    width, piece = queries.shape
    kv_heads = kv_chunks[0].shape[1] // HEAD_SIZE
    rows = width // kv_heads
    group = rows // HEAD_SIZE
    block = min(256, piece)
    chunks = len(kv_chunks)
    per_head = pl.BlockSpec((rows, piece), lambda h, *_: (h, 0))
    kv_spec = pl.BlockSpec((2, HEAD_SIZE, piece), lambda h, *_: (0, h, 0))
    return run(
        functools.partial(attend_body, block),
        "attend",
        (kv_heads,),
        [(start, whole(start)), (queries, per_head)] + [(kv, kv_spec) for kv in kv_chunks],
        [
            ((width, piece), BF16, per_head),
            (
                (width, num_seqs * piece),
                BF16,
                pl.BlockSpec((rows, piece), lambda h, *_: (h, seq)),
            ),
            (
                (kv_heads, group, piece),
                F32,
                pl.BlockSpec((None, group, piece), lambda h, *_: (h, 0, 0)),
            ),
        ],
        scratch=[
            pltpu.VMEM((chunks * piece, HEAD_SIZE), BF16),
            pltpu.VMEM((HEAD_SIZE + 16, chunks * piece), BF16),
            pltpu.VMEM((HEAD_SIZE + 16, group * block), F32),
        ],
        prefetch=[low, full],
        into={1: mixed},
        after=after,
    )


def attend_back_body(
    block, low_ref, full_ref, start_ref, cos_ref, sin_ref, q_ref, o_ref, do_ref, lse_ref, *refs
):
    *refs, keys, keys_t, values, dq_sum, dk_sum, dv_sum = refs
    chunks = (len(refs) - 1) // 2
    kv_refs, dq_ref, dkv_refs = refs[:chunks], refs[chunks], refs[chunks + 1 :]
    piece = q_ref.shape[1]
    group = q_ref.shape[0] // HEAD_SIZE
    own = (chunks - 1) * piece
    scale = 1.0 / math.sqrt(HEAD_SIZE)
    dk_sum[...] = jnp.zeros(dk_sum.shape, F32)
    dv_sum[...] = jnp.zeros(dv_sum.shape, F32)
    for chunk, kv_ref in enumerate(kv_refs):
        at = slice(chunk * piece, (chunk + 1) * piece)
        keys_t[:, at] = kv_ref[0]
        keys[at, :] = kv_ref[0].T
        values[at, :] = kv_ref[1].T
    for at in range(0, piece, block):
        here = slice(at, at + block)
        start_row = jnp.concatenate([start_ref[:, here]] * group, axis=1)
        queries = side_by_side(q_ref, group, here)
        grads = side_by_side(do_ref, group, here)
        outs = side_by_side(o_ref, group, here)
        delta = jnp.sum(outs.astype(F32) * grads.astype(F32), axis=0, keepdims=True)
        lse = jnp.concatenate([lse_ref[r : r + 1, here] for r in range(group)], axis=1)
        dq_sum[...] = jnp.zeros(dq_sum.shape, F32)

        def step(masked, key_block, carry):
            key_at = pl.multiple_of(key_block * block, block)
            inside = pl.ds(key_at, block)
            scores = nn(keys[inside, :], queries)
            if masked:
                allowed = allowed_block(key_at, own + at, start_row, block, group)
                scores = jnp.where(allowed, scores, NEG_BIG)
            probs = jnp.exp2(scores - lse)
            dv_sum[:, inside] = dv_sum[:, inside] + nt(grads, probs.astype(BF16))
            grad = (probs * (nn(values[inside, :], grads) - delta)).astype(BF16)
            dk_sum[:, inside] = dk_sum[:, inside] + nt(queries, grad)
            dq_sum[...] = dq_sum[...] + nn(keys_t[:, inside], grad)
            return carry

        key_loops(low_ref[at // block], full_ref[at // block], (own + at) // block, step, 0)
        cos, sin = cos_ref[:, here], sin_ref[:, here]
        for r in range(group):
            rounded = (dq_sum[:, r * block : (r + 1) * block] * scale).astype(BF16).astype(F32)
            dq_ref[r * HEAD_SIZE : (r + 1) * HEAD_SIZE, here] = rotated_back(
                rounded, cos, sin
            ).astype(BF16)
    for chunk, dkv_ref in enumerate(dkv_refs):
        at = slice(chunk * piece, (chunk + 1) * piece)
        dkv_ref[0] = (dk_sum[:, at] * (1.0 / LOG2E)).astype(BF16)
        dkv_ref[1] = dv_sum[:, at].astype(BF16)


def attend_back(
    seq, num_seqs, low, full, start, cos, sin, queries, mixed, grad_mixed, lse, kv_chunks, dq, after
):
    width, piece = queries.shape
    kv_heads = kv_chunks[0].shape[1] // HEAD_SIZE
    rows = width // kv_heads
    group = rows // HEAD_SIZE
    block = min(256, piece)
    keys = len(kv_chunks) * piece
    per_head = pl.BlockSpec((rows, piece), lambda h, *_: (h, 0))
    per_head_seq = pl.BlockSpec((rows, piece), lambda h, *_: (h, seq))
    table = pl.BlockSpec((None, HALF, piece), lambda h, *_: (seq, 0, 0))
    kv_spec = pl.BlockSpec((2, HEAD_SIZE, piece), lambda h, *_: (0, h, 0))
    return run(
        functools.partial(attend_back_body, block),
        "attend_back",
        (kv_heads,),
        [
            (start, whole(start)),
            (cos, table),
            (sin, table),
            (queries, per_head),
            (mixed, per_head_seq),
            (grad_mixed, per_head),
            (lse, pl.BlockSpec((None, group, piece), lambda h, *_: (h, 0, 0))),
        ]
        + [(kv, kv_spec) for kv in kv_chunks],
        [
            ((width, num_seqs * piece), BF16, per_head_seq),
        ]
        + [(kv.shape, BF16, kv_spec) for kv in kv_chunks],
        scratch=[
            pltpu.VMEM((keys, HEAD_SIZE), BF16),
            pltpu.VMEM((HEAD_SIZE, keys), BF16),
            pltpu.VMEM((keys, HEAD_SIZE), BF16),
            pltpu.VMEM((HEAD_SIZE, group * block), F32),
            pltpu.VMEM((HEAD_SIZE, keys), F32),
            pltpu.VMEM((HEAD_SIZE, keys), F32),
        ],
        prefetch=[low, full],
        into={0: dq},
        after=after,
    )


def qkv_back_body(
    dq_ref, cos_ref, sin_ref, wq_ref, wk_ref, wv_ref, own_ref, came_ref, *refs
):
    dkv_ref, out_ref, dq_rows, dk_rows, dv_rows = refs
    width = wk_ref.shape[0]

    @pl.when(pl.program_id(0) == 0)
    def _():
        cos, sin = cos_ref[...], sin_ref[...]
        for at in range(0, width, HEAD_SIZE):
            head = slice(at, at + HEAD_SIZE)
            rows = own_ref[0, head].astype(F32) + came_ref[0, head].astype(F32)
            rows = rows.astype(BF16).astype(F32)
            dkv_ref[at : at + HEAD_SIZE, :] = rotated_back(rows, cos, sin).astype(BF16)
        dkv_ref[width:, :] = (own_ref[1].astype(F32) + came_ref[1].astype(F32)).astype(BF16)
        dq_rows[...] = dq_ref[...].T
        dk_rows[...] = dkv_ref[:width].T
        dv_rows[...] = dkv_ref[width:].T

    out_ref[...] = (
        nt(dq_rows[...], wq_ref[...])
        + nn(dk_rows[...], wk_ref[...])
        + nn(dv_rows[...], wv_ref[...])
    ).astype(BF16)


def qkv_back(seq, dq, cos, sin, w_query, key_t, value_t, own, came, dkv, after):
    model, width_q = w_query.shape
    width = key_t.shape[0]
    piece = own.shape[-1]
    tile = 1280
    table = pl.BlockSpec((None, HALF, piece), lambda j: (seq, 0, 0))
    narrow = pl.BlockSpec((width, tile), lambda j: (0, j))
    return run(
        qkv_back_body,
        "qkv_back",
        (model // tile,),
        [
            (dq, pl.BlockSpec((width_q, piece), lambda j: (0, seq))),
            (cos, table),
            (sin, table),
            (w_query, pl.BlockSpec((tile, width_q), lambda j: (j, 0))),
            (key_t, narrow),
            (value_t, narrow),
            (own, whole(own)),
            (came, whole(came)),
        ],
        [
            (
                (2 * width, dq.shape[1]),
                BF16,
                pl.BlockSpec((2 * width, piece), lambda j: (0, seq)),
            ),
            ((piece, model), BF16, pl.BlockSpec((piece, tile), lambda j: (0, j))),
        ],
        scratch=[
            pltpu.VMEM((piece, width_q), BF16),
            pltpu.VMEM((piece, width), BF16),
            pltpu.VMEM((piece, width), BF16),
        ],
        into={0: dkv},
        after=after,
    )


def forward_body(counts, heads, h_ref, gain_ref, wg_ref, wu_ref, wd_ref, *refs):
    o_refs, wo_refs, refs = refs[:heads], refs[heads : 2 * heads], refs[2 * heads :]
    m_ref, nt_ref, z_ref, a_ref, b_ref, part_ref, o_rows, attn, normed, inner = refs
    attn_steps, norm_steps, wide_steps, out_steps = counts
    step = pl.program_id(0)

    @pl.when(step == 0)
    def _():
        for at, o_ref in enumerate(o_refs):
            o_rows[at] = o_ref[...].T

    @in_phase(step, 0, attn_steps)
    def _():
        total = nn(o_rows[0], wo_refs[0][...])
        for at in range(1, heads):
            total = total + nn(o_rows[at], wo_refs[at][...])
        attn[step] = total

    @in_phase(step, attn_steps, norm_steps)
    def _():
        at = pl.ds(pl.multiple_of((step - attn_steps) * ROWS, ROWS), ROWS)
        added = jnp.concatenate([attn[part, at, :] for part in range(attn_steps)], axis=1)
        middle = h_ref[...].astype(F32) + added
        m_ref[...] = middle.astype(BF16)
        rows = (middle * rms_scale(middle) * gain_ref[...]).astype(BF16)
        normed[at, :] = rows
        nt_ref[...] = rows.T

    first = attn_steps + norm_steps

    @in_phase(step, first, wide_steps)
    def _():
        gate = nn(normed[...], wg_ref[...])
        up = nn(normed[...], wu_ref[...])
        sig = jax.nn.sigmoid(gate)
        silu = gate * sig
        z = (silu * up).astype(BF16)
        z_ref[...] = z
        inner[step - first] = z
        a_ref[...] = (up * sig * (1.0 + gate * (1.0 - sig))).astype(BF16)
        b_ref[...] = silu.astype(BF16)

    @in_phase(step, first + wide_steps, out_steps)
    def _():
        width = inner.shape[2]
        total = nn(inner[0], wd_ref[:width])
        for at in range(1, wide_steps):
            total = total + nn(inner[at], wd_ref[at * width : (at + 1) * width])
        part_ref[...] = total.astype(BF16)


def forward_mlp(seq, hidden, gain, w_gate, w_up, w_down, mixed, w_outs, normed_t, inner, after):
    num_seqs, rows, model = hidden.shape
    hidden_width = w_gate.shape[1]
    width = mixed[0].shape[0]
    wide, narrow = divisor(hidden_width, 512), 640
    counts = (model // narrow, rows // ROWS, hidden_width // wide, model // narrow)
    attn, norm, mid, out = (phase(sum(counts[:at]), count) for at, count in enumerate(counts))
    row_spec = pl.BlockSpec((ROWS, model), lambda i: (norm(i), 0))
    weight_spec = pl.BlockSpec((model, wide), lambda i: (0, mid(i)))
    wide_spec = pl.BlockSpec((rows, wide), lambda i: (0, mid(i)))
    return run(
        functools.partial(forward_body, counts, len(mixed)),
        "forward_mlp",
        (sum(counts),),
        [
            (hidden, pl.BlockSpec((None, ROWS, model), lambda i: (seq, norm(i), 0))),
            (gain, whole(gain)),
            (w_gate, weight_spec),
            (w_up, weight_spec),
            (w_down, pl.BlockSpec((hidden_width, narrow), lambda i: (0, out(i)))),
        ]
        + [(part, whole(part)) for part in mixed]
        + [(part, pl.BlockSpec((width, narrow), lambda i: (0, attn(i)))) for part in w_outs],
        [
            ((rows, model), BF16, row_spec),
            (
                (model, num_seqs * rows),
                BF16,
                pl.BlockSpec((model, ROWS), lambda i: (0, seq * counts[1] + norm(i))),
            ),
            (
                (num_seqs, rows, hidden_width),
                BF16,
                pl.BlockSpec((None, rows, wide), lambda i: (seq, 0, mid(i))),
            ),
            ((rows, hidden_width), BF16, wide_spec),
            ((rows, hidden_width), BF16, wide_spec),
            ((rows, model), BF16, pl.BlockSpec((rows, narrow), lambda i: (0, out(i)))),
        ],
        scratch=[
            pltpu.VMEM((len(mixed), rows, width), BF16),
            pltpu.VMEM((counts[0], rows, narrow), F32),
            pltpu.VMEM((rows, model), BF16),
            pltpu.VMEM((counts[2], rows, wide), BF16),
        ],
        into={1: normed_t, 2: inner},
        after=after,
    )


def error_body(m_ref, teacher_ref, valid_ref, *refs):
    *parts, out_ref, dy_ref, dyt_ref, loss_ref = refs
    output = m_ref[...].astype(F32) + total_of(parts)
    out_ref[...] = output.astype(BF16)
    errors = output - teacher_ref[...].astype(F32)
    valid = valid_ref[...]
    rounded = (valid * errors).astype(BF16)
    dy_ref[...] = rounded
    dyt_ref[...] = rounded.T
    squares = jnp.sum(valid * errors * errors, axis=0, keepdims=True)
    accumulate(loss_ref, squares, pl.program_id(0) == 0)


def output_error(seq, middle, teacher, valid, parts, layer_out, grad_t, after):
    num_seqs, rows, model = teacher.shape
    steps = rows // ROWS
    row_spec = pl.BlockSpec((ROWS, model), lambda i: (i, 0))
    seq_spec = pl.BlockSpec((None, ROWS, model), lambda i: (seq, i, 0))
    return run(
        error_body,
        "output_error",
        (steps,),
        [
            (middle, row_spec),
            (teacher, seq_spec),
            (valid, pl.BlockSpec((None, ROWS, 1), lambda i: (seq, i, 0))),
        ]
        + [(part, row_spec) for part in parts],
        [
            ((num_seqs, rows, model), BF16, seq_spec),
            ((rows, model), BF16, row_spec),
            (
                (model, num_seqs * rows),
                BF16,
                pl.BlockSpec((model, ROWS), lambda i: (0, seq * steps + i)),
            ),
            ((1, model), F32, pl.BlockSpec((1, model), lambda i: (0, 0))),
        ],
        into={0: layer_out, 2: grad_t},
        after=after,
    )


def backward_body(counts, dy_ref, wd_ref, a_ref, b_ref, wg_ref, wu_ref, *refs):
    dg_ref, du_ref, part_ref, gates, ups = refs
    wide_steps, out_steps = counts
    step = pl.program_id(0)

    @in_phase(step, 0, wide_steps)
    def _():
        grad_inner = nt(dy_ref[...], wd_ref[...])
        d_gate = (grad_inner * a_ref[...].astype(F32)).astype(BF16)
        d_up = (grad_inner * b_ref[...].astype(F32)).astype(BF16)
        dg_ref[...] = d_gate
        du_ref[...] = d_up
        gates[step] = d_gate
        ups[step] = d_up

    @in_phase(step, wide_steps, out_steps)
    def _():
        width = gates.shape[2]
        total = None
        for at in range(wide_steps):
            columns = slice(at * width, (at + 1) * width)
            term = nt(gates[at], wg_ref[:, columns]) + nt(ups[at], wu_ref[:, columns])
            total = term if total is None else total + term
        part_ref[...] = total.astype(BF16)


def backward_mlp(seq, num_seqs, grad_out, w_down, a, b, w_gate, w_up, kept, after):
    rows, model = grad_out.shape
    hidden_width = w_gate.shape[1]
    wide, narrow = divisor(hidden_width, 512), 512
    counts = (hidden_width // wide, model // narrow)
    mid, out = phase(0, counts[0]), phase(counts[0], counts[1])
    wide_spec = pl.BlockSpec((rows, wide), lambda i: (0, mid(i)))
    wide_seq = pl.BlockSpec((None, rows, wide), lambda i: (seq, 0, mid(i)))
    weight_spec = pl.BlockSpec((narrow, hidden_width), lambda i: (out(i), 0))
    return run(
        functools.partial(backward_body, counts),
        "backward_mlp",
        (sum(counts),),
        [
            (grad_out, whole(grad_out)),
            (w_down, pl.BlockSpec((wide, model), lambda i: (mid(i), 0))),
            (a, wide_spec),
            (b, wide_spec),
            (w_gate, weight_spec),
            (w_up, weight_spec),
        ],
        [
            ((num_seqs, rows, hidden_width), BF16, wide_seq),
            ((num_seqs, rows, hidden_width), BF16, wide_seq),
            ((rows, model), BF16, pl.BlockSpec((rows, narrow), lambda i: (0, out(i)))),
        ],
        scratch=[
            pltpu.VMEM((counts[0], rows, wide), BF16),
            pltpu.VMEM((counts[0], rows, wide), BF16),
        ],
        into=dict(zip((0, 1), kept)),
        after=after,
    )


def middle_back_body(counts, m_ref, dy_ref, gain_ref, w_ref, *refs):
    *parts, dm_ref, dmt_ref, dg_ref, do_ref, grad_t = refs
    norm_steps, out_steps = counts
    step = pl.program_id(0)

    @in_phase(step, 0, norm_steps)
    def _():
        grad_rows, grad_gain = norm_back(
            m_ref[...].astype(F32), gain_ref[...], total_of(parts)
        )
        rounded = (dy_ref[...].astype(F32) + grad_rows).astype(BF16)
        dm_ref[...] = rounded
        rounded_t = rounded.T
        dmt_ref[...] = rounded_t
        grad_t[step] = rounded_t
        accumulate(dg_ref, grad_gain, step == 0)

    @in_phase(step, norm_steps, out_steps)
    def _():
        columns = jnp.concatenate([grad_t[at] for at in range(norm_steps)], axis=1)
        do_ref[...] = nn(w_ref[...], columns).astype(BF16)


def middle_back(seq, num_seqs, middle, grad_output, gain, w_out, parts, grad_t, after):
    rows, model = middle.shape
    width = w_out.shape[0]
    tile = divisor(width, 640)
    counts = (rows // ROWS, width // tile)
    norm, out = phase(0, counts[0]), phase(counts[0], counts[1])
    row_spec = pl.BlockSpec((ROWS, model), lambda i: (norm(i), 0))
    return run(
        functools.partial(middle_back_body, counts),
        "middle_back",
        (sum(counts),),
        [
            (middle, row_spec),
            (grad_output, row_spec),
            (gain, whole(gain)),
            (w_out, pl.BlockSpec((tile, model), lambda i: (out(i), 0))),
        ]
        + [(part, row_spec) for part in parts],
        [
            ((rows, model), BF16, row_spec),
            (
                (model, num_seqs * rows),
                BF16,
                pl.BlockSpec((model, ROWS), lambda i: (0, seq * counts[0] + norm(i))),
            ),
            ((1, model), F32, pl.BlockSpec((1, model), lambda i: (0, 0))),
            ((width, rows), BF16, pl.BlockSpec((tile, rows), lambda i: (out(i), 0))),
        ],
        scratch=[pltpu.VMEM((counts[0], model, ROWS), BF16)],
        into={1: grad_t},
        after=after,
    )


def input_back_body(scale_ref, h_ref, dm_ref, gain_ref, *refs):
    *parts, grad_ref, dg_ref = refs
    grad_rows, grad_gain = norm_back(h_ref[...].astype(F32), gain_ref[...], total_of(parts))
    grad_ref[...] = scale_ref[0] * (dm_ref[...].astype(F32) + grad_rows)
    accumulate(dg_ref, grad_gain, pl.program_id(0) == 0)


def input_back(seq, scale, hidden, grad_middle, gain, parts, earlier, after):
    num_seqs, rows, model = hidden.shape
    row_spec = pl.BlockSpec((ROWS, model), lambda i: (i, 0))
    seq_spec = pl.BlockSpec((None, ROWS, model), lambda i: (seq, i, 0))
    return run(
        input_back_body,
        "input_back",
        (rows // ROWS,),
        [
            (scale, pl.BlockSpec(memory_space=pltpu.SMEM)),
            (hidden, seq_spec),
            (grad_middle, row_spec),
            (gain, whole(gain)),
        ]
        + [(part, row_spec) for part in parts],
        [
            ((num_seqs, rows, model), F32, seq_spec),
            ((1, model), F32, pl.BlockSpec((1, model), lambda i: (0, 0))),
        ],
        into={0: earlier},
        after=after,
    )


def weight_body(flipped, x_ref, y_ref, y_before_ref, far_ref, sent_ref, kept_ref, *refs):
    x_all, staged, landed, send_sem, recv_sem = refs
    tiles = landed.shape[0]
    step = pl.program_id(0)
    dp, ctx = lax.axis_index("dp"), lax.axis_index("ctx")
    ctx_size = lax.axis_size("ctx")
    core, chip = dp % 2, dp // 2
    partner = dp + 1 - 2 * core
    half = x_all.shape[0] // 2

    def sending(at):
        return pltpu.make_async_remote_copy(
            src_ref=staged.at[at % 2],
            dst_ref=landed.at[at],
            send_sem=send_sem.at[at % 2],
            recv_sem=recv_sem.at[at],
            device_id={"dp": partner},
            device_id_type=pl.DeviceIdType.MESH,
        )

    @pl.when(step == 0)
    def _():
        barrier = pltpu.get_barrier_semaphore()
        pl.semaphore_signal(
            barrier, inc=1, device_id={"dp": partner}, device_id_type=pl.DeviceIdType.MESH
        )
        pl.semaphore_wait(barrier, 1)
        size = x_ref.shape[0] // (lax.axis_size("dp") * ctx_size)
        low, high = ctx % 2, ctx // 2
        at = 0
        for other_core in (1, 0):
            to_core = core + other_core * (1 - 2 * core)
            for other_chip in (1, 0):
                to_dp = 2 * (chip + other_chip * (1 - 2 * chip)) + to_core
                for other_low in (1, 0):
                    for other_high in (1, 0):
                        to_ctx = 2 * (high + other_high * (1 - 2 * high))
                        to_ctx = to_ctx + low + other_low * (1 - 2 * low)
                        row = pl.multiple_of((to_dp * ctx_size + to_ctx) * size, size)
                        x_all[at : at + size, :] = x_ref[pl.ds(row, size), :]
                        at += size

    def product(rows, ref):
        y = ref[...]
        return nt(rows, y) if flipped else nn(rows, y.reshape(-1, y.shape[-1]))

    @pl.when((step >= 2) & (step < tiles))
    def _():
        sending(step - 2).wait_send()

    @pl.when(step < tiles)
    def _():
        staged[step % 2] = product(x_all[:half, :], y_ref).astype(BF16)
        sending(step).start()

    @pl.when(step > 0)
    def _():
        total = product(x_all[half:, :], y_before_ref)
        sending(step - 1).wait_recv()
        total = (total + landed[step - 1].astype(F32)).astype(BF16)
        far_ref[...] = total[: half // 2]
        sent_ref[...] = total[half // 2 : half // 4 * 3]
        kept_ref[...] = total[half // 4 * 3 :]

    @pl.when(step == tiles)
    def _():
        for at in range(max(tiles - 2, 0), tiles):
            sending(at).wait_send()


def weight_grad(meets, x_t, y, flipped, after):
    model, tokens = x_t.shape
    if flipped:
        tile = divisor(y.shape[0], 640)
        tiles = y.shape[0] // tile
        y_block, place = (tile, tokens), lambda at: (at, 0)
    else:
        tile = divisor(y.shape[2], 512)
        tiles = y.shape[2] // tile
        y_block, place = y.shape[:2] + (tile,), lambda at: (0, 0, at)
    width = tile * tiles
    before = lambda i: jnp.maximum(i - 1, 0)
    outs = [
        ((rows, width), BF16, pl.BlockSpec((rows, tile), lambda i: (0, before(i))))
        for rows in (model // 4, model // 8, model // 8)
    ]
    return run(
        functools.partial(weight_body, flipped),
        "weight_grad",
        (tiles + 1,),
        [
            (x_t, whole(x_t)),
            (y, pl.BlockSpec(y_block, lambda i: place(jnp.minimum(i, tiles - 1)))),
            (y, pl.BlockSpec(y_block, lambda i: place(before(i)))),
        ],
        outs,
        scratch=[
            pltpu.VMEM((model, tokens), BF16),
            pltpu.VMEM((2, model // 2, tile), BF16),
            pltpu.VMEM((tiles, model // 2, tile), BF16),
            pltpu.SemaphoreType.DMA((2,)),
            pltpu.SemaphoreType.DMA((tiles,)),
        ],
        after=after,
        meets=meets,
    )


def add_body(*refs):
    refs[-1][...] = total_of(refs[:-1]).astype(BF16)


def final_body(scale_ref, *refs):
    count = 4
    total = total_of(refs[:count]) * scale_ref[0]
    at = 0
    for out_ref in refs[count:]:
        out_ref[...] = total[:, at : at + out_ref.shape[1]]
        at += out_ref.shape[1]


def swap(value, axis, bit):
    size = lax.axis_size(axis)
    return lax.ppermute(value, axis, [(i, i ^ bit) for i in range(size)])


class Halving:
    def __init__(self, meets, x_t, y, flipped, after):
        far, self.sent, self.kept = weight_grad(meets, x_t, y, flipped, after)
        self.came = swap(far, "dp", 2)
        self.last = far

    def added(self, name, rows, parts, after):
        width = self.sent.shape[1]
        tile = divisor(width, 1792, 640)
        ins = [
            (
                array,
                pl.BlockSpec((rows, tile), functools.partial(lambda at, j: (at, j), first // rows)),
            )
            for array, first in parts
        ]
        spec = pl.BlockSpec((rows, tile), lambda j: (0, j))
        return run(
            add_body, name, (width // tile,), ins, [((rows, width), BF16, spec)], after=after
        )[0]

    def near(self, after):
        rows = self.sent.shape[0]
        send = self.added("near", rows, [(self.sent, 0), (self.came, 0)], after)
        self.pair = swap(send, "ctx", 1)
        return send

    def fold(self, after):
        rows = self.sent.shape[0] // 2
        parts = [(self.kept, 0), (self.came, 2 * rows), (self.pair, 0)]
        send = self.added("fold", rows, parts, after)
        self.end = swap(send, "ctx", 2)
        return send

    def final(self, scale, widths, after):
        rows, width = self.end.shape
        tile = width if len(widths) > 1 else divisor(width, 896, 640)
        tiles = [(tile,), widths][len(widths) > 1]
        parts = [(self.kept, 1), (self.came, 3), (self.pair, 1), (self.end, 0)]
        self.result = run(
            final_body,
            "final",
            (width // tile,),
            [(scale, pl.BlockSpec(memory_space=pltpu.SMEM))]
            + [
                (part, pl.BlockSpec((rows, tile), functools.partial(lambda at, j: (at, j), at)))
                for part, at in parts
            ],
            [
                ((rows, each), F32, pl.BlockSpec((rows, cut), lambda j: (0, j)))
                for each, cut in zip(widths, tiles)
            ],
            after=after,
        )
        return self.result[0]


def tensor_parts(partial):
    if lax.axis_size("tensor") == 2:
        return [partial, swap(partial, "tensor", 1)]
    return [lax.psum(partial, "tensor")]


def tensor_copies(value):
    if lax.axis_size("tensor") == 2:
        return [value, swap(value, "tensor", 1)]
    return list(lax.all_gather(value, "tensor"))


def tensor_weights(weight, after):
    size, count = lax.axis_size("dp"), weight.shape[0]
    if lax.axis_size("tensor") != 2 or count % (16 * size):
        return list(lax.all_gather(weight, "tensor"))
    rows = count // size
    part = lax.dynamic_slice_in_dim(weight, lax.axis_index("dp") * rows, rows)
    return [weight, lax.all_gather(held(swap(part, "tensor", 1), after), "dp", axis=0, tiled=True)]


def held(value, *others):
    return lax.optimization_barrier((value, *others))[0]


def shift(value, step):
    size = lax.axis_size("ctx")
    pairs = [(i, i + step) for i in range(size) if 0 <= i + step < size]
    return lax.ppermute(value, "ctx", pairs)


def local(
    hidden_in,
    w_query,
    key_weight_matrix,
    value_weight_matrix,
    w_out,
    w_gate,
    w_up,
    w_down,
    attn_gain,
    mlp_gain,
    segments,
    valid_mask,
    teacher,
):
    num_seqs, piece, model = hidden_in.shape
    seqs = range(num_seqs)
    ctx_size = lax.axis_size("ctx")
    ctx = lax.axis_index("ctx")
    query_places = ctx * piece + jnp.arange(piece, dtype=jnp.int32)
    positions = (query_places[None, :] - segments).astype(F32)
    freqs = THETA ** (-2.0 * jnp.arange(HALF, dtype=F32) / HEAD_SIZE)
    angles = positions[:, None, :] * freqs[None, :, None]
    cos, sin = jnp.cos(angles), jnp.sin(angles)
    starts = (segments + (ctx_size - 1 - ctx) * piece)[:, None, :]
    block = min(256, piece)
    lows = starts[:, 0, ::block] // block
    fulls = (starts[:, 0, block - 1 :: block] + block - 1) // block
    attn_gain_row, mlp_gain_row = attn_gain[None, :], mlp_gain[None, :]
    key_t, value_t = key_weight_matrix.T, value_weight_matrix.T
    valid = valid_mask.astype(F32)[..., None]


    normed, queries, kv_chunks = [], [], []
    normed_t, last = None, hidden_in
    for s in seqs:
        n_rows, normed_t, kv_own = kv_project(
            s, hidden_in, attn_gain_row, key_t, value_t, cos, sin, normed_t, [last]
        )
        normed.append(n_rows)
        kv_chunks.append([kv_own])
        last = n_rows
    kv_chunks[0].append(shift(kv_chunks[0][0], 1))
    for s in seqs:
        queries.append(q_project(s, normed[s], w_query, cos, sin, [last, kv_chunks[0][-1]]))
        kv_chunks[0].append(shift(held(kv_chunks[0][-1], last), 1))
        last = queries[-1]
    for s in seqs[1:]:
        own = held(kv_chunks[s][0], kv_chunks[0][-1], last)
        for step in range(1, ctx_size):
            kv_chunks[s].append(shift(own, step))

    made = {"count": jnp.sum(valid_mask).reshape(1, 1)}
    lse, middle, rows_a, rows_b = [], [], [], []
    losses, dys, mlp_gains, attn_gains, grad_middle = [], [], [], [], []
    heads, mlp_parts, dn2_parts, dn1_parts, pieces, came = [], [], [], [], [], [None, None]
    w_outs = tensor_weights(w_out, queries[-1])
    tokens = num_seqs * piece * ctx_size * lax.axis_size("dp")
    last_seq = num_seqs - 1

    def scale():
        return (tokens / made["count"].reshape(()).astype(F32)).reshape(1)

    def attention(s, after):
        heads_out, made["mixed"], lse_rows = attend(
            s,
            num_seqs,
            lows[s],
            fulls[s],
            starts[s],
            queries[s],
            kv_chunks[s][::-1],
            made.get("mixed"),
            after + [made["count"]],
        )
        lse.append(lse_rows)
        heads.append(tensor_copies(heads_out))
        return lse_rows

    def forward(s, after):
        m_rows, made["n2"], made["z"], a, b, partial = forward_mlp(
            s,
            hidden_in,
            mlp_gain_row,
            w_gate,
            w_up,
            w_down,
            heads[s],
            w_outs,
            made.get("n2"),
            made.get("z"),
            after,
        )
        middle.append(m_rows)
        rows_a.append(a)
        rows_b.append(b)
        mlp_parts.append(tensor_parts(partial))
        return m_rows

    def error(s, after):
        made["y"], dy, made["dy"], loss_row = output_error(
            s,
            middle[s],
            teacher,
            valid,
            mlp_parts[s],
            made.get("y"),
            made.get("dy"),
            after + [made["count"]],
        )
        dys.append(dy)
        losses.append(loss_row)
        return dy

    def backward(s, after):
        made["dgate"], made["dup"], partial = backward_mlp(
            s,
            num_seqs,
            dys[s],
            w_down,
            rows_a[s],
            rows_b[s],
            w_gate,
            w_up,
            (made.get("dgate"), made.get("dup")),
            after,
        )
        dn2_parts.append(tensor_parts(partial))
        return partial

    def middle_step(s, after):
        dm, made["dm"], gain_row, made["do", s] = middle_back(
            s,
            num_seqs,
            middle[s],
            dys[s],
            mlp_gain_row,
            w_out,
            dn2_parts[s],
            made.get("dm"),
            after,
        )
        grad_middle.append(dm)
        mlp_gains.append(gain_row)
        return dm

    def attention_back(s, after):
        made["dq"], *parts = attend_back(
            s,
            num_seqs,
            lows[s],
            fulls[s],
            starts[s],
            cos,
            sin,
            queries[s],
            made["mixed"],
            made["do", s],
            lse[s],
            kv_chunks[s][::-1],
            made.get("dq"),
            after,
        )
        pieces.append(parts)
        return parts[0]

    def hop(s, at, after):
        total = pieces[s][at]
        if came[s] is not None:
            total = (total.astype(F32) + held(came[s], *after).astype(F32)).astype(BF16)
        came[s] = shift(total, -1)
        return after[0]

    def projections(s, after):
        made["dkv"], partial = qkv_back(
            s,
            made["dq"],
            cos,
            sin,
            w_query,
            key_t,
            value_t,
            pieces[s][-1],
            came[s],
            made.get("dkv"),
            after,
        )
        dn1_parts.append(tensor_parts(partial))
        return partial

    def halving(name, meets, x_t, y, flipped, after):
        made[name] = Halving(meets, made.get(x_t, normed_t), made[y], flipped, after)
        return made[name].last

    def input_step(s, after):
        made["dx"], gain_row = input_back(
            s,
            scale(),
            hidden_in,
            grad_middle[s],
            attn_gain_row,
            dn1_parts[s],
            made.get("dx"),
            after,
        )
        attn_gains.append(gain_row)
        return gain_row

    def hop_of(name, at, after):
        axis, bit = (("dp", 1), ("dp", 2), ("ctx", 1), ("ctx", 2))[at]
        total = made[name] if name == "count" and at < 2 else held(made[name], *after)
        made[name] = total + swap(total, axis, bit)
        return after[0]

    def small_hop(at, after):
        if at == 0:
            loss = jnp.full((1, model), jnp.sum(sum(losses)))
            made["small"] = jnp.concatenate([sum(attn_gains), sum(mlp_gains), loss], axis=0)
        return hop_of("small", at, after)

    def finish(name, after):
        widths = (made[name].sent.shape[1],)
        if name == "k":
            widths = key_t.shape[:1] * 2
        return made[name].final(scale(), widths, after)

    steps = {
        "Gd": functools.partial(halving, "d", 0, "dy", "z", False),
        "Gg": functools.partial(halving, "g", 3, "n2", "dgate", False),
        "Gu": functools.partial(halving, "u", 4, "n2", "dup", False),
        "Go": functools.partial(halving, "o", 1, "dm", "mixed", True),
        "Gq": functools.partial(halving, "q", 2, "n1", "dq", True),
        "Gk": functools.partial(halving, "k", 5, "n1", "dkv", True),
    }
    for name in "dguoqk":
        for short, stage in (("n", "near"), ("f", "fold")):
            steps[short + name] = lambda after, name=name, stage=stage: getattr(
                made[name], stage
            )(after)
        steps["e" + name] = functools.partial(finish, name)
    for at in range(4):
        steps["s%d" % at] = functools.partial(small_hop, at)
        steps["c%d" % at] = functools.partial(hop_of, "count", at)
    for s in seqs:
        for short, one in (
            ("at", attention),
            ("fw", forward),
            ("er", error),
            ("bw", backward),
            ("mb", middle_step),
            ("ab", attention_back),
            ("qb", projections),
            ("in", input_step),
        ):
            steps[short + str(s)] = functools.partial(one, s)
        for at in range(ctx_size - 1):
            steps["h%d%d" % (s, at)] = functools.partial(hop, s, at)
    for name in ORDER:
        PRESENT[0] = WEIGHTS.get(name, 5)
        last = steps[name]([last])

    (out_sum,), (gate_sum,), (up_sum,), (down_sum,) = (made[name].result for name in "ogud")
    size = model // (lax.axis_size("dp") * ctx_size)
    here = (lax.axis_index("dp") * ctx_size + ctx) * size
    small = made["small"]
    gains = lax.dynamic_slice_in_dim(small[:2], here, size, axis=1) * scale()
    return (
        made["y"],
        small[2, 0] / (made["count"].reshape(()).astype(F32) * model),
        made["dx"],
        *made["q"].result,
        *made["k"].result,
        out_sum.T,
        gate_sum,
        up_sum,
        down_sum.T,
        gains[0],
        gains[1],
    )


def solution(mesh):
    placed = (
        P("dp", "ctx", None),
        P(None, "tensor"),
        P(None, "tensor"),
        P(None, "tensor"),
        P("tensor", None),
        P(None, "tensor"),
        P(None, "tensor"),
        P("tensor", None),
        P(),
        P(),
        P("dp", "ctx"),
        P("dp", "ctx"),
        P("dp", "ctx", None),
    )
    return jax.shard_map(
        local,
        mesh=mesh,
        in_specs=placed,
        out_specs=(
            P("dp", "ctx", None),
            P(),
            P("dp", "ctx", None),
            P(("dp", "ctx"), "tensor"),
            P(("dp", "ctx"), "tensor"),
            P(("dp", "ctx"), "tensor"),
            P("tensor", ("dp", "ctx")),
            P(("dp", "ctx"), "tensor"),
            P(("dp", "ctx"), "tensor"),
            P("tensor", ("dp", "ctx")),
            P(("dp", "ctx")),
            P(("dp", "ctx")),
        ),
        check_vma=False,
    )
```

```python
import functools
import math

import jax
import jax.numpy as jnp
import numpy as np
from jax import lax
from jax.experimental import pallas as pl
from jax.experimental.pallas import tpu as pltpu
from jax.sharding import PartitionSpec as P

HEAD_SIZE = 80
HALF = HEAD_SIZE // 2
EPS = 1e-05
THETA = 1000000.0
NEG_BIG = -1e30
LOG2E = 1.4426950408889634
BF16 = jnp.bfloat16
F32 = jnp.float32
MIB = 1024 * 1024
ROWS = 128
WEIGHTS = {'at1': 30, 'ab1': 100, 'eb': 30, 'Gu': 60, 'at0': 30, 's0': 0, 'fw0': 30, 'Gb': 0.5, 'Gk': 0, 'in0': 15, 'eo': 60, 'na': 0.5, 'nk': 60, 'eq': 0, 'Ga': 60, 'nu': 15, 'fa': 0, 'h12': 0, 'fw1': 15, 'mb1': 0.5, 's1': 0, 'qb1': 8, 'h10': 60, 'c2': 1, 's3': 2, 'fg': 15}
ORDER = (
    "at0", "c2", "at1", "c3", "fw0", "fw1", "er0", "bw0", "er1", "Ga", "Gb", "bw1", "na", "Gg", "mb0", "nb", "fa", "ab0", "h00", "Gu", "fb", "h01", "mb1", "ng", "ab1", "h10", "h02", "ea", "h11", "nu", "h12", "Go", "fg", "qb0", "eb", "Gq", "qb1", "Gk", "in0", "no", "eg", "fu", "in1", "s0", "nk", "s1", "fo", "s2", "nq", "eu", "s3", "fq", "eo", "fk", "eq", "ek",
)
PRESENT = [5]


def nn(left, right):
    return lax.dot_general(left, right, (((1,), (0,)), ((), ())), preferred_element_type=F32)


def nt(left, right):
    return lax.dot_general(left, right, (((1,), (1,)), ((), ())), preferred_element_type=F32)


def run(body, name, grid, ins, outs, scratch=(), prefetch=(), into=None, after=(), meets=None):
    num_ins = len(prefetch) + len(ins)
    kept = [(out, array) for out, array in (into or {}).items() if array is not None]
    aliases = {num_ins + at: out for at, (out, _) in enumerate(kept)}
    hidden = [array for _, array in kept] + list(after)

    def inner(*refs):
        body(*refs[:num_ins], *refs[num_ins + len(hidden) :])

    return pl.pallas_call(
        inner,
        grid_spec=pltpu.PrefetchScalarGridSpec(
            num_scalar_prefetch=len(prefetch),
            grid=grid,
            in_specs=[spec for _, spec in ins] + [pl.BlockSpec(memory_space=pl.ANY)] * len(hidden),
            out_specs=[spec for _, _, spec in outs],
            scratch_shapes=list(scratch),
        ),
        out_shape=[jax.ShapeDtypeStruct(shape, dtype) for shape, dtype, _ in outs],
        input_output_aliases=aliases,
        compiler_params=pltpu.CompilerParams(
            vmem_limit_bytes=61 * MIB, collective_id=meets, has_side_effects=meets is not None
        ),
        cost_estimate=pl.CostEstimate(
            flops=1000 + int(1e9 * PRESENT[0]),
            bytes_accessed=1000,
            transcendentals=0,
        ),
        name=name,
    )(*prefetch, *[array for array, _ in ins], *hidden)


def phase(first, count):
    return lambda i: jnp.clip(i - first, 0, count - 1)


def in_phase(step, first, count):
    return pl.when((step >= first) & (step < first + count))


def divisor(total, *sizes):
    return next(size for size in sizes + (total,) if total % size == 0)


def whole(array, *prefetch):
    zeros = (0,) * array.ndim
    return pl.BlockSpec(array.shape, lambda *_: zeros)


def rms_scale(rows):
    return lax.rsqrt(jnp.mean(rows * rows, axis=-1, keepdims=True) + EPS)


def norm_back(rows, gain, grad_normed):
    scale = rms_scale(rows)
    unit_rows = rows * scale
    weighted = grad_normed * gain
    grad_rows = scale * (
        weighted - unit_rows * jnp.mean(weighted * unit_rows, axis=-1, keepdims=True)
    )
    return grad_rows, jnp.sum(grad_normed * unit_rows, axis=0, keepdims=True)


def rotated(head, cos, sin):
    first, second = head[:HALF], head[HALF:]
    return jnp.concatenate([first * cos - second * sin, second * cos + first * sin], axis=0)


def rotated_back(head, cos, sin):
    first, second = head[:HALF], head[HALF:]
    return jnp.concatenate([first * cos + second * sin, second * cos - first * sin], axis=0)


def total_of(parts):
    total = parts[0][...].astype(F32)
    for part in parts[1:]:
        total = total + part[...].astype(F32)
    return total


def accumulate(ref, value, first):
    @pl.when(first)
    def _():
        ref[...] = value

    @pl.when(jnp.logical_not(first))
    def _():
        ref[...] = ref[...] + value


def kv_body(h_ref, gain_ref, wk_ref, wv_ref, cos_ref, sin_ref, n_ref, nt_ref, kv_ref):
    h = h_ref[...].astype(F32)
    normed = (h * rms_scale(h) * gain_ref[...]).astype(BF16)
    n_ref[...] = normed
    nt_ref[...] = normed.T
    cos, sin = cos_ref[...], sin_ref[...]
    keys = nt(wk_ref[...], normed)
    for at in range(0, wk_ref.shape[0], HEAD_SIZE):
        kv_ref[0, at : at + HEAD_SIZE, :] = rotated(keys[at : at + HEAD_SIZE], cos, sin).astype(
            BF16
        )
    kv_ref[1] = nt(wv_ref[...], normed).astype(BF16)


def kv_project(seq, hidden, gain, key_t, value_t, cos, sin, n_cols, after):
    num_seqs, rows, model = hidden.shape
    width = key_t.shape[0]
    tile = min(256, rows)
    steps = rows // tile
    table = pl.BlockSpec((None, HALF, tile), lambda i: (seq, 0, i))
    return run(
        kv_body,
        "kv_project",
        (steps,),
        [
            (hidden, pl.BlockSpec((None, tile, model), lambda i: (seq, i, 0))),
            (gain, whole(gain)),
            (key_t, whole(key_t)),
            (value_t, whole(value_t)),
            (cos, table),
            (sin, table),
        ],
        [
            ((rows, model), BF16, pl.BlockSpec((tile, model), lambda i: (i, 0))),
            (
                (model, num_seqs * rows),
                BF16,
                pl.BlockSpec((model, tile), lambda i: (0, seq * steps + i)),
            ),
            ((2, width, rows), BF16, pl.BlockSpec((2, width, tile), lambda i: (0, 0, i))),
        ],
        into={1: n_cols},
        after=after,
    )


def q_body(n_ref, w_ref, cos_ref, sin_ref, q_ref):
    factor = LOG2E / math.sqrt(HEAD_SIZE)
    cos, sin = cos_ref[...] * factor, sin_ref[...] * factor
    queries = nn(n_ref[...], w_ref[...]).T
    for at in range(0, w_ref.shape[1], HEAD_SIZE):
        q_ref[at : at + HEAD_SIZE, :] = rotated(queries[at : at + HEAD_SIZE], cos, sin).astype(BF16)


def q_project(seq, normed, w_query, cos, sin, after):
    rows, model = normed.shape
    width = w_query.shape[1]
    tile = divisor(width, 640)
    table = pl.BlockSpec((None, HALF, rows), lambda j: (seq, 0, 0))
    return run(
        q_body,
        "q_project",
        (width // tile,),
        [
            (normed, whole(normed)),
            (w_query, pl.BlockSpec((model, tile), lambda j: (0, j))),
            (cos, table),
            (sin, table),
        ],
        [((width, rows), BF16, pl.BlockSpec((tile, rows), lambda j: (j, 0)))],
        after=after,
    )[0]


def side_by_side(ref, group, here):
    return jnp.concatenate(
        [ref[r * HEAD_SIZE : (r + 1) * HEAD_SIZE, here] for r in range(group)], axis=1
    )


def allowed_block(key_at, query_at, start_row, block, group):
    shape = (block, block * group)
    key_place = key_at + lax.broadcasted_iota(jnp.int32, shape, 0)
    query_place = query_at + lax.broadcasted_iota(jnp.int32, (1, block * group), 1) % block
    return (key_place >= start_row) & (key_place <= query_place)


def key_loops(low, full, diagonal, step, carry):
    carry = lax.fori_loop(low, jnp.minimum(full, diagonal), functools.partial(step, True), carry)
    carry = lax.fori_loop(
        jnp.maximum(full, low), diagonal, functools.partial(step, False), carry
    )
    return step(True, diagonal, carry)


def attend_body(block, low_ref, full_ref, start_ref, q_ref, *refs):
    *kv_refs, o_ref, all_ref, lse_ref, keys, values, mixed = refs
    chunks = len(kv_refs)
    piece = q_ref.shape[1]
    group = q_ref.shape[0] // HEAD_SIZE
    own = (chunks - 1) * piece
    for chunk, kv_ref in enumerate(kv_refs):
        at = slice(chunk * piece, (chunk + 1) * piece)
        keys[at, :] = kv_ref[0].T
        values[:HEAD_SIZE, at] = kv_ref[1]
    values[HEAD_SIZE:, :] = jnp.ones((values.shape[0] - HEAD_SIZE, values.shape[1]), BF16)
    for at in range(0, piece, block):
        here = slice(at, at + block)
        start_row = jnp.concatenate([start_ref[:, here]] * group, axis=1)
        queries = side_by_side(q_ref, group, here)
        mixed[...] = jnp.zeros(mixed.shape, F32)

        def step(masked, key_block, top):
            key_at = pl.multiple_of(key_block * block, block)
            scores = nn(keys[pl.ds(key_at, block), :], queries)
            if masked:
                allowed = allowed_block(key_at, own + at, start_row, block, group)
                scores = jnp.where(allowed, scores, NEG_BIG)
            new = jnp.maximum(top, jnp.max(scores, axis=0, keepdims=True))
            weights = jnp.exp2(scores - new).astype(BF16)
            mixed[...] = mixed[...] * jnp.exp2(top - new) + nn(
                values[:, pl.ds(key_at, block)], weights
            )
            return new

        top = key_loops(
            low_ref[at // block],
            full_ref[at // block],
            (own + at) // block,
            step,
            jnp.full((1, block * group), NEG_BIG, F32),
        )
        total = mixed[HEAD_SIZE : HEAD_SIZE + 1, :]
        result = (mixed[:HEAD_SIZE, :] / total).astype(BF16)
        lse = top + jnp.log2(total)
        for r in range(group):
            head, part = slice(r * HEAD_SIZE, (r + 1) * HEAD_SIZE), slice(r * block, (r + 1) * block)
            o_ref[head, here] = result[:, part]
            all_ref[head, here] = result[:, part]
            lse_ref[r : r + 1, here] = lse[:, part]


def attend(seq, num_seqs, low, full, start, queries, kv_chunks, mixed, after):
    width, piece = queries.shape
    kv_heads = kv_chunks[0].shape[1] // HEAD_SIZE
    rows = width // kv_heads
    group = rows // HEAD_SIZE
    block = min(256, piece)
    chunks = len(kv_chunks)
    per_head = pl.BlockSpec((rows, piece), lambda h, *_: (h, 0))
    kv_spec = pl.BlockSpec((2, HEAD_SIZE, piece), lambda h, *_: (0, h, 0))
    return run(
        functools.partial(attend_body, block),
        "attend",
        (kv_heads,),
        [(start, whole(start)), (queries, per_head)] + [(kv, kv_spec) for kv in kv_chunks],
        [
            ((width, piece), BF16, per_head),
            (
                (width, num_seqs * piece),
                BF16,
                pl.BlockSpec((rows, piece), lambda h, *_: (h, seq)),
            ),
            (
                (kv_heads, group, piece),
                F32,
                pl.BlockSpec((None, group, piece), lambda h, *_: (h, 0, 0)),
            ),
        ],
        scratch=[
            pltpu.VMEM((chunks * piece, HEAD_SIZE), BF16),
            pltpu.VMEM((HEAD_SIZE + 16, chunks * piece), BF16),
            pltpu.VMEM((HEAD_SIZE + 16, group * block), F32),
        ],
        prefetch=[low, full],
        into={1: mixed},
        after=after,
    )


def attend_back_body(
    block, low_ref, full_ref, start_ref, cos_ref, sin_ref, q_ref, o_ref, do_ref, lse_ref, *refs
):
    *refs, keys, keys_t, values, dq_sum, dk_sum, dv_sum = refs
    chunks = (len(refs) - 1) // 2
    kv_refs, dq_ref, dkv_refs = refs[:chunks], refs[chunks], refs[chunks + 1 :]
    piece = q_ref.shape[1]
    group = q_ref.shape[0] // HEAD_SIZE
    own = (chunks - 1) * piece
    scale = 1.0 / math.sqrt(HEAD_SIZE)
    dk_sum[...] = jnp.zeros(dk_sum.shape, F32)
    dv_sum[...] = jnp.zeros(dv_sum.shape, F32)
    for chunk, kv_ref in enumerate(kv_refs):
        at = slice(chunk * piece, (chunk + 1) * piece)
        keys_t[:, at] = kv_ref[0]
        keys[at, :] = kv_ref[0].T
        values[at, :] = kv_ref[1].T
    for at in range(0, piece, block):
        here = slice(at, at + block)
        start_row = jnp.concatenate([start_ref[:, here]] * group, axis=1)
        queries = side_by_side(q_ref, group, here)
        grads = side_by_side(do_ref, group, here)
        outs = side_by_side(o_ref, group, here)
        delta = jnp.sum(outs.astype(F32) * grads.astype(F32), axis=0, keepdims=True)
        lse = jnp.concatenate([lse_ref[r : r + 1, here] for r in range(group)], axis=1)
        dq_sum[...] = jnp.zeros(dq_sum.shape, F32)

        def step(masked, key_block, carry):
            key_at = pl.multiple_of(key_block * block, block)
            inside = pl.ds(key_at, block)
            scores = nn(keys[inside, :], queries)
            if masked:
                allowed = allowed_block(key_at, own + at, start_row, block, group)
                scores = jnp.where(allowed, scores, NEG_BIG)
            probs = jnp.exp2(scores - lse)
            dv_sum[:, inside] = dv_sum[:, inside] + nt(grads, probs.astype(BF16))
            grad = (probs * (nn(values[inside, :], grads) - delta)).astype(BF16)
            dk_sum[:, inside] = dk_sum[:, inside] + nt(queries, grad)
            dq_sum[...] = dq_sum[...] + nn(keys_t[:, inside], grad)
            return carry

        key_loops(low_ref[at // block], full_ref[at // block], (own + at) // block, step, 0)
        cos, sin = cos_ref[:, here], sin_ref[:, here]
        for r in range(group):
            rounded = (dq_sum[:, r * block : (r + 1) * block] * scale).astype(BF16).astype(F32)
            dq_ref[r * HEAD_SIZE : (r + 1) * HEAD_SIZE, here] = rotated_back(
                rounded, cos, sin
            ).astype(BF16)
    for chunk, dkv_ref in enumerate(dkv_refs):
        at = slice(chunk * piece, (chunk + 1) * piece)
        dkv_ref[0] = (dk_sum[:, at] * (1.0 / LOG2E)).astype(BF16)
        dkv_ref[1] = dv_sum[:, at].astype(BF16)


def attend_back(
    seq, num_seqs, low, full, start, cos, sin, queries, mixed, grad_mixed, lse, kv_chunks, dq, after
):
    width, piece = queries.shape
    kv_heads = kv_chunks[0].shape[1] // HEAD_SIZE
    rows = width // kv_heads
    group = rows // HEAD_SIZE
    block = min(256, piece)
    keys = len(kv_chunks) * piece
    per_head = pl.BlockSpec((rows, piece), lambda h, *_: (h, 0))
    per_head_seq = pl.BlockSpec((rows, piece), lambda h, *_: (h, seq))
    table = pl.BlockSpec((None, HALF, piece), lambda h, *_: (seq, 0, 0))
    kv_spec = pl.BlockSpec((2, HEAD_SIZE, piece), lambda h, *_: (0, h, 0))
    return run(
        functools.partial(attend_back_body, block),
        "attend_back",
        (kv_heads,),
        [
            (start, whole(start)),
            (cos, table),
            (sin, table),
            (queries, per_head),
            (mixed, per_head_seq),
            (grad_mixed, per_head),
            (lse, pl.BlockSpec((None, group, piece), lambda h, *_: (h, 0, 0))),
        ]
        + [(kv, kv_spec) for kv in kv_chunks],
        [
            ((width, num_seqs * piece), BF16, per_head_seq),
        ]
        + [(kv.shape, BF16, kv_spec) for kv in kv_chunks],
        scratch=[
            pltpu.VMEM((keys, HEAD_SIZE), BF16),
            pltpu.VMEM((HEAD_SIZE, keys), BF16),
            pltpu.VMEM((keys, HEAD_SIZE), BF16),
            pltpu.VMEM((HEAD_SIZE, group * block), F32),
            pltpu.VMEM((HEAD_SIZE, keys), F32),
            pltpu.VMEM((HEAD_SIZE, keys), F32),
        ],
        prefetch=[low, full],
        into={0: dq},
        after=after,
    )


def qkv_back_body(
    dq_ref, cos_ref, sin_ref, wq_ref, wk_ref, wv_ref, own_ref, came_ref, *refs
):
    dkv_ref, out_ref, dq_rows, dk_rows, dv_rows = refs
    width = wk_ref.shape[0]

    @pl.when(pl.program_id(0) == 0)
    def _():
        cos, sin = cos_ref[...], sin_ref[...]
        for at in range(0, width, HEAD_SIZE):
            head = slice(at, at + HEAD_SIZE)
            rows = own_ref[0, head].astype(F32) + came_ref[0, head].astype(F32)
            rows = rows.astype(BF16).astype(F32)
            dkv_ref[at : at + HEAD_SIZE, :] = rotated_back(rows, cos, sin).astype(BF16)
        dkv_ref[width:, :] = (own_ref[1].astype(F32) + came_ref[1].astype(F32)).astype(BF16)
        dq_rows[...] = dq_ref[...].T
        dk_rows[...] = dkv_ref[:width].T
        dv_rows[...] = dkv_ref[width:].T

    out_ref[...] = (
        nt(dq_rows[...], wq_ref[...])
        + nn(dk_rows[...], wk_ref[...])
        + nn(dv_rows[...], wv_ref[...])
    ).astype(BF16)


def qkv_back(seq, dq, cos, sin, w_query, key_t, value_t, own, came, dkv, after):
    model, width_q = w_query.shape
    width = key_t.shape[0]
    piece = own.shape[-1]
    tile = 1280
    table = pl.BlockSpec((None, HALF, piece), lambda j: (seq, 0, 0))
    narrow = pl.BlockSpec((width, tile), lambda j: (0, j))
    return run(
        qkv_back_body,
        "qkv_back",
        (model // tile,),
        [
            (dq, pl.BlockSpec((width_q, piece), lambda j: (0, seq))),
            (cos, table),
            (sin, table),
            (w_query, pl.BlockSpec((tile, width_q), lambda j: (j, 0))),
            (key_t, narrow),
            (value_t, narrow),
            (own, whole(own)),
            (came, whole(came)),
        ],
        [
            (
                (2 * width, dq.shape[1]),
                BF16,
                pl.BlockSpec((2 * width, piece), lambda j: (0, seq)),
            ),
            ((piece, model), BF16, pl.BlockSpec((piece, tile), lambda j: (0, j))),
        ],
        scratch=[
            pltpu.VMEM((piece, width_q), BF16),
            pltpu.VMEM((piece, width), BF16),
            pltpu.VMEM((piece, width), BF16),
        ],
        into={0: dkv},
        after=after,
    )


def forward_body(counts, heads, h_ref, gain_ref, wg_ref, wu_ref, wd_ref, *refs):
    o_refs, wo_refs, refs = refs[:heads], refs[heads : 2 * heads], refs[2 * heads :]
    m_ref, nt_ref, z_ref, a_ref, b_ref, part_ref, o_rows, attn, normed, inner = refs
    attn_steps, norm_steps, wide_steps, out_steps = counts
    step = pl.program_id(0)

    @pl.when(step == 0)
    def _():
        for at, o_ref in enumerate(o_refs):
            o_rows[at] = o_ref[...].T

    @in_phase(step, 0, attn_steps)
    def _():
        total = nn(o_rows[0], wo_refs[0][...])
        for at in range(1, heads):
            total = total + nn(o_rows[at], wo_refs[at][...])
        attn[step] = total

    @in_phase(step, attn_steps, norm_steps)
    def _():
        at = pl.ds(pl.multiple_of((step - attn_steps) * ROWS, ROWS), ROWS)
        added = jnp.concatenate([attn[part, at, :] for part in range(attn_steps)], axis=1)
        middle = h_ref[...].astype(F32) + added
        m_ref[...] = middle.astype(BF16)
        rows = (middle * rms_scale(middle) * gain_ref[...]).astype(BF16)
        normed[at, :] = rows
        nt_ref[...] = rows.T

    first = attn_steps + norm_steps

    @in_phase(step, first, wide_steps)
    def _():
        gate = nn(normed[...], wg_ref[...])
        up = nn(normed[...], wu_ref[...])
        sig = jax.nn.sigmoid(gate)
        silu = gate * sig
        z = (silu * up).astype(BF16)
        z_ref[...] = z
        inner[step - first] = z
        a_ref[...] = (up * sig * (1.0 + gate * (1.0 - sig))).astype(BF16)
        b_ref[...] = silu.astype(BF16)

    @in_phase(step, first + wide_steps, out_steps)
    def _():
        width = inner.shape[2]
        total = nn(inner[0], wd_ref[:width])
        for at in range(1, wide_steps):
            total = total + nn(inner[at], wd_ref[at * width : (at + 1) * width])
        part_ref[...] = total.astype(BF16)


def forward_mlp(seq, hidden, gain, w_gate, w_up, w_down, mixed, w_outs, normed_t, inner, after):
    num_seqs, rows, model = hidden.shape
    hidden_width = w_gate.shape[1]
    width = mixed[0].shape[0]
    wide, narrow = divisor(hidden_width, 512), 640
    counts = (model // narrow, rows // ROWS, hidden_width // wide, model // narrow)
    attn, norm, mid, out = (phase(sum(counts[:at]), count) for at, count in enumerate(counts))
    row_spec = pl.BlockSpec((ROWS, model), lambda i: (norm(i), 0))
    weight_spec = pl.BlockSpec((model, wide), lambda i: (0, mid(i)))
    wide_spec = pl.BlockSpec((rows, wide), lambda i: (0, mid(i)))
    return run(
        functools.partial(forward_body, counts, len(mixed)),
        "forward_mlp",
        (sum(counts),),
        [
            (hidden, pl.BlockSpec((None, ROWS, model), lambda i: (seq, norm(i), 0))),
            (gain, whole(gain)),
            (w_gate, weight_spec),
            (w_up, weight_spec),
            (w_down, pl.BlockSpec((hidden_width, narrow), lambda i: (0, out(i)))),
        ]
        + [(part, whole(part)) for part in mixed]
        + [(part, pl.BlockSpec((width, narrow), lambda i: (0, attn(i)))) for part in w_outs],
        [
            ((rows, model), BF16, row_spec),
            (
                (model, num_seqs * rows),
                BF16,
                pl.BlockSpec((model, ROWS), lambda i: (0, seq * counts[1] + norm(i))),
            ),
            (
                (num_seqs, rows, hidden_width),
                BF16,
                pl.BlockSpec((None, rows, wide), lambda i: (seq, 0, mid(i))),
            ),
            ((rows, hidden_width), BF16, wide_spec),
            ((rows, hidden_width), BF16, wide_spec),
            ((rows, model), BF16, pl.BlockSpec((rows, narrow), lambda i: (0, out(i)))),
        ],
        scratch=[
            pltpu.VMEM((len(mixed), rows, width), BF16),
            pltpu.VMEM((counts[0], rows, narrow), F32),
            pltpu.VMEM((rows, model), BF16),
            pltpu.VMEM((counts[2], rows, wide), BF16),
        ],
        into={1: normed_t, 2: inner},
        after=after,
    )


def error_body(m_ref, teacher_ref, valid_ref, *refs):
    *parts, out_ref, dy_ref, dyt_ref, loss_ref = refs
    output = m_ref[...].astype(F32) + total_of(parts)
    out_ref[...] = output.astype(BF16)
    errors = output - teacher_ref[...].astype(F32)
    valid = valid_ref[...]
    rounded = (valid * errors).astype(BF16)
    dy_ref[...] = rounded
    dyt_ref[...] = rounded.T
    squares = jnp.sum(valid * errors * errors, axis=0, keepdims=True)
    accumulate(loss_ref, squares, pl.program_id(0) == 0)


def output_error(seq, middle, teacher, valid, parts, layer_out, grad_t, after):
    num_seqs, rows, model = teacher.shape
    steps = rows // ROWS
    row_spec = pl.BlockSpec((ROWS, model), lambda i: (i, 0))
    seq_spec = pl.BlockSpec((None, ROWS, model), lambda i: (seq, i, 0))
    return run(
        error_body,
        "output_error",
        (steps,),
        [
            (middle, row_spec),
            (teacher, seq_spec),
            (valid, pl.BlockSpec((None, ROWS, 1), lambda i: (seq, i, 0))),
        ]
        + [(part, row_spec) for part in parts],
        [
            ((num_seqs, rows, model), BF16, seq_spec),
            ((rows, model), BF16, row_spec),
            (
                (model, num_seqs * rows),
                BF16,
                pl.BlockSpec((model, ROWS), lambda i: (0, seq * steps + i)),
            ),
            ((1, model), F32, pl.BlockSpec((1, model), lambda i: (0, 0))),
        ],
        into={0: layer_out, 2: grad_t},
        after=after,
    )


def backward_body(counts, dy_ref, wd_ref, a_ref, b_ref, wg_ref, wu_ref, *refs):
    dg_ref, du_ref, part_ref, gates, ups = refs
    wide_steps, out_steps = counts
    step = pl.program_id(0)

    @in_phase(step, 0, wide_steps)
    def _():
        grad_inner = nt(dy_ref[...], wd_ref[...])
        d_gate = (grad_inner * a_ref[...].astype(F32)).astype(BF16)
        d_up = (grad_inner * b_ref[...].astype(F32)).astype(BF16)
        dg_ref[...] = d_gate
        du_ref[...] = d_up
        gates[step] = d_gate
        ups[step] = d_up

    @in_phase(step, wide_steps, out_steps)
    def _():
        width = gates.shape[2]
        total = None
        for at in range(wide_steps):
            columns = slice(at * width, (at + 1) * width)
            term = nt(gates[at], wg_ref[:, columns]) + nt(ups[at], wu_ref[:, columns])
            total = term if total is None else total + term
        part_ref[...] = total.astype(BF16)


def backward_mlp(seq, num_seqs, grad_out, w_down, a, b, w_gate, w_up, kept, after):
    rows, model = grad_out.shape
    hidden_width = w_gate.shape[1]
    wide, narrow = divisor(hidden_width, 512), 512
    counts = (hidden_width // wide, model // narrow)
    mid, out = phase(0, counts[0]), phase(counts[0], counts[1])
    wide_spec = pl.BlockSpec((rows, wide), lambda i: (0, mid(i)))
    wide_seq = pl.BlockSpec((None, rows, wide), lambda i: (seq, 0, mid(i)))
    weight_spec = pl.BlockSpec((narrow, hidden_width), lambda i: (out(i), 0))
    return run(
        functools.partial(backward_body, counts),
        "backward_mlp",
        (sum(counts),),
        [
            (grad_out, whole(grad_out)),
            (w_down, pl.BlockSpec((wide, model), lambda i: (mid(i), 0))),
            (a, wide_spec),
            (b, wide_spec),
            (w_gate, weight_spec),
            (w_up, weight_spec),
        ],
        [
            ((num_seqs, rows, hidden_width), BF16, wide_seq),
            ((num_seqs, rows, hidden_width), BF16, wide_seq),
            ((rows, model), BF16, pl.BlockSpec((rows, narrow), lambda i: (0, out(i)))),
        ],
        scratch=[
            pltpu.VMEM((counts[0], rows, wide), BF16),
            pltpu.VMEM((counts[0], rows, wide), BF16),
        ],
        into=dict(zip((0, 1), kept)),
        after=after,
    )


def middle_back_body(counts, m_ref, dy_ref, gain_ref, w_ref, *refs):
    *parts, dm_ref, dmt_ref, dg_ref, do_ref, grad_t = refs
    norm_steps, out_steps = counts
    step = pl.program_id(0)

    @in_phase(step, 0, norm_steps)
    def _():
        grad_rows, grad_gain = norm_back(
            m_ref[...].astype(F32), gain_ref[...], total_of(parts)
        )
        rounded = (dy_ref[...].astype(F32) + grad_rows).astype(BF16)
        dm_ref[...] = rounded
        rounded_t = rounded.T
        dmt_ref[...] = rounded_t
        grad_t[step] = rounded_t
        accumulate(dg_ref, grad_gain, step == 0)

    @in_phase(step, norm_steps, out_steps)
    def _():
        columns = jnp.concatenate([grad_t[at] for at in range(norm_steps)], axis=1)
        do_ref[...] = nn(w_ref[...], columns).astype(BF16)


def middle_back(seq, num_seqs, middle, grad_output, gain, w_out, parts, grad_t, after):
    rows, model = middle.shape
    width = w_out.shape[0]
    tile = divisor(width, 640)
    counts = (rows // ROWS, width // tile)
    norm, out = phase(0, counts[0]), phase(counts[0], counts[1])
    row_spec = pl.BlockSpec((ROWS, model), lambda i: (norm(i), 0))
    return run(
        functools.partial(middle_back_body, counts),
        "middle_back",
        (sum(counts),),
        [
            (middle, row_spec),
            (grad_output, row_spec),
            (gain, whole(gain)),
            (w_out, pl.BlockSpec((tile, model), lambda i: (out(i), 0))),
        ]
        + [(part, row_spec) for part in parts],
        [
            ((rows, model), BF16, row_spec),
            (
                (model, num_seqs * rows),
                BF16,
                pl.BlockSpec((model, ROWS), lambda i: (0, seq * counts[0] + norm(i))),
            ),
            ((1, model), F32, pl.BlockSpec((1, model), lambda i: (0, 0))),
            ((width, rows), BF16, pl.BlockSpec((tile, rows), lambda i: (out(i), 0))),
        ],
        scratch=[pltpu.VMEM((counts[0], model, ROWS), BF16)],
        into={1: grad_t},
        after=after,
    )


def input_back_body(scale_ref, h_ref, dm_ref, gain_ref, *refs):
    *parts, grad_ref, dg_ref = refs
    grad_rows, grad_gain = norm_back(h_ref[...].astype(F32), gain_ref[...], total_of(parts))
    grad_ref[...] = scale_ref[0] * (dm_ref[...].astype(F32) + grad_rows)
    accumulate(dg_ref, grad_gain, pl.program_id(0) == 0)


def input_back(seq, scale, hidden, grad_middle, gain, parts, earlier, after):
    num_seqs, rows, model = hidden.shape
    row_spec = pl.BlockSpec((ROWS, model), lambda i: (i, 0))
    seq_spec = pl.BlockSpec((None, ROWS, model), lambda i: (seq, i, 0))
    return run(
        input_back_body,
        "input_back",
        (rows // ROWS,),
        [
            (scale, pl.BlockSpec(memory_space=pltpu.SMEM)),
            (hidden, seq_spec),
            (grad_middle, row_spec),
            (gain, whole(gain)),
        ]
        + [(part, row_spec) for part in parts],
        [
            ((num_seqs, rows, model), F32, seq_spec),
            ((1, model), F32, pl.BlockSpec((1, model), lambda i: (0, 0))),
        ],
        into={0: earlier},
        after=after,
    )


def weight_body(flipped, x_ref, y_ref, y_before_ref, far_ref, sent_ref, kept_ref, *refs):
    x_all, staged, landed, send_sem, recv_sem = refs
    tiles = landed.shape[0]
    step = pl.program_id(0)
    dp, ctx = lax.axis_index("dp"), lax.axis_index("ctx")
    ctx_size = lax.axis_size("ctx")
    core, chip = dp % 2, dp // 2
    partner = dp + 1 - 2 * core
    half = x_all.shape[0] // 2

    def sending(at):
        return pltpu.make_async_remote_copy(
            src_ref=staged.at[at % 2],
            dst_ref=landed.at[at],
            send_sem=send_sem.at[at % 2],
            recv_sem=recv_sem.at[at],
            device_id={"dp": partner},
            device_id_type=pl.DeviceIdType.MESH,
        )

    @pl.when(step == 0)
    def _():
        barrier = pltpu.get_barrier_semaphore()
        pl.semaphore_signal(
            barrier, inc=1, device_id={"dp": partner}, device_id_type=pl.DeviceIdType.MESH
        )
        pl.semaphore_wait(barrier, 1)
        size = x_ref.shape[0] // (lax.axis_size("dp") * ctx_size)
        low, high = ctx % 2, ctx // 2
        at = 0
        for other_core in (1, 0):
            to_core = core + other_core * (1 - 2 * core)
            for other_chip in (1, 0):
                to_dp = 2 * (chip + other_chip * (1 - 2 * chip)) + to_core
                for other_low in (1, 0):
                    for other_high in (1, 0):
                        to_ctx = 2 * (high + other_high * (1 - 2 * high))
                        to_ctx = to_ctx + low + other_low * (1 - 2 * low)
                        row = pl.multiple_of((to_dp * ctx_size + to_ctx) * size, size)
                        x_all[at : at + size, :] = x_ref[pl.ds(row, size), :]
                        at += size

    def product(rows, ref):
        y = ref[...]
        return nt(rows, y) if flipped else nn(rows, y.reshape(-1, y.shape[-1]))

    @pl.when((step >= 2) & (step < tiles))
    def _():
        sending(step - 2).wait_send()

    @pl.when(step < tiles)
    def _():
        staged[step % 2] = product(x_all[:half, :], y_ref).astype(BF16)
        sending(step).start()

    @pl.when(step > 0)
    def _():
        total = product(x_all[half:, :], y_before_ref)
        sending(step - 1).wait_recv()
        total = (total + landed[step - 1].astype(F32)).astype(BF16)
        far_ref[...] = total[: half // 2]
        sent_ref[...] = total[half // 2 : half // 4 * 3]
        kept_ref[...] = total[half // 4 * 3 :]

    @pl.when(step == tiles)
    def _():
        for at in range(max(tiles - 2, 0), tiles):
            sending(at).wait_send()


def weight_grad(meets, x_t, y, flipped, half, after):
    model, tokens = x_t.shape
    if flipped:
        tile = divisor(y.shape[0], 640)
        tiles, first = y.shape[0] // tile, 0
        y_block, place = (tile, tokens), lambda at: (at, 0)
    else:
        tile = divisor(y.shape[2], 512, 128)
        tiles, first = y.shape[2] // tile, 0
        if half is not None:
            first, tiles = ((0, tiles // 2), (tiles // 2, tiles - tiles // 2))[half]
        y_block, place = y.shape[:2] + (tile,), lambda at: (0, 0, first + at)
    width = tile * tiles
    before = lambda i: jnp.maximum(i - 1, 0)
    outs = [
        ((rows, width), BF16, pl.BlockSpec((rows, tile), lambda i: (0, before(i))))
        for rows in (model // 4, model // 8, model // 8)
    ]
    return run(
        functools.partial(weight_body, flipped),
        "weight_grad",
        (tiles + 1,),
        [
            (x_t, whole(x_t)),
            (y, pl.BlockSpec(y_block, lambda i: place(jnp.minimum(i, tiles - 1)))),
            (y, pl.BlockSpec(y_block, lambda i: place(before(i)))),
        ],
        outs,
        scratch=[
            pltpu.VMEM((model, tokens), BF16),
            pltpu.VMEM((2, model // 2, tile), BF16),
            pltpu.VMEM((tiles, model // 2, tile), BF16),
            pltpu.SemaphoreType.DMA((2,)),
            pltpu.SemaphoreType.DMA((tiles,)),
        ],
        after=after,
        meets=meets,
    )


def add_body(*refs):
    refs[-1][...] = total_of(refs[:-1]).astype(BF16)


def final_body(scale_ref, *refs):
    count = 4
    total = total_of(refs[:count]) * scale_ref[0]
    at = 0
    for out_ref in refs[count:]:
        out_ref[...] = total[:, at : at + out_ref.shape[1]]
        at += out_ref.shape[1]


def swap(value, axis, bit):
    size = lax.axis_size(axis)
    return lax.ppermute(value, axis, [(i, i ^ bit) for i in range(size)])


class Halving:
    def __init__(self, meets, x_t, y, flipped, half, after):
        far, self.sent, self.kept = weight_grad(meets, x_t, y, flipped, half, after)
        self.came = swap(far, "dp", 2)
        self.last = far

    def added(self, name, rows, parts, after):
        width = self.sent.shape[1]
        tile = divisor(width, 1792, 1024, 768, 640)
        ins = [
            (
                array,
                pl.BlockSpec((rows, tile), functools.partial(lambda at, j: (at, j), first // rows)),
            )
            for array, first in parts
        ]
        spec = pl.BlockSpec((rows, tile), lambda j: (0, j))
        return run(
            add_body, name, (width // tile,), ins, [((rows, width), BF16, spec)], after=after
        )[0]

    def near(self, after):
        rows = self.sent.shape[0]
        send = self.added("near", rows, [(self.sent, 0), (self.came, 0)], after)
        self.pair = swap(send, "ctx", 1)
        return send

    def fold(self, after):
        rows = self.sent.shape[0] // 2
        parts = [(self.kept, 0), (self.came, 2 * rows), (self.pair, 0)]
        send = self.added("fold", rows, parts, after)
        self.end = swap(send, "ctx", 2)
        return send

    def final(self, scale, widths, after):
        rows, width = self.end.shape
        tile = width if len(widths) > 1 else divisor(width, 896, 1024, 768, 640)
        tiles = [(tile,), widths][len(widths) > 1]
        parts = [(self.kept, 1), (self.came, 3), (self.pair, 1), (self.end, 0)]
        self.result = run(
            final_body,
            "final",
            (width // tile,),
            [(scale, pl.BlockSpec(memory_space=pltpu.SMEM))]
            + [
                (part, pl.BlockSpec((rows, tile), functools.partial(lambda at, j: (at, j), at)))
                for part, at in parts
            ],
            [
                ((rows, each), F32, pl.BlockSpec((rows, cut), lambda j: (0, j)))
                for each, cut in zip(widths, tiles)
            ],
            after=after,
        )
        return self.result[0]


def tensor_parts(partial):
    if lax.axis_size("tensor") == 2:
        return [partial, swap(partial, "tensor", 1)]
    return [lax.psum(partial, "tensor")]


def tensor_copies(value):
    if lax.axis_size("tensor") == 2:
        return [value, swap(value, "tensor", 1)]
    return list(lax.all_gather(value, "tensor"))


def tensor_weights(weight, after):
    size, count = lax.axis_size("dp"), weight.shape[0]
    if lax.axis_size("tensor") != 2 or count % (16 * size):
        return list(lax.all_gather(weight, "tensor"))
    rows = count // size
    part = lax.dynamic_slice_in_dim(weight, lax.axis_index("dp") * rows, rows)
    return [weight, lax.all_gather(held(swap(part, "tensor", 1), after), "dp", axis=0, tiled=True)]


def held(value, *others):
    return lax.optimization_barrier((value, *others))[0]


def shift(value, step):
    size = lax.axis_size("ctx")
    pairs = [(i, i + step) for i in range(size) if 0 <= i + step < size]
    return lax.ppermute(value, "ctx", pairs)


def local(
    hidden_in,
    w_query,
    key_weight_matrix,
    value_weight_matrix,
    w_out,
    w_gate,
    w_up,
    w_down,
    attn_gain,
    mlp_gain,
    segments,
    valid_mask,
    teacher,
):
    num_seqs, piece, model = hidden_in.shape
    seqs = range(num_seqs)
    ctx_size = lax.axis_size("ctx")
    ctx = lax.axis_index("ctx")
    query_places = ctx * piece + jnp.arange(piece, dtype=jnp.int32)
    positions = (query_places[None, :] - segments).astype(F32)
    freqs = THETA ** (-2.0 * jnp.arange(HALF, dtype=F32) / HEAD_SIZE)
    angles = positions[:, None, :] * freqs[None, :, None]
    cos, sin = jnp.cos(angles), jnp.sin(angles)
    starts = (segments + (ctx_size - 1 - ctx) * piece)[:, None, :]
    block = min(256, piece)
    lows = starts[:, 0, ::block] // block
    fulls = (starts[:, 0, block - 1 :: block] + block - 1) // block
    attn_gain_row, mlp_gain_row = attn_gain[None, :], mlp_gain[None, :]
    key_t, value_t = key_weight_matrix.T, value_weight_matrix.T
    valid = valid_mask.astype(F32)[..., None]


    count = jnp.sum(valid_mask).reshape(1, 1)
    count = count + swap(count, "dp", 1)
    normed, queries, kv_chunks = [], [], []
    normed_t, last = None, hidden_in
    for s in seqs:
        n_rows, normed_t, kv_own = kv_project(
            s, hidden_in, attn_gain_row, key_t, value_t, cos, sin, normed_t, [last]
        )
        normed.append(n_rows)
        kv_chunks.append([kv_own])
        last = n_rows
    kv_chunks[0].append(shift(kv_chunks[0][0], 1))
    after = [last, kv_chunks[0][-1], count]
    kv_chunks[0].append(shift(held(kv_chunks[0][-1], last), 1))
    for s in seqs:
        queries.append(q_project(s, normed[s], w_query, cos, sin, after))
        last = queries[-1]
        after = [last]
    count = count + swap(held(count, queries[0]), "dp", 2)
    kv_chunks[0].append(shift(held(kv_chunks[0][-1], last), 1))
    for s in seqs[1:]:
        own = held(kv_chunks[s][0], kv_chunks[0][-1], last)
        for step in range(1, ctx_size):
            kv_chunks[s].append(shift(own, step))

    made = {"count": count}
    lse, middle, rows_a, rows_b = [], [], [], []
    losses, dys, mlp_gains, attn_gains, grad_middle = [], [], [], [], []
    heads, mlp_parts, dn2_parts, dn1_parts, pieces, came = [], [], [], [], [], [None, None]
    w_outs = tensor_weights(w_out, queries[-1])
    tokens = num_seqs * piece * ctx_size * lax.axis_size("dp")
    last_seq = num_seqs - 1

    def scale():
        return (tokens / made["count"].reshape(()).astype(F32)).reshape(1)

    def attention(s, after):
        heads_out, made["mixed"], lse_rows = attend(
            s,
            num_seqs,
            lows[s],
            fulls[s],
            starts[s],
            queries[s],
            kv_chunks[s][::-1],
            made.get("mixed"),
            after,
        )
        lse.append(lse_rows)
        heads.append(tensor_copies(heads_out))
        return lse_rows

    def forward(s, after):
        m_rows, made["n2"], made["z"], a, b, partial = forward_mlp(
            s,
            hidden_in,
            mlp_gain_row,
            w_gate,
            w_up,
            w_down,
            heads[s],
            w_outs,
            made.get("n2"),
            made.get("z"),
            after + [made["count"]],
        )
        middle.append(m_rows)
        rows_a.append(a)
        rows_b.append(b)
        mlp_parts.append(tensor_parts(partial))
        return m_rows

    def error(s, after):
        made["y"], dy, made["dy"], loss_row = output_error(
            s,
            middle[s],
            teacher,
            valid,
            mlp_parts[s],
            made.get("y"),
            made.get("dy"),
            after,
        )
        dys.append(dy)
        losses.append(loss_row)
        return dy

    def backward(s, after):
        made["dgate"], made["dup"], partial = backward_mlp(
            s,
            num_seqs,
            dys[s],
            w_down,
            rows_a[s],
            rows_b[s],
            w_gate,
            w_up,
            (made.get("dgate"), made.get("dup")),
            after,
        )
        dn2_parts.append(tensor_parts(partial))
        return partial

    def middle_step(s, after):
        dm, made["dm"], gain_row, made["do", s] = middle_back(
            s,
            num_seqs,
            middle[s],
            dys[s],
            mlp_gain_row,
            w_out,
            dn2_parts[s],
            made.get("dm"),
            after,
        )
        grad_middle.append(dm)
        mlp_gains.append(gain_row)
        return dm

    def attention_back(s, after):
        made["dq"], *parts = attend_back(
            s,
            num_seqs,
            lows[s],
            fulls[s],
            starts[s],
            cos,
            sin,
            queries[s],
            made["mixed"],
            made["do", s],
            lse[s],
            kv_chunks[s][::-1],
            made.get("dq"),
            after,
        )
        pieces.append(parts)
        return parts[0]

    def hop(s, at, after):
        total = pieces[s][at]
        if came[s] is not None:
            total = (total.astype(F32) + held(came[s], *after).astype(F32)).astype(BF16)
        came[s] = shift(total, -1)
        return after[0]

    def projections(s, after):
        made["dkv"], partial = qkv_back(
            s,
            made["dq"],
            cos,
            sin,
            w_query,
            key_t,
            value_t,
            pieces[s][-1],
            came[s],
            made.get("dkv"),
            after,
        )
        dn1_parts.append(tensor_parts(partial))
        return partial

    def halving(name, meets, x_t, y, flipped, half, after):
        made[name] = Halving(meets, made.get(x_t, normed_t), made[y], flipped, half, after)
        return made[name].last

    def input_step(s, after):
        made["dx"], gain_row = input_back(
            s,
            scale(),
            hidden_in,
            grad_middle[s],
            attn_gain_row,
            dn1_parts[s],
            made.get("dx"),
            after,
        )
        attn_gains.append(gain_row)
        return gain_row

    def hop_of(name, at, after):
        axis, bit = (("dp", 1), ("dp", 2), ("ctx", 1), ("ctx", 2))[at]
        total = held(made[name], *after)
        made[name] = total + swap(total, axis, bit)
        return after[0]

    def small_hop(at, after):
        if at == 0:
            loss = jnp.full((1, model), jnp.sum(sum(losses)))
            made["small"] = jnp.concatenate([sum(attn_gains), sum(mlp_gains), loss], axis=0)
        return hop_of("small", at, after)

    def finish(name, after):
        widths = (made[name].sent.shape[1],)
        if name == "k":
            widths = key_t.shape[:1] * 2
        return made[name].final(scale(), widths, after)

    steps = {
        "Ga": functools.partial(halving, "a", 0, "dy", "z", False, 0),
        "Gb": functools.partial(halving, "b", 6, "dy", "z", False, 1),
        "Gg": functools.partial(halving, "g", 3, "n2", "dgate", False, None),
        "Gu": functools.partial(halving, "u", 4, "n2", "dup", False, None),
        "Go": functools.partial(halving, "o", 1, "dm", "mixed", True, None),
        "Gq": functools.partial(halving, "q", 2, "n1", "dq", True, None),
        "Gk": functools.partial(halving, "k", 5, "n1", "dkv", True, None),
    }
    for name in "abguoqk":
        for short, stage in (("n", "near"), ("f", "fold")):
            steps[short + name] = lambda after, name=name, stage=stage: getattr(
                made[name], stage
            )(after)
        steps["e" + name] = functools.partial(finish, name)
    for at in range(4):
        steps["s%d" % at] = functools.partial(small_hop, at)
        steps["c%d" % at] = functools.partial(hop_of, "count", at)
    for s in seqs:
        for short, one in (
            ("at", attention),
            ("fw", forward),
            ("er", error),
            ("bw", backward),
            ("mb", middle_step),
            ("ab", attention_back),
            ("qb", projections),
            ("in", input_step),
        ):
            steps[short + str(s)] = functools.partial(one, s)
        for at in range(ctx_size - 1):
            steps["h%d%d" % (s, at)] = functools.partial(hop, s, at)
    for name in ORDER:
        PRESENT[0] = WEIGHTS.get(name, 5)
        last = steps[name]([last])

    (out_sum,), (gate_sum,), (up_sum,) = (made[name].result for name in "ogu")
    down_sum = jnp.concatenate(made["a"].result + made["b"].result, axis=1)
    size = model // (lax.axis_size("dp") * ctx_size)
    here = (lax.axis_index("dp") * ctx_size + ctx) * size
    small = made["small"]
    gains = lax.dynamic_slice_in_dim(small[:2], here, size, axis=1) * scale()
    return (
        made["y"],
        small[2, 0] / (made["count"].reshape(()).astype(F32) * model),
        made["dx"],
        *made["q"].result,
        *made["k"].result,
        out_sum.T,
        gate_sum,
        up_sum,
        down_sum.T,
        gains[0],
        gains[1],
    )


def solution(mesh):
    placed = (
        P("dp", "ctx", None),
        P(None, "tensor"),
        P(None, "tensor"),
        P(None, "tensor"),
        P("tensor", None),
        P(None, "tensor"),
        P(None, "tensor"),
        P("tensor", None),
        P(),
        P(),
        P("dp", "ctx"),
        P("dp", "ctx"),
        P("dp", "ctx", None),
    )
    return jax.shard_map(
        local,
        mesh=mesh,
        in_specs=placed,
        out_specs=(
            P("dp", "ctx", None),
            P(),
            P("dp", "ctx", None),
            P(("dp", "ctx"), "tensor"),
            P(("dp", "ctx"), "tensor"),
            P(("dp", "ctx"), "tensor"),
            P("tensor", ("dp", "ctx")),
            P(("dp", "ctx"), "tensor"),
            P(("dp", "ctx"), "tensor"),
            P("tensor", ("dp", "ctx")),
            P(("dp", "ctx")),
            P(("dp", "ctx")),
        ),
        check_vma=False,
    )
```

```python
import functools
import math

import jax
import jax.numpy as jnp
import numpy as np
from jax import lax
from jax.experimental import pallas as pl
from jax.experimental.pallas import tpu as pltpu
from jax.sharding import PartitionSpec as P

HEAD_SIZE = 80
HALF = HEAD_SIZE // 2
EPS = 1e-05
THETA = 1000000.0
NEG_BIG = -1e30
LOG2E = 1.4426950408889634
BF16 = jnp.bfloat16
F32 = jnp.float32
MIB = 1024 * 1024
ROWS = 128
WEIGHTS = {'at1': 30, 'ab1': 100, 'eb': 30, 'Gu': 60, 'at0': 30, 's0': 0, 'fw0': 30, 'Gb': 0.5, 'Gk': 0, 'in0': 15, 'eo': 60, 'na': 0.5, 'nk': 60, 'nu': 15, 'fa': 0, 'h12': 0, 'fw1': 15, 'mb1': 100, 's1': 0}
ORDER = (
    "at0", "c2", "qp1", "at1", "c3", "fw0", "fw1", "er0", "bw0", "er1", "Ga", "Gb", "bw1", "na", "Gg", "mb0", "nb", "fa", "ab0", "h00", "Gu", "h01", "fb", "mb1", "ng", "ab1", "h10", "h02", "ea", "h11", "nu", "h12", "Go", "fg", "qb0", "eb", "Gq", "qb1", "Gk", "in0", "no", "fu", "eg", "in1", "s0", "nk", "s1", "fo", "s2", "nq", "eu", "s3", "fq", "eo", "fk", "eq", "ek",
)
PRESENT = [5]


def nn(left, right):
    return lax.dot_general(left, right, (((1,), (0,)), ((), ())), preferred_element_type=F32)


def nt(left, right):
    return lax.dot_general(left, right, (((1,), (1,)), ((), ())), preferred_element_type=F32)


def run(body, name, grid, ins, outs, scratch=(), prefetch=(), into=None, after=(), meets=None):
    num_ins = len(prefetch) + len(ins)
    kept = [(out, array) for out, array in (into or {}).items() if array is not None]
    aliases = {num_ins + at: out for at, (out, _) in enumerate(kept)}
    hidden = [array for _, array in kept] + list(after)

    def inner(*refs):
        body(*refs[:num_ins], *refs[num_ins + len(hidden) :])

    return pl.pallas_call(
        inner,
        grid_spec=pltpu.PrefetchScalarGridSpec(
            num_scalar_prefetch=len(prefetch),
            grid=grid,
            in_specs=[spec for _, spec in ins] + [pl.BlockSpec(memory_space=pl.ANY)] * len(hidden),
            out_specs=[spec for _, _, spec in outs],
            scratch_shapes=list(scratch),
        ),
        out_shape=[jax.ShapeDtypeStruct(shape, dtype) for shape, dtype, _ in outs],
        input_output_aliases=aliases,
        compiler_params=pltpu.CompilerParams(
            vmem_limit_bytes=61 * MIB, collective_id=meets, has_side_effects=meets is not None
        ),
        cost_estimate=pl.CostEstimate(
            flops=1000 + int(1e9 * PRESENT[0]),
            bytes_accessed=1000,
            transcendentals=0,
        ),
        name=name,
    )(*prefetch, *[array for array, _ in ins], *hidden)


def phase(first, count):
    return lambda i: jnp.clip(i - first, 0, count - 1)


def in_phase(step, first, count):
    return pl.when((step >= first) & (step < first + count))


def divisor(total, *sizes):
    return next(size for size in sizes + (total,) if total % size == 0)


def whole(array, *prefetch):
    zeros = (0,) * array.ndim
    return pl.BlockSpec(array.shape, lambda *_: zeros)


def rms_scale(rows):
    return lax.rsqrt(jnp.mean(rows * rows, axis=-1, keepdims=True) + EPS)


def norm_back(rows, gain, grad_normed):
    scale = rms_scale(rows)
    unit_rows = rows * scale
    weighted = grad_normed * gain
    grad_rows = scale * (
        weighted - unit_rows * jnp.mean(weighted * unit_rows, axis=-1, keepdims=True)
    )
    return grad_rows, jnp.sum(grad_normed * unit_rows, axis=0, keepdims=True)


def rotated(head, cos, sin):
    first, second = head[:HALF], head[HALF:]
    return jnp.concatenate([first * cos - second * sin, second * cos + first * sin], axis=0)


def rotated_back(head, cos, sin):
    first, second = head[:HALF], head[HALF:]
    return jnp.concatenate([first * cos + second * sin, second * cos - first * sin], axis=0)


def total_of(parts):
    total = parts[0][...].astype(F32)
    for part in parts[1:]:
        total = total + part[...].astype(F32)
    return total


def accumulate(ref, value, first):
    @pl.when(first)
    def _():
        ref[...] = value

    @pl.when(jnp.logical_not(first))
    def _():
        ref[...] = ref[...] + value


def kv_body(h_ref, gain_ref, wk_ref, wv_ref, cos_ref, sin_ref, n_ref, nt_ref, kv_ref):
    h = h_ref[...].astype(F32)
    normed = (h * rms_scale(h) * gain_ref[...]).astype(BF16)
    n_ref[...] = normed
    nt_ref[...] = normed.T
    cos, sin = cos_ref[...], sin_ref[...]
    keys = nt(wk_ref[...], normed)
    for at in range(0, wk_ref.shape[0], HEAD_SIZE):
        kv_ref[0, at : at + HEAD_SIZE, :] = rotated(keys[at : at + HEAD_SIZE], cos, sin).astype(
            BF16
        )
    kv_ref[1] = nt(wv_ref[...], normed).astype(BF16)


def kv_project(seq, hidden, gain, key_t, value_t, cos, sin, n_cols, after):
    num_seqs, rows, model = hidden.shape
    width = key_t.shape[0]
    tile = min(256, rows)
    steps = rows // tile
    table = pl.BlockSpec((None, HALF, tile), lambda i: (seq, 0, i))
    return run(
        kv_body,
        "kv_project",
        (steps,),
        [
            (hidden, pl.BlockSpec((None, tile, model), lambda i: (seq, i, 0))),
            (gain, whole(gain)),
            (key_t, whole(key_t)),
            (value_t, whole(value_t)),
            (cos, table),
            (sin, table),
        ],
        [
            ((rows, model), BF16, pl.BlockSpec((tile, model), lambda i: (i, 0))),
            (
                (model, num_seqs * rows),
                BF16,
                pl.BlockSpec((model, tile), lambda i: (0, seq * steps + i)),
            ),
            ((2, width, rows), BF16, pl.BlockSpec((2, width, tile), lambda i: (0, 0, i))),
        ],
        into={1: n_cols},
        after=after,
    )


def q_body(n_ref, w_ref, cos_ref, sin_ref, q_ref):
    factor = LOG2E / math.sqrt(HEAD_SIZE)
    cos, sin = cos_ref[...] * factor, sin_ref[...] * factor
    queries = nn(n_ref[...], w_ref[...]).T
    for at in range(0, w_ref.shape[1], HEAD_SIZE):
        q_ref[at : at + HEAD_SIZE, :] = rotated(queries[at : at + HEAD_SIZE], cos, sin).astype(BF16)


def q_project(seq, normed, w_query, cos, sin, after):
    rows, model = normed.shape
    width = w_query.shape[1]
    tile = divisor(width, 640)
    table = pl.BlockSpec((None, HALF, rows), lambda j: (seq, 0, 0))
    return run(
        q_body,
        "q_project",
        (width // tile,),
        [
            (normed, whole(normed)),
            (w_query, pl.BlockSpec((model, tile), lambda j: (0, j))),
            (cos, table),
            (sin, table),
        ],
        [((width, rows), BF16, pl.BlockSpec((tile, rows), lambda j: (j, 0)))],
        after=after,
    )[0]


def side_by_side(ref, group, here):
    return jnp.concatenate(
        [ref[r * HEAD_SIZE : (r + 1) * HEAD_SIZE, here] for r in range(group)], axis=1
    )


def allowed_block(key_at, query_at, start_row, block, group):
    shape = (block, block * group)
    key_place = key_at + lax.broadcasted_iota(jnp.int32, shape, 0)
    query_place = query_at + lax.broadcasted_iota(jnp.int32, (1, block * group), 1) % block
    return (key_place >= start_row) & (key_place <= query_place)


def key_loops(low, full, diagonal, step, carry):
    carry = lax.fori_loop(low, jnp.minimum(full, diagonal), functools.partial(step, True), carry)
    carry = lax.fori_loop(
        jnp.maximum(full, low), diagonal, functools.partial(step, False), carry
    )
    return step(True, diagonal, carry)


def attend_body(block, low_ref, full_ref, start_ref, q_ref, *refs):
    *kv_refs, o_ref, all_ref, lse_ref, keys, values, mixed = refs
    chunks = len(kv_refs)
    piece = q_ref.shape[1]
    group = q_ref.shape[0] // HEAD_SIZE
    own = (chunks - 1) * piece
    for chunk, kv_ref in enumerate(kv_refs):
        at = slice(chunk * piece, (chunk + 1) * piece)
        keys[at, :] = kv_ref[0].T
        values[:HEAD_SIZE, at] = kv_ref[1]
    values[HEAD_SIZE:, :] = jnp.ones((values.shape[0] - HEAD_SIZE, values.shape[1]), BF16)
    for at in range(0, piece, block):
        here = slice(at, at + block)
        start_row = jnp.concatenate([start_ref[:, here]] * group, axis=1)
        queries = side_by_side(q_ref, group, here)
        mixed[...] = jnp.zeros(mixed.shape, F32)

        def step(masked, key_block, top):
            key_at = pl.multiple_of(key_block * block, block)
            scores = nn(keys[pl.ds(key_at, block), :], queries)
            if masked:
                allowed = allowed_block(key_at, own + at, start_row, block, group)
                scores = jnp.where(allowed, scores, NEG_BIG)
            new = jnp.maximum(top, jnp.max(scores, axis=0, keepdims=True))
            weights = jnp.exp2(scores - new).astype(BF16)
            mixed[...] = mixed[...] * jnp.exp2(top - new) + nn(
                values[:, pl.ds(key_at, block)], weights
            )
            return new

        top = key_loops(
            low_ref[at // block],
            full_ref[at // block],
            (own + at) // block,
            step,
            jnp.full((1, block * group), NEG_BIG, F32),
        )
        total = mixed[HEAD_SIZE : HEAD_SIZE + 1, :]
        result = (mixed[:HEAD_SIZE, :] / total).astype(BF16)
        lse = top + jnp.log2(total)
        for r in range(group):
            head, part = slice(r * HEAD_SIZE, (r + 1) * HEAD_SIZE), slice(r * block, (r + 1) * block)
            o_ref[head, here] = result[:, part]
            all_ref[head, here] = result[:, part]
            lse_ref[r : r + 1, here] = lse[:, part]


def attend(seq, num_seqs, low, full, start, queries, kv_chunks, mixed, after):
    width, piece = queries.shape
    kv_heads = kv_chunks[0].shape[1] // HEAD_SIZE
    rows = width // kv_heads
    group = rows // HEAD_SIZE
    block = min(256, piece)
    chunks = len(kv_chunks)
    per_head = pl.BlockSpec((rows, piece), lambda h, *_: (h, 0))
    kv_spec = pl.BlockSpec((2, HEAD_SIZE, piece), lambda h, *_: (0, h, 0))
    return run(
        functools.partial(attend_body, block),
        "attend",
        (kv_heads,),
        [(start, whole(start)), (queries, per_head)] + [(kv, kv_spec) for kv in kv_chunks],
        [
            ((width, piece), BF16, per_head),
            (
                (width, num_seqs * piece),
                BF16,
                pl.BlockSpec((rows, piece), lambda h, *_: (h, seq)),
            ),
            (
                (kv_heads, group, piece),
                F32,
                pl.BlockSpec((None, group, piece), lambda h, *_: (h, 0, 0)),
            ),
        ],
        scratch=[
            pltpu.VMEM((chunks * piece, HEAD_SIZE), BF16),
            pltpu.VMEM((HEAD_SIZE + 16, chunks * piece), BF16),
            pltpu.VMEM((HEAD_SIZE + 16, group * block), F32),
        ],
        prefetch=[low, full],
        into={1: mixed},
        after=after,
    )


def attend_back_body(
    block, low_ref, full_ref, start_ref, cos_ref, sin_ref, q_ref, o_ref, do_ref, lse_ref, *refs
):
    *refs, keys, keys_t, values, dq_sum, dk_sum, dv_sum = refs
    chunks = (len(refs) - 1) // 2
    kv_refs, dq_ref, dkv_refs = refs[:chunks], refs[chunks], refs[chunks + 1 :]
    piece = q_ref.shape[1]
    group = q_ref.shape[0] // HEAD_SIZE
    own = (chunks - 1) * piece
    scale = 1.0 / math.sqrt(HEAD_SIZE)
    dk_sum[...] = jnp.zeros(dk_sum.shape, F32)
    dv_sum[...] = jnp.zeros(dv_sum.shape, F32)
    for chunk, kv_ref in enumerate(kv_refs):
        at = slice(chunk * piece, (chunk + 1) * piece)
        keys_t[:, at] = kv_ref[0]
        keys[at, :] = kv_ref[0].T
        values[at, :] = kv_ref[1].T
    for at in range(0, piece, block):
        here = slice(at, at + block)
        start_row = jnp.concatenate([start_ref[:, here]] * group, axis=1)
        queries = side_by_side(q_ref, group, here)
        grads = side_by_side(do_ref, group, here)
        outs = side_by_side(o_ref, group, here)
        delta = jnp.sum(outs.astype(F32) * grads.astype(F32), axis=0, keepdims=True)
        lse = jnp.concatenate([lse_ref[r : r + 1, here] for r in range(group)], axis=1)
        dq_sum[...] = jnp.zeros(dq_sum.shape, F32)

        def step(masked, key_block, carry):
            key_at = pl.multiple_of(key_block * block, block)
            inside = pl.ds(key_at, block)
            scores = nn(keys[inside, :], queries)
            if masked:
                allowed = allowed_block(key_at, own + at, start_row, block, group)
                scores = jnp.where(allowed, scores, NEG_BIG)
            probs = jnp.exp2(scores - lse)
            dv_sum[:, inside] = dv_sum[:, inside] + nt(grads, probs.astype(BF16))
            grad = (probs * (nn(values[inside, :], grads) - delta)).astype(BF16)
            dk_sum[:, inside] = dk_sum[:, inside] + nt(queries, grad)
            dq_sum[...] = dq_sum[...] + nn(keys_t[:, inside], grad)
            return carry

        key_loops(low_ref[at // block], full_ref[at // block], (own + at) // block, step, 0)
        cos, sin = cos_ref[:, here], sin_ref[:, here]
        for r in range(group):
            rounded = (dq_sum[:, r * block : (r + 1) * block] * scale).astype(BF16).astype(F32)
            dq_ref[r * HEAD_SIZE : (r + 1) * HEAD_SIZE, here] = rotated_back(
                rounded, cos, sin
            ).astype(BF16)
    for chunk, dkv_ref in enumerate(dkv_refs):
        at = slice(chunk * piece, (chunk + 1) * piece)
        dkv_ref[0] = (dk_sum[:, at] * (1.0 / LOG2E)).astype(BF16)
        dkv_ref[1] = dv_sum[:, at].astype(BF16)


def attend_back(
    seq, num_seqs, low, full, start, cos, sin, queries, mixed, grad_mixed, lse, kv_chunks, dq, after
):
    width, piece = queries.shape
    kv_heads = kv_chunks[0].shape[1] // HEAD_SIZE
    rows = width // kv_heads
    group = rows // HEAD_SIZE
    block = min(256, piece)
    keys = len(kv_chunks) * piece
    per_head = pl.BlockSpec((rows, piece), lambda h, *_: (h, 0))
    per_head_seq = pl.BlockSpec((rows, piece), lambda h, *_: (h, seq))
    table = pl.BlockSpec((None, HALF, piece), lambda h, *_: (seq, 0, 0))
    kv_spec = pl.BlockSpec((2, HEAD_SIZE, piece), lambda h, *_: (0, h, 0))
    return run(
        functools.partial(attend_back_body, block),
        "attend_back",
        (kv_heads,),
        [
            (start, whole(start)),
            (cos, table),
            (sin, table),
            (queries, per_head),
            (mixed, per_head_seq),
            (grad_mixed, per_head),
            (lse, pl.BlockSpec((None, group, piece), lambda h, *_: (h, 0, 0))),
        ]
        + [(kv, kv_spec) for kv in kv_chunks],
        [
            ((width, num_seqs * piece), BF16, per_head_seq),
        ]
        + [(kv.shape, BF16, kv_spec) for kv in kv_chunks],
        scratch=[
            pltpu.VMEM((keys, HEAD_SIZE), BF16),
            pltpu.VMEM((HEAD_SIZE, keys), BF16),
            pltpu.VMEM((keys, HEAD_SIZE), BF16),
            pltpu.VMEM((HEAD_SIZE, group * block), F32),
            pltpu.VMEM((HEAD_SIZE, keys), F32),
            pltpu.VMEM((HEAD_SIZE, keys), F32),
        ],
        prefetch=[low, full],
        into={0: dq},
        after=after,
    )


def qkv_back_body(
    dq_ref, cos_ref, sin_ref, wq_ref, wk_ref, wv_ref, own_ref, came_ref, *refs
):
    dkv_ref, out_ref, dq_rows, dk_rows, dv_rows = refs
    width = wk_ref.shape[0]

    @pl.when(pl.program_id(0) == 0)
    def _():
        cos, sin = cos_ref[...], sin_ref[...]
        for at in range(0, width, HEAD_SIZE):
            head = slice(at, at + HEAD_SIZE)
            rows = own_ref[0, head].astype(F32) + came_ref[0, head].astype(F32)
            rows = rows.astype(BF16).astype(F32)
            dkv_ref[at : at + HEAD_SIZE, :] = rotated_back(rows, cos, sin).astype(BF16)
        dkv_ref[width:, :] = (own_ref[1].astype(F32) + came_ref[1].astype(F32)).astype(BF16)
        dq_rows[...] = dq_ref[...].T
        dk_rows[...] = dkv_ref[:width].T
        dv_rows[...] = dkv_ref[width:].T

    out_ref[...] = (
        nt(dq_rows[...], wq_ref[...])
        + nn(dk_rows[...], wk_ref[...])
        + nn(dv_rows[...], wv_ref[...])
    ).astype(BF16)


def qkv_back(seq, dq, cos, sin, w_query, key_t, value_t, own, came, dkv, after):
    model, width_q = w_query.shape
    width = key_t.shape[0]
    piece = own.shape[-1]
    tile = 1280
    table = pl.BlockSpec((None, HALF, piece), lambda j: (seq, 0, 0))
    narrow = pl.BlockSpec((width, tile), lambda j: (0, j))
    return run(
        qkv_back_body,
        "qkv_back",
        (model // tile,),
        [
            (dq, pl.BlockSpec((width_q, piece), lambda j: (0, seq))),
            (cos, table),
            (sin, table),
            (w_query, pl.BlockSpec((tile, width_q), lambda j: (j, 0))),
            (key_t, narrow),
            (value_t, narrow),
            (own, whole(own)),
            (came, whole(came)),
        ],
        [
            (
                (2 * width, dq.shape[1]),
                BF16,
                pl.BlockSpec((2 * width, piece), lambda j: (0, seq)),
            ),
            ((piece, model), BF16, pl.BlockSpec((piece, tile), lambda j: (0, j))),
        ],
        scratch=[
            pltpu.VMEM((piece, width_q), BF16),
            pltpu.VMEM((piece, width), BF16),
            pltpu.VMEM((piece, width), BF16),
        ],
        into={0: dkv},
        after=after,
    )


def forward_body(counts, heads, h_ref, gain_ref, wg_ref, wu_ref, wd_ref, *refs):
    o_refs, wo_refs, refs = refs[:heads], refs[heads : 2 * heads], refs[2 * heads :]
    m_ref, nt_ref, z_ref, a_ref, b_ref, part_ref, o_rows, attn, normed, inner = refs
    attn_steps, norm_steps, wide_steps, out_steps = counts
    step = pl.program_id(0)

    @pl.when(step == 0)
    def _():
        for at, o_ref in enumerate(o_refs):
            o_rows[at] = o_ref[...].T

    @in_phase(step, 0, attn_steps)
    def _():
        total = nn(o_rows[0], wo_refs[0][...])
        for at in range(1, heads):
            total = total + nn(o_rows[at], wo_refs[at][...])
        attn[step] = total

    @in_phase(step, attn_steps, norm_steps)
    def _():
        at = pl.ds(pl.multiple_of((step - attn_steps) * ROWS, ROWS), ROWS)
        added = jnp.concatenate([attn[part, at, :] for part in range(attn_steps)], axis=1)
        middle = h_ref[...].astype(F32) + added
        m_ref[...] = middle.astype(BF16)
        rows = (middle * rms_scale(middle) * gain_ref[...]).astype(BF16)
        normed[at, :] = rows
        nt_ref[...] = rows.T

    first = attn_steps + norm_steps

    @in_phase(step, first, wide_steps)
    def _():
        gate = nn(normed[...], wg_ref[...])
        up = nn(normed[...], wu_ref[...])
        sig = jax.nn.sigmoid(gate)
        silu = gate * sig
        z = (silu * up).astype(BF16)
        z_ref[...] = z
        inner[step - first] = z
        a_ref[...] = (up * sig * (1.0 + gate * (1.0 - sig))).astype(BF16)
        b_ref[...] = silu.astype(BF16)

    @in_phase(step, first + wide_steps, out_steps)
    def _():
        width = inner.shape[2]
        total = nn(inner[0], wd_ref[:width])
        for at in range(1, wide_steps):
            total = total + nn(inner[at], wd_ref[at * width : (at + 1) * width])
        part_ref[...] = total.astype(BF16)


def forward_mlp(seq, hidden, gain, w_gate, w_up, w_down, mixed, w_outs, normed_t, inner, after):
    num_seqs, rows, model = hidden.shape
    hidden_width = w_gate.shape[1]
    width = mixed[0].shape[0]
    wide, narrow = divisor(hidden_width, 512), 512
    counts = (model // narrow, rows // ROWS, hidden_width // wide, model // narrow)
    attn, norm, mid, out = (phase(sum(counts[:at]), count) for at, count in enumerate(counts))
    row_spec = pl.BlockSpec((ROWS, model), lambda i: (norm(i), 0))
    weight_spec = pl.BlockSpec((model, wide), lambda i: (0, mid(i)))
    wide_spec = pl.BlockSpec((rows, wide), lambda i: (0, mid(i)))
    return run(
        functools.partial(forward_body, counts, len(mixed)),
        "forward_mlp",
        (sum(counts),),
        [
            (hidden, pl.BlockSpec((None, ROWS, model), lambda i: (seq, norm(i), 0))),
            (gain, whole(gain)),
            (w_gate, weight_spec),
            (w_up, weight_spec),
            (w_down, pl.BlockSpec((hidden_width, narrow), lambda i: (0, out(i)))),
        ]
        + [(part, whole(part)) for part in mixed]
        + [(part, pl.BlockSpec((width, narrow), lambda i: (0, attn(i)))) for part in w_outs],
        [
            ((rows, model), BF16, row_spec),
            (
                (model, num_seqs * rows),
                BF16,
                pl.BlockSpec((model, ROWS), lambda i: (0, seq * counts[1] + norm(i))),
            ),
            (
                (num_seqs, rows, hidden_width),
                BF16,
                pl.BlockSpec((None, rows, wide), lambda i: (seq, 0, mid(i))),
            ),
            ((rows, hidden_width), BF16, wide_spec),
            ((rows, hidden_width), BF16, wide_spec),
            ((rows, model), BF16, pl.BlockSpec((rows, narrow), lambda i: (0, out(i)))),
        ],
        scratch=[
            pltpu.VMEM((len(mixed), rows, width), BF16),
            pltpu.VMEM((counts[0], rows, narrow), F32),
            pltpu.VMEM((rows, model), BF16),
            pltpu.VMEM((counts[2], rows, wide), BF16),
        ],
        into={1: normed_t, 2: inner},
        after=after,
    )


def error_body(m_ref, teacher_ref, valid_ref, *refs):
    *parts, out_ref, dy_ref, dyt_ref, loss_ref = refs
    output = m_ref[...].astype(F32) + total_of(parts)
    out_ref[...] = output.astype(BF16)
    errors = output - teacher_ref[...].astype(F32)
    valid = valid_ref[...]
    rounded = (valid * errors).astype(BF16)
    dy_ref[...] = rounded
    dyt_ref[...] = rounded.T
    squares = jnp.sum(valid * errors * errors, axis=0, keepdims=True)
    accumulate(loss_ref, squares, pl.program_id(0) == 0)


def output_error(seq, middle, teacher, valid, parts, layer_out, grad_t, after):
    num_seqs, rows, model = teacher.shape
    steps = rows // ROWS
    row_spec = pl.BlockSpec((ROWS, model), lambda i: (i, 0))
    seq_spec = pl.BlockSpec((None, ROWS, model), lambda i: (seq, i, 0))
    return run(
        error_body,
        "output_error",
        (steps,),
        [
            (middle, row_spec),
            (teacher, seq_spec),
            (valid, pl.BlockSpec((None, ROWS, 1), lambda i: (seq, i, 0))),
        ]
        + [(part, row_spec) for part in parts],
        [
            ((num_seqs, rows, model), BF16, seq_spec),
            ((rows, model), BF16, row_spec),
            (
                (model, num_seqs * rows),
                BF16,
                pl.BlockSpec((model, ROWS), lambda i: (0, seq * steps + i)),
            ),
            ((1, model), F32, pl.BlockSpec((1, model), lambda i: (0, 0))),
        ],
        into={0: layer_out, 2: grad_t},
        after=after,
    )


def backward_body(counts, dy_ref, wd_ref, a_ref, b_ref, wg_ref, wu_ref, *refs):
    dg_ref, du_ref, part_ref, gates, ups = refs
    wide_steps, out_steps = counts
    step = pl.program_id(0)

    @in_phase(step, 0, wide_steps)
    def _():
        grad_inner = nt(dy_ref[...], wd_ref[...])
        d_gate = (grad_inner * a_ref[...].astype(F32)).astype(BF16)
        d_up = (grad_inner * b_ref[...].astype(F32)).astype(BF16)
        dg_ref[...] = d_gate
        du_ref[...] = d_up
        gates[step] = d_gate
        ups[step] = d_up

    @in_phase(step, wide_steps, out_steps)
    def _():
        width = gates.shape[2]
        total = None
        for at in range(wide_steps):
            columns = slice(at * width, (at + 1) * width)
            term = nt(gates[at], wg_ref[:, columns]) + nt(ups[at], wu_ref[:, columns])
            total = term if total is None else total + term
        part_ref[...] = total.astype(BF16)


def backward_mlp(seq, num_seqs, grad_out, w_down, a, b, w_gate, w_up, kept, after):
    rows, model = grad_out.shape
    hidden_width = w_gate.shape[1]
    wide, narrow = divisor(hidden_width, 512), 512
    counts = (hidden_width // wide, model // narrow)
    mid, out = phase(0, counts[0]), phase(counts[0], counts[1])
    wide_spec = pl.BlockSpec((rows, wide), lambda i: (0, mid(i)))
    wide_seq = pl.BlockSpec((None, rows, wide), lambda i: (seq, 0, mid(i)))
    weight_spec = pl.BlockSpec((narrow, hidden_width), lambda i: (out(i), 0))
    return run(
        functools.partial(backward_body, counts),
        "backward_mlp",
        (sum(counts),),
        [
            (grad_out, whole(grad_out)),
            (w_down, pl.BlockSpec((wide, model), lambda i: (mid(i), 0))),
            (a, wide_spec),
            (b, wide_spec),
            (w_gate, weight_spec),
            (w_up, weight_spec),
        ],
        [
            ((num_seqs, rows, hidden_width), BF16, wide_seq),
            ((num_seqs, rows, hidden_width), BF16, wide_seq),
            ((rows, model), BF16, pl.BlockSpec((rows, narrow), lambda i: (0, out(i)))),
        ],
        scratch=[
            pltpu.VMEM((counts[0], rows, wide), BF16),
            pltpu.VMEM((counts[0], rows, wide), BF16),
        ],
        into=dict(zip((0, 1), kept)),
        after=after,
    )


def middle_back_body(counts, m_ref, dy_ref, gain_ref, w_ref, *refs):
    *parts, dm_ref, dmt_ref, dg_ref, do_ref, grad_t = refs
    norm_steps, out_steps = counts
    step = pl.program_id(0)

    @in_phase(step, 0, norm_steps)
    def _():
        grad_rows, grad_gain = norm_back(
            m_ref[...].astype(F32), gain_ref[...], total_of(parts)
        )
        rounded = (dy_ref[...].astype(F32) + grad_rows).astype(BF16)
        dm_ref[...] = rounded
        rounded_t = rounded.T
        dmt_ref[...] = rounded_t
        grad_t[step] = rounded_t
        accumulate(dg_ref, grad_gain, step == 0)

    @in_phase(step, norm_steps, out_steps)
    def _():
        columns = jnp.concatenate([grad_t[at] for at in range(norm_steps)], axis=1)
        do_ref[...] = nn(w_ref[...], columns).astype(BF16)


def middle_back(seq, num_seqs, middle, grad_output, gain, w_out, parts, grad_t, after):
    rows, model = middle.shape
    width = w_out.shape[0]
    tile = divisor(width, 640)
    counts = (rows // ROWS, width // tile)
    norm, out = phase(0, counts[0]), phase(counts[0], counts[1])
    row_spec = pl.BlockSpec((ROWS, model), lambda i: (norm(i), 0))
    return run(
        functools.partial(middle_back_body, counts),
        "middle_back",
        (sum(counts),),
        [
            (middle, row_spec),
            (grad_output, row_spec),
            (gain, whole(gain)),
            (w_out, pl.BlockSpec((tile, model), lambda i: (out(i), 0))),
        ]
        + [(part, row_spec) for part in parts],
        [
            ((rows, model), BF16, row_spec),
            (
                (model, num_seqs * rows),
                BF16,
                pl.BlockSpec((model, ROWS), lambda i: (0, seq * counts[0] + norm(i))),
            ),
            ((1, model), F32, pl.BlockSpec((1, model), lambda i: (0, 0))),
            ((width, rows), BF16, pl.BlockSpec((tile, rows), lambda i: (out(i), 0))),
        ],
        scratch=[pltpu.VMEM((counts[0], model, ROWS), BF16)],
        into={1: grad_t},
        after=after,
    )


def input_back_body(scale_ref, h_ref, dm_ref, gain_ref, *refs):
    *parts, grad_ref, dg_ref = refs
    grad_rows, grad_gain = norm_back(h_ref[...].astype(F32), gain_ref[...], total_of(parts))
    grad_ref[...] = scale_ref[0] * (dm_ref[...].astype(F32) + grad_rows)
    accumulate(dg_ref, grad_gain, pl.program_id(0) == 0)


def input_back(seq, scale, hidden, grad_middle, gain, parts, earlier, after):
    num_seqs, rows, model = hidden.shape
    row_spec = pl.BlockSpec((ROWS, model), lambda i: (i, 0))
    seq_spec = pl.BlockSpec((None, ROWS, model), lambda i: (seq, i, 0))
    return run(
        input_back_body,
        "input_back",
        (rows // ROWS,),
        [
            (scale, pl.BlockSpec(memory_space=pltpu.SMEM)),
            (hidden, seq_spec),
            (grad_middle, row_spec),
            (gain, whole(gain)),
        ]
        + [(part, row_spec) for part in parts],
        [
            ((num_seqs, rows, model), F32, seq_spec),
            ((1, model), F32, pl.BlockSpec((1, model), lambda i: (0, 0))),
        ],
        into={0: earlier},
        after=after,
    )


def weight_body(flipped, x_ref, y_ref, y_before_ref, far_ref, sent_ref, kept_ref, *refs):
    x_all, staged, landed, send_sem, recv_sem = refs
    tiles = landed.shape[0]
    step = pl.program_id(0)
    dp, ctx = lax.axis_index("dp"), lax.axis_index("ctx")
    ctx_size = lax.axis_size("ctx")
    core, chip = dp % 2, dp // 2
    partner = dp + 1 - 2 * core
    half = x_all.shape[0] // 2

    def sending(at):
        return pltpu.make_async_remote_copy(
            src_ref=staged.at[at % 2],
            dst_ref=landed.at[at],
            send_sem=send_sem.at[at % 2],
            recv_sem=recv_sem.at[at],
            device_id={"dp": partner},
            device_id_type=pl.DeviceIdType.MESH,
        )

    @pl.when(step == 0)
    def _():
        barrier = pltpu.get_barrier_semaphore()
        pl.semaphore_signal(
            barrier, inc=1, device_id={"dp": partner}, device_id_type=pl.DeviceIdType.MESH
        )
        pl.semaphore_wait(barrier, 1)
        size = x_ref.shape[0] // (lax.axis_size("dp") * ctx_size)
        low, high = ctx % 2, ctx // 2
        at = 0
        for other_core in (1, 0):
            to_core = core + other_core * (1 - 2 * core)
            for other_chip in (1, 0):
                to_dp = 2 * (chip + other_chip * (1 - 2 * chip)) + to_core
                for other_low in (1, 0):
                    for other_high in (1, 0):
                        to_ctx = 2 * (high + other_high * (1 - 2 * high))
                        to_ctx = to_ctx + low + other_low * (1 - 2 * low)
                        row = pl.multiple_of((to_dp * ctx_size + to_ctx) * size, size)
                        x_all[at : at + size, :] = x_ref[pl.ds(row, size), :]
                        at += size

    def product(rows, ref):
        y = ref[...]
        return nt(rows, y) if flipped else nn(rows, y.reshape(-1, y.shape[-1]))

    @pl.when((step >= 2) & (step < tiles))
    def _():
        sending(step - 2).wait_send()

    @pl.when(step < tiles)
    def _():
        staged[step % 2] = product(x_all[:half, :], y_ref).astype(BF16)
        sending(step).start()

    @pl.when(step > 0)
    def _():
        total = product(x_all[half:, :], y_before_ref)
        sending(step - 1).wait_recv()
        total = (total + landed[step - 1].astype(F32)).astype(BF16)
        far_ref[...] = total[: half // 2]
        sent_ref[...] = total[half // 2 : half // 4 * 3]
        kept_ref[...] = total[half // 4 * 3 :]

    @pl.when(step == tiles)
    def _():
        for at in range(max(tiles - 2, 0), tiles):
            sending(at).wait_send()


def weight_grad(meets, x_t, y, flipped, half, after):
    model, tokens = x_t.shape
    if flipped:
        tile = divisor(y.shape[0], 640)
        tiles, first = y.shape[0] // tile, 0
        y_block, place = (tile, tokens), lambda at: (at, 0)
    else:
        tile = divisor(y.shape[2], 512, 128)
        tiles, first = y.shape[2] // tile, 0
        if half is not None:
            first, tiles = ((0, tiles // 2), (tiles // 2, tiles - tiles // 2))[half]
        y_block, place = y.shape[:2] + (tile,), lambda at: (0, 0, first + at)
    width = tile * tiles
    before = lambda i: jnp.maximum(i - 1, 0)
    outs = [
        ((rows, width), BF16, pl.BlockSpec((rows, tile), lambda i: (0, before(i))))
        for rows in (model // 4, model // 8, model // 8)
    ]
    return run(
        functools.partial(weight_body, flipped),
        "weight_grad",
        (tiles + 1,),
        [
            (x_t, whole(x_t)),
            (y, pl.BlockSpec(y_block, lambda i: place(jnp.minimum(i, tiles - 1)))),
            (y, pl.BlockSpec(y_block, lambda i: place(before(i)))),
        ],
        outs,
        scratch=[
            pltpu.VMEM((model, tokens), BF16),
            pltpu.VMEM((2, model // 2, tile), BF16),
            pltpu.VMEM((tiles, model // 2, tile), BF16),
            pltpu.SemaphoreType.DMA((2,)),
            pltpu.SemaphoreType.DMA((tiles,)),
        ],
        after=after,
        meets=meets,
    )


def add_body(*refs):
    refs[-1][...] = total_of(refs[:-1]).astype(BF16)


def final_body(scale_ref, *refs):
    count = 4
    total = total_of(refs[:count]) * scale_ref[0]
    at = 0
    for out_ref in refs[count:]:
        out_ref[...] = total[:, at : at + out_ref.shape[1]]
        at += out_ref.shape[1]


def swap(value, axis, bit):
    size = lax.axis_size(axis)
    return lax.ppermute(value, axis, [(i, i ^ bit) for i in range(size)])


class Halving:
    def __init__(self, meets, x_t, y, flipped, half, after):
        far, self.sent, self.kept = weight_grad(meets, x_t, y, flipped, half, after)
        self.came = swap(far, "dp", 2)
        self.last = far

    def added(self, name, rows, parts, after):
        width = self.sent.shape[1]
        tile = divisor(width, 1792, 1024, 768, 640)
        ins = [
            (
                array,
                pl.BlockSpec((rows, tile), functools.partial(lambda at, j: (at, j), first // rows)),
            )
            for array, first in parts
        ]
        spec = pl.BlockSpec((rows, tile), lambda j: (0, j))
        return run(
            add_body, name, (width // tile,), ins, [((rows, width), BF16, spec)], after=after
        )[0]

    def near(self, after):
        rows = self.sent.shape[0]
        send = self.added("near", rows, [(self.sent, 0), (self.came, 0)], after)
        self.pair = swap(send, "ctx", 1)
        return send

    def fold(self, after):
        rows = self.sent.shape[0] // 2
        parts = [(self.kept, 0), (self.came, 2 * rows), (self.pair, 0)]
        send = self.added("fold", rows, parts, after)
        self.end = swap(send, "ctx", 2)
        return send

    def final(self, scale, widths, after):
        rows, width = self.end.shape
        tile = width if len(widths) > 1 else divisor(width, 896, 1024, 768, 640)
        tiles = [(tile,), widths][len(widths) > 1]
        parts = [(self.kept, 1), (self.came, 3), (self.pair, 1), (self.end, 0)]
        self.result = run(
            final_body,
            "final",
            (width // tile,),
            [(scale, pl.BlockSpec(memory_space=pltpu.SMEM))]
            + [
                (part, pl.BlockSpec((rows, tile), functools.partial(lambda at, j: (at, j), at)))
                for part, at in parts
            ],
            [
                ((rows, each), F32, pl.BlockSpec((rows, cut), lambda j: (0, j)))
                for each, cut in zip(widths, tiles)
            ],
            after=after,
        )
        return self.result[0]


def tensor_parts(partial):
    if lax.axis_size("tensor") == 2:
        return [partial, swap(partial, "tensor", 1)]
    return [lax.psum(partial, "tensor")]


def tensor_copies(value):
    if lax.axis_size("tensor") == 2:
        return [value, swap(value, "tensor", 1)]
    return list(lax.all_gather(value, "tensor"))


def tensor_weights(weight, after):
    size, count = lax.axis_size("dp"), weight.shape[0]
    if lax.axis_size("tensor") != 2 or count % (16 * size):
        return list(lax.all_gather(weight, "tensor"))
    rows = count // size
    part = lax.dynamic_slice_in_dim(weight, lax.axis_index("dp") * rows, rows)
    return [weight, lax.all_gather(held(swap(part, "tensor", 1), after), "dp", axis=0, tiled=True)]


def held(value, *others):
    return lax.optimization_barrier((value, *others))[0]


def shift(value, step):
    size = lax.axis_size("ctx")
    pairs = [(i, i + step) for i in range(size) if 0 <= i + step < size]
    return lax.ppermute(value, "ctx", pairs)


def local(
    hidden_in,
    w_query,
    key_weight_matrix,
    value_weight_matrix,
    w_out,
    w_gate,
    w_up,
    w_down,
    attn_gain,
    mlp_gain,
    segments,
    valid_mask,
    teacher,
):
    num_seqs, piece, model = hidden_in.shape
    seqs = range(num_seqs)
    ctx_size = lax.axis_size("ctx")
    ctx = lax.axis_index("ctx")
    query_places = ctx * piece + jnp.arange(piece, dtype=jnp.int32)
    positions = (query_places[None, :] - segments).astype(F32)
    freqs = THETA ** (-2.0 * jnp.arange(HALF, dtype=F32) / HEAD_SIZE)
    angles = positions[:, None, :] * freqs[None, :, None]
    cos, sin = jnp.cos(angles), jnp.sin(angles)
    starts = (segments + (ctx_size - 1 - ctx) * piece)[:, None, :]
    block = min(256, piece)
    lows = starts[:, 0, ::block] // block
    fulls = (starts[:, 0, block - 1 :: block] + block - 1) // block
    attn_gain_row, mlp_gain_row = attn_gain[None, :], mlp_gain[None, :]
    key_t, value_t = key_weight_matrix.T, value_weight_matrix.T
    valid = valid_mask.astype(F32)[..., None]


    count = jnp.sum(valid_mask).reshape(1, 1)
    count = count + swap(count, "dp", 1)
    normed, kv_chunks = [], []
    normed_t, last = None, hidden_in
    for s in seqs:
        n_rows, normed_t, kv_own = kv_project(
            s, hidden_in, attn_gain_row, key_t, value_t, cos, sin, normed_t, [last]
        )
        normed.append(n_rows)
        kv_chunks.append([kv_own])
        last = n_rows
    kv_chunks[0].append(shift(kv_chunks[0][0], 1))
    kv_chunks[0].append(shift(held(kv_chunks[0][-1], last), 1))
    last = q_project(0, normed[0], w_query, cos, sin, [last, kv_chunks[0][1]])
    queries = [last]
    count = count + swap(held(count, last), "dp", 2)
    kv_chunks[0].append(shift(held(kv_chunks[0][-1], last), 1))
    for s in seqs[1:]:
        own = held(kv_chunks[s][0], kv_chunks[0][-1])
        for step in range(1, ctx_size):
            kv_chunks[s].append(shift(own, step))

    made = {"count": count}
    lse, middle, rows_a, rows_b = [], [], [], []
    losses, dys, mlp_gains, attn_gains, grad_middle = [], [], [], [], []
    heads, mlp_parts, dn2_parts, dn1_parts, pieces, came = [], [], [], [], [], [None, None]
    w_outs = tensor_weights(held(w_out, normed[0]), kv_chunks[0][-1])
    tokens = num_seqs * piece * ctx_size * lax.axis_size("dp")
    last_seq = num_seqs - 1

    def scale():
        return (tokens / made["count"].reshape(()).astype(F32)).reshape(1)

    def attention(s, after):
        heads_out, made["mixed"], lse_rows = attend(
            s,
            num_seqs,
            lows[s],
            fulls[s],
            starts[s],
            queries[s],
            kv_chunks[s][::-1],
            made.get("mixed"),
            after,
        )
        lse.append(lse_rows)
        heads.append(tensor_copies(heads_out))
        return lse_rows

    def query(s, after):
        queries.append(q_project(s, normed[s], w_query, cos, sin, after))
        return queries[s]

    def forward(s, after):
        m_rows, made["n2"], made["z"], a, b, partial = forward_mlp(
            s,
            hidden_in,
            mlp_gain_row,
            w_gate,
            w_up,
            w_down,
            heads[s],
            w_outs,
            made.get("n2"),
            made.get("z"),
            after + [made["count"]],
        )
        middle.append(m_rows)
        rows_a.append(a)
        rows_b.append(b)
        mlp_parts.append(tensor_parts(partial))
        return m_rows

    def error(s, after):
        made["y"], dy, made["dy"], loss_row = output_error(
            s,
            middle[s],
            teacher,
            valid,
            mlp_parts[s],
            made.get("y"),
            made.get("dy"),
            after,
        )
        dys.append(dy)
        losses.append(loss_row)
        return dy

    def backward(s, after):
        made["dgate"], made["dup"], partial = backward_mlp(
            s,
            num_seqs,
            dys[s],
            w_down,
            rows_a[s],
            rows_b[s],
            w_gate,
            w_up,
            (made.get("dgate"), made.get("dup")),
            after,
        )
        dn2_parts.append(tensor_parts(partial))
        return partial

    def middle_step(s, after):
        dm, made["dm"], gain_row, made["do", s] = middle_back(
            s,
            num_seqs,
            middle[s],
            dys[s],
            mlp_gain_row,
            w_out,
            dn2_parts[s],
            made.get("dm"),
            after,
        )
        grad_middle.append(dm)
        mlp_gains.append(gain_row)
        return dm

    def attention_back(s, after):
        made["dq"], *parts = attend_back(
            s,
            num_seqs,
            lows[s],
            fulls[s],
            starts[s],
            cos,
            sin,
            queries[s],
            made["mixed"],
            made["do", s],
            lse[s],
            kv_chunks[s][::-1],
            made.get("dq"),
            after,
        )
        pieces.append(parts)
        return parts[0]

    def hop(s, at, after):
        total = pieces[s][at]
        if came[s] is not None:
            total = (total.astype(F32) + held(came[s], *after).astype(F32)).astype(BF16)
        came[s] = shift(total, -1)
        return after[0]

    def projections(s, after):
        made["dkv"], partial = qkv_back(
            s,
            made["dq"],
            cos,
            sin,
            w_query,
            key_t,
            value_t,
            pieces[s][-1],
            came[s],
            made.get("dkv"),
            after,
        )
        dn1_parts.append(tensor_parts(partial))
        return partial

    def halving(name, meets, x_t, y, flipped, half, after):
        made[name] = Halving(meets, made.get(x_t, normed_t), made[y], flipped, half, after)
        return made[name].last

    def input_step(s, after):
        made["dx"], gain_row = input_back(
            s,
            scale(),
            hidden_in,
            grad_middle[s],
            attn_gain_row,
            dn1_parts[s],
            made.get("dx"),
            after,
        )
        attn_gains.append(gain_row)
        return gain_row

    def hop_of(name, at, after):
        axis, bit = (("dp", 1), ("dp", 2), ("ctx", 1), ("ctx", 2))[at]
        total = held(made[name], *after)
        made[name] = total + swap(total, axis, bit)
        return after[0]

    def small_hop(at, after):
        if at == 0:
            loss = jnp.full((1, model), jnp.sum(sum(losses)))
            made["small"] = jnp.concatenate([sum(attn_gains), sum(mlp_gains), loss], axis=0)
        return hop_of("small", at, after)

    def finish(name, after):
        widths = (made[name].sent.shape[1],)
        if name == "k":
            widths = key_t.shape[:1] * 2
        return made[name].final(scale(), widths, after)

    steps = {
        "Ga": functools.partial(halving, "a", 0, "dy", "z", False, 0),
        "Gb": functools.partial(halving, "b", 6, "dy", "z", False, 1),
        "Gg": functools.partial(halving, "g", 3, "n2", "dgate", False, None),
        "Gu": functools.partial(halving, "u", 4, "n2", "dup", False, None),
        "Go": functools.partial(halving, "o", 1, "dm", "mixed", True, None),
        "Gq": functools.partial(halving, "q", 2, "n1", "dq", True, None),
        "Gk": functools.partial(halving, "k", 5, "n1", "dkv", True, None),
    }
    for name in "abguoqk":
        for short, stage in (("n", "near"), ("f", "fold")):
            steps[short + name] = lambda after, name=name, stage=stage: getattr(
                made[name], stage
            )(after)
        steps["e" + name] = functools.partial(finish, name)
    for at in range(4):
        steps["s%d" % at] = functools.partial(small_hop, at)
        steps["c%d" % at] = functools.partial(hop_of, "count", at)
    for s in seqs:
        for short, one in (
            ("at", attention),
            ("qp", query),
            ("fw", forward),
            ("er", error),
            ("bw", backward),
            ("mb", middle_step),
            ("ab", attention_back),
            ("qb", projections),
            ("in", input_step),
        ):
            steps[short + str(s)] = functools.partial(one, s)
        for at in range(ctx_size - 1):
            steps["h%d%d" % (s, at)] = functools.partial(hop, s, at)
    for name in ORDER:
        PRESENT[0] = WEIGHTS.get(name, 5)
        last = steps[name]([last])

    (out_sum,), (gate_sum,), (up_sum,) = (made[name].result for name in "ogu")
    down_sum = jnp.concatenate(made["a"].result + made["b"].result, axis=1)
    size = model // (lax.axis_size("dp") * ctx_size)
    here = (lax.axis_index("dp") * ctx_size + ctx) * size
    small = made["small"]
    gains = lax.dynamic_slice_in_dim(small[:2], here, size, axis=1) * scale()
    return (
        made["y"],
        small[2, 0] / (made["count"].reshape(()).astype(F32) * model),
        made["dx"],
        *made["q"].result,
        *made["k"].result,
        out_sum.T,
        gate_sum,
        up_sum,
        down_sum.T,
        gains[0],
        gains[1],
    )


def solution(mesh):
    placed = (
        P("dp", "ctx", None),
        P(None, "tensor"),
        P(None, "tensor"),
        P(None, "tensor"),
        P("tensor", None),
        P(None, "tensor"),
        P(None, "tensor"),
        P("tensor", None),
        P(),
        P(),
        P("dp", "ctx"),
        P("dp", "ctx"),
        P("dp", "ctx", None),
    )
    return jax.shard_map(
        local,
        mesh=mesh,
        in_specs=placed,
        out_specs=(
            P("dp", "ctx", None),
            P(),
            P("dp", "ctx", None),
            P(("dp", "ctx"), "tensor"),
            P(("dp", "ctx"), "tensor"),
            P(("dp", "ctx"), "tensor"),
            P("tensor", ("dp", "ctx")),
            P(("dp", "ctx"), "tensor"),
            P(("dp", "ctx"), "tensor"),
            P("tensor", ("dp", "ctx")),
            P(("dp", "ctx")),
            P(("dp", "ctx")),
        ),
        check_vma=False,
    )
```
